32 devices in a mesh: dp: 8 (over y, x, core), tensor: 4 (over z).
Axes of the slice: x: 2, y: 2, z: 4, core: 2. Of those that a mesh axis runs over, the one named last changes fastest.
Arguments:
- inputs: bfloat16 [8192, 2048], P('dp'), may hold values from -6 to 6
- segments: int32 [8, 1024], P('dp'), may hold values from 0 to 7, never falling along the last dimension, each value on 1 to 512 neighbouring positions
- cotangent: bfloat16 [8192, 2048], P('dp'), may hold values from -6 to 6
- norm1_gain: float32 [2048], replicated, may hold values from 0.25 to 1.75
- norm1_bias: float32 [2048], replicated, may hold values from -3 to 3
- query_weight: bfloat16 [2048, 2048], P(None, 'tensor'), may hold values from -0.125 to 0.125
- query_bias: float32 [2048], P('tensor'), may hold values from -3 to 3
- key_weight: bfloat16 [2048, 2048], P(None, 'tensor'), may hold values from -0.125 to 0.125
- value_weight: bfloat16 [2048, 2048], P(None, 'tensor'), may hold values from -0.125 to 0.125
- value_bias: float32 [2048], P('tensor'), may hold values from -2 to 2
- output_weight: bfloat16 [2048, 2048], P('tensor'), may hold values from -0.25 to 0.25
- output_bias: float32 [2048], replicated, may hold values from -3 to 3
- norm2_gain: float32 [2048], replicated, may hold values from 0.25 to 1.75
- norm2_bias: float32 [2048], replicated, may hold values from -3 to 3
- up_weight: bfloat16 [2048, 8192], P(None, 'tensor'), may hold values from -0.125 to 0.125
- up_bias: float32 [8192], P('tensor'), may hold values from -3 to 3
- down_weight: bfloat16 [8192, 2048], P('tensor'), may hold values from -0.0625 to 0.0625
- down_bias: float32 [2048], replicated, may hold values from -3 to 3
Outputs:
- output: bfloat16 [8192, 2048], P(('dp', 'tensor'))
- input_grad: float32 [8192, 2048], P(('dp', 'tensor'))
- norm1_gain_grad: float32 [2048], P('dp')
- norm1_bias_grad: float32 [2048], P('dp')
- query_weight_grad: float32 [2048, 2048], P('dp', 'tensor')
- query_bias_grad: float32 [2048], P(('tensor', 'dp'))
- key_weight_grad: float32 [2048, 2048], P('dp', 'tensor')
- value_weight_grad: float32 [2048, 2048], P('dp', 'tensor')
- value_bias_grad: float32 [2048], P(('tensor', 'dp'))
- output_weight_grad: float32 [2048, 2048], P('tensor', 'dp')
- output_bias_grad: float32 [2048], P('dp')
- norm2_gain_grad: float32 [2048], P('dp')
- norm2_bias_grad: float32 [2048], P('dp')
- up_weight_grad: float32 [2048, 8192], P('dp', 'tensor')
- up_bias_grad: float32 [8192], P(('tensor', 'dp'))
- down_weight_grad: float32 [8192, 2048], P('tensor', 'dp')
- down_bias_grad: float32 [2048], P('dp')
The draws below stay inside these ranges and needn't reach their ends.
Inputs may be any that keep to these rules, and one draw needn't show every extreme that they name: `segments`: each row is one sequence; its document numbers start at 0 and never fall along the row; each of the 8 documents has 1 to 512 tokens and one has exactly 512.
All inputs are finite; a program needn't handle non-finite values.
Results may differ from the reference program's by a relative error of at most 0.014.
Values may be sent and summed in bfloat16 or wider, within the bound.
No kernel may reach another device: no remote copies, remote signals or barrier semaphores. Data moves between devices by JAX's collectives and lax.ppermute only.
A program may use at most 256 MiB of HBM per device.

```python
import math
from functools import partial
import jax
import jax.numpy as jnp
import numpy as np
from jax import lax

D = 2048
HEADS = 16
HEAD_DIM = 128
FF = 8192
LEN = 1024
DOCS = 8
MOST = 512
SEQS_ALL = 8
TOKENS = 8192


def block_levels(rng, extent, split, low, high):
    level = 1.0
    for position, parts in split:
        steps = jax.random.uniform(jax.random.fold_in(jax.random.fold_in(rng, 6), position), (parts,), jnp.float32, low / len(split), high / len(split))
        level = level * jnp.repeat(jnp.exp(steps), extent[position] // parts).reshape((-1,) + (1,) * (len(extent) - 1 - position))
    return level


def split_up(count, total, limit, skew):
    portions = [(1 << 20) // math.isqrt(standing ** skew) + 1 for standing in range(2, count + 1)]
    surplus, holding = total - limit - (count - 1), [1] * (count - 1)
    while surplus > 0:
        candidates = [i for i in range(count - 1) if holding[i] < limit]
        whole, budget = sum([portions[i] for i in candidates]), surplus
        for i in candidates:
            addition = min(limit - holding[i], max(1, budget * portions[i] // whole), surplus)
            holding[i] = holding[i] + addition
            surplus = surplus - addition
    return np.array([limit] + holding)


def ragged_sizes(rng, count, total, most, lean):
    if count == 2:
        one = jax.random.randint(rng, (), max(1, total - most), min(most, total - 1) + 1)
        return jnp.stack([one, total - one])
    tallies = jnp.asarray(split_up(count, total, most, lean), jnp.int32)
    pairs = (count - 1) // 2
    giver, taker = tallies[1:1 + 2 * pairs:2], tallies[2:2 + 2 * pairs:2]
    margin = jnp.minimum(giver - 1, most - taker)
    shifted = jax.random.randint(jax.random.fold_in(rng, 1), (pairs,), 0, 1 << 20) % (margin + 1)
    tallies = tallies.at[1:1 + 2 * pairs:2].set(giver - shifted).at[2:2 + 2 * pairs:2].set(taker + shifted)
    return tallies[jax.random.permutation(jax.random.fold_in(rng, 2), count)]


def scatter_about(key, extent, scale, most, cuts=(), kind=jnp.bfloat16):
    array = jax.random.normal(key, extent, jnp.float32) * scale
    if len(cuts) > 0:
        array = block_levels(key, extent, cuts, -0.22, 0.18) * array
    return jnp.clip(array, min=-most, max=most).astype(kind)


def setup_inputs(seed: int = 0) -> dict:
    splits = jax.random.split(jax.random.key(seed), 19)
    return {
        "inputs": scatter_about(splits[0], (TOKENS, D), 1.0, 6.0, ((0, 8),)),
        "segments": jax.vmap(lambda own: jnp.searchsorted(jnp.cumsum(ragged_sizes(own, DOCS, LEN, MOST, 2)), jnp.arange(LEN), side="right"))(jax.random.split(splits[1], SEQS_ALL)).reshape((SEQS_ALL, LEN)).astype(jnp.int32),
        "cotangent": scatter_about(splits[2], (TOKENS, D), 1.0, 6.0, ((0, 8),)),
        "norm1_gain": jnp.clip(1.0 + 0.15 * jax.random.normal(splits[3], (D,), jnp.float32), 0.25, 1.75),
        "norm1_bias": scatter_about(splits[4], (D,), 0.3, 3.0, (), jnp.float32),
        "query_weight": scatter_about(splits[5], (D, D), D ** -0.5, 0.125, ((1, 4),)),
        "query_bias": scatter_about(splits[6], (D,), 0.5, 3.0, ((0, 4),), jnp.float32),
        "key_weight": scatter_about(splits[7], (D, D), D ** -0.5, 0.125, ((1, 4),)),
        "value_weight": scatter_about(splits[8], (D, D), D ** -0.5, 0.125, ((1, 4),)),
        "value_bias": scatter_about(splits[9], (D,), 0.2, 2.0, ((0, 4),), jnp.float32),
        "output_weight": scatter_about(splits[10], (D, D), (D // 4) ** -0.5, 0.25, ((0, 4),)),
        "output_bias": scatter_about(splits[11], (D,), 0.3, 3.0, (), jnp.float32),
        "norm2_gain": jnp.clip(1.0 + 0.15 * jax.random.normal(splits[12], (D,), jnp.float32), 0.25, 1.75),
        "norm2_bias": scatter_about(splits[13], (D,), 0.3, 3.0, (), jnp.float32),
        "up_weight": scatter_about(splits[14], (D, FF), D ** -0.5, 0.125, ((1, 4),)),
        "up_bias": scatter_about(splits[15], (FF,), 0.5, 3.0, ((0, 4),), jnp.float32),
        "down_weight": scatter_about(splits[16], (FF, D), FF ** -0.5, 0.0625, ((0, 4),)),
        "down_bias": scatter_about(splits[17], (D,), 0.3, 3.0, (), jnp.float32),
    }


EPSILON = 1e-05
MASKED_SCORE = -1e+30

@jax.custom_vjp
def low(v):
    return lax.optimization_barrier(v.astype(jnp.bfloat16)).astype(jnp.float32)

@jax.custom_vjp
def low_back(v):
    return v

def low_keep(v):
    return (low(v), None)

def low_pass(kept, grad):
    return (grad,)

def back_keep(v):
    return (v, None)

def back_low(kept, grad):
    return (low(grad),)
low.defvjp(low_keep, low_pass)
low_back.defvjp(back_keep, back_low)

def layer_norm(row_block, gain_vector, shift_vector):
    average = lax.optimization_barrier(jnp.mean(row_block, axis=-1, keepdims=True))
    centred = row_block - average
    spread = lax.optimization_barrier(jnp.mean(centred * centred, axis=-1, keepdims=True))
    return centred * lax.rsqrt(spread + EPSILON) * gain_vector + shift_vector

def matmul(left_side, right_side):
    return jnp.dot(left_side, right_side, precision=lax.Precision.HIGHEST)

def attend_sequence(blocks):
    query_seq, key_seq, value_seq, seg_row = blocks
    highest = lax.Precision.HIGHEST
    scores = low_back(jnp.einsum('qhd,khd->hqk', query_seq, key_seq, precision=highest))
    places = jnp.arange(seg_row.shape[0])
    allowed = (places[:, None] >= places[None, :]) & (seg_row[:, None] == seg_row[None, :])
    scores = jnp.where(allowed[None], scores, MASKED_SCORE)
    probabilities = low(jax.nn.softmax(scores, axis=-1))
    return jnp.einsum('hqk,khd->qhd', probabilities, value_seq, precision=highest)

def layer_forward(segments, inputs, norm1_gain, norm1_bias, query_weight, query_bias, key_weight, value_weight, value_bias, output_weight, output_bias, norm2_gain, norm2_bias, up_weight, up_bias, down_weight, down_bias):
    scaling = HEAD_DIM ** (-0.5)
    normed = low(layer_norm(inputs, norm1_gain, norm1_bias))
    query_all = low(low_back(matmul(normed, query_weight) + query_bias) * scaling)
    key_all = low(low_back(matmul(normed, key_weight)))
    value_all = low(low_back(matmul(normed, value_weight) + value_bias))
    blocked = (SEQS_ALL, LEN, HEADS, HEAD_DIM)
    attended = lax.map(jax.checkpoint(attend_sequence), (query_all.reshape(blocked), key_all.reshape(blocked), value_all.reshape(blocked), segments))
    attended = low(low_back(attended.reshape(TOKENS, D)))
    branch = low_back(matmul(attended, output_weight) + output_bias)
    middle = inputs + branch
    normed_two = low(layer_norm(middle, norm2_gain, norm2_bias))
    up_value = low_back(matmul(normed_two, up_weight) + up_bias)
    hidden = low(jax.nn.gelu(up_value, approximate=False))
    return middle + (matmul(hidden, down_weight) + down_bias)

def reference(inputs, segments, cotangent, norm1_gain, norm1_bias, query_weight, query_bias, key_weight, value_weight, value_bias, output_weight, output_bias, norm2_gain, norm2_bias, up_weight, up_bias, down_weight, down_bias):
    floats = tuple((item.astype(jnp.float32) for item in (inputs, norm1_gain, norm1_bias, query_weight, query_bias, key_weight, value_weight, value_bias, output_weight, output_bias, norm2_gain, norm2_bias, up_weight, up_bias, down_weight, down_bias)))
    result, pullback = jax.vjp(partial(layer_forward, segments), *floats)
    grads = pullback(cotangent.astype(jnp.float32))
    return (result.astype(jnp.bfloat16), grads[0], grads[1], grads[2], grads[3], grads[4], grads[5], grads[6], grads[7], grads[8], grads[9], grads[10], grads[11], grads[12], grads[13], grads[14], grads[15])
```

```python
import functools

import jax
import jax.numpy as jnp
from jax import lax
from jax.experimental import pallas as pl
from jax.experimental.pallas import tpu as pltpu
from jax.sharding import PartitionSpec as P

HEAD_DIM = 128
LONGEST = 512
EPSILON = 1e-05
MASKED_SCORE = -1e30
SCALING = HEAD_DIM ** (-0.5)
F32 = jnp.float32
BF16 = jnp.bfloat16
PARTS = 2


def mm(left_side, right_side):
    return lax.dot_general(
        left_side, right_side, (((1,), (0,)), ((), ())), preferred_element_type=F32
    )


def times_trans(left_side, right_side):
    return lax.dot_general(
        left_side, right_side, (((1,), (1,)), ((), ())), preferred_element_type=F32
    )


def trans_times(left_side, right_side):
    return lax.dot_general(
        left_side, right_side, (((0,), (0,)), ((), ())), preferred_element_type=F32
    )


def column_sums(values):
    return jnp.sum(values.astype(F32), axis=0)


def row_stats(rows):
    average = jnp.mean(rows, axis=-1, keepdims=True)
    centred = rows - average
    spread = jnp.mean(centred * centred, axis=-1, keepdims=True)
    return average, lax.rsqrt(spread + EPSILON)


def norm_back(d_normed, gain, xhat, inverse):
    scaled = d_normed * gain
    first = jnp.mean(scaled, axis=-1, keepdims=True)
    second = jnp.mean(scaled * xhat, axis=-1, keepdims=True)
    return inverse * (scaled - first - xhat * second)


def cost(flops):
    return pl.CostEstimate(flops=flops, bytes_accessed=16 * 2**20, transcendentals=0)


def key_start(block, size):
    return max(0, (block * size - (LONGEST - 1)) // size * size)


def probabilities(seg_row, seg_col, query, keys, block, size):
    low, high = key_start(block, size), (block + 1) * size
    scores = times_trans(keys[low:high, :], query)
    shape = (high - low, size)
    key_place = lax.broadcasted_iota(jnp.int32, shape, 0) + low
    query_place = lax.broadcasted_iota(jnp.int32, shape, 1) + block * size
    same = seg_col[low:high, :] == seg_row[:, block * size : high]
    scores = jnp.where(same & (key_place <= query_place), scores, MASKED_SCORE)
    weights = jnp.exp(scores - jnp.max(scores, axis=0, keepdims=True))
    return weights * (1.0 / jnp.sum(weights, axis=0, keepdims=True))


def forward_kernel(size, seg_row, seg_col, query, key, value, attended):
    for block in range(query.shape[0] // size):
        low, high = key_start(block, size), (block + 1) * size
        rows = slice(block * size, high)
        probs = probabilities(seg_row, seg_col, query[rows, :], key, block, size)
        attended[rows, :] = trans_times(probs.astype(BF16), value[low:high, :]).astype(BF16)


def backward_kernel(size, pieces, here_ref, seg_row, seg_col, query, key, value, *refs):
    count = len(pieces) * len(pieces[0])
    got = refs[:count]
    d_query, d_key, d_value, d_attended, key_sum, value_sum = refs[count:]
    groups = len(pieces[0])
    part = got[0].shape[0]
    share = len(pieces) * part
    for c in range(len(pieces)):
        for m in range(groups):
            start = lax.rem(here_ref[1] + m, groups) * share + c * part
            rows = pl.ds(pl.multiple_of(start, part), part)
            d_attended[rows, :] = got[c * groups + m][...]
    key_sum[...] = jnp.zeros_like(key_sum)
    value_sum[...] = jnp.zeros_like(value_sum)
    for block in range(query.shape[0] // size):
        low, high = key_start(block, size), (block + 1) * size
        rows = slice(block * size, high)
        probs = probabilities(seg_row, seg_col, query[rows, :], key, block, size)
        value_sum[low:high, :] += mm(probs.astype(BF16), d_attended[rows, :])
        d_probs = times_trans(value[low:high, :], d_attended[rows, :])
        inner = jnp.sum(probs * d_probs, axis=0, keepdims=True)
        d_scores = (probs * (d_probs - inner)).astype(BF16)
        d_query[rows, :] = (trans_times(d_scores, key[low:high, :]) * SCALING).astype(BF16)
        key_sum[low:high, :] += mm(d_scores, query[rows, :])
    d_key[...] = key_sum[...].astype(BF16)
    d_value[...] = value_sum[...].astype(BF16)


def segment_views(segments):
    seqs, length = segments.shape
    return segments.reshape(seqs, 1, length), segments.reshape(seqs, length, 1)


def attend(segments, query, key, value):
    seqs, length = segments.shape
    tall = pl.BlockSpec((length, HEAD_DIM), lambda s, h: (s, h))
    return pl.pallas_call(
        functools.partial(forward_kernel, min(256, length)),
        grid=(seqs, query.shape[1] // HEAD_DIM),
        in_specs=[
            pl.BlockSpec((None, 1, length), lambda s, h: (s, 0, 0)),
            pl.BlockSpec((None, length, 1), lambda s, h: (s, 0, 0)),
        ]
        + [tall] * 3,
        out_specs=tall,
        out_shape=jax.ShapeDtypeStruct(query.shape, BF16),
        compiler_params=pltpu.CompilerParams(vmem_limit_bytes=48 * 2**20),
        cost_estimate=cost(4 * query.shape[0] * length * query.shape[1]),
    )(*segment_views(segments), query, key, value)


def attend_back(segments, query, key, value, pieces, me):
    length = query.shape[0]
    tall = pl.BlockSpec((length, HEAD_DIM), lambda h, m: (0, h))
    flat = [piece for row in pieces for piece in row]
    kernel = functools.partial(backward_kernel, min(256, length), pieces)
    return pl.pallas_call(
        kernel,
        grid_spec=pltpu.PrefetchScalarGridSpec(
            num_scalar_prefetch=1,
            grid=(query.shape[1] // HEAD_DIM,),
            in_specs=[
                pl.BlockSpec((None, 1, length), lambda h, m: (0, 0, 0)),
                pl.BlockSpec((None, length, 1), lambda h, m: (0, 0, 0)),
            ]
            + [tall] * 3
            + [pl.BlockSpec((p.shape[0], HEAD_DIM), lambda h, m: (0, h)) for p in flat],
            out_specs=[tall] * 3,
            scratch_shapes=[
                pltpu.VMEM((length, HEAD_DIM), BF16),
                pltpu.VMEM((length, HEAD_DIM), F32),
                pltpu.VMEM((length, HEAD_DIM), F32),
            ],
        ),
        out_shape=[jax.ShapeDtypeStruct(query.shape, BF16)] * 3,
        compiler_params=pltpu.CompilerParams(vmem_limit_bytes=48 * 2**20),
        cost_estimate=cost(10 * query.shape[0] * length * query.shape[1]),
    )(me, *segment_views(segments), query, key, value, *flat)


def place_bits(blocks):
    return blocks.bit_length() - 1


def xor_source(place, me, bits):
    distance = 0
    for bit in range(bits):
        distance = distance + (((place >> (bits - 1 - bit)) & 1) << bit)
    return distance ^ me


def norm_rows(values, gain, bias):
    average = jnp.mean(values, axis=-1, keepdims=True)
    centred = values - average
    inverse = lax.rsqrt(jnp.mean(centred * centred, axis=-1, keepdims=True) + EPSILON)
    return centred * inverse * gain + bias


def project_kernel(x, gain, bias, wq, bq, wk, wv, bv, normed, query, key, value):
    low = norm_rows(x[...].astype(F32), gain[...], bias[...]).astype(BF16)
    normed[...] = low
    query[...] = ((mm(low, wq[...]) + bq[...]) * SCALING).astype(BF16)
    key[...] = mm(low, wk[...]).astype(BF16)
    value[...] = (mm(low, wv[...]) + bv[...]).astype(BF16)


def whole_spec(array):
    return pl.BlockSpec(array.shape, lambda *_: (0,) * array.ndim)


def project(x, gain, bias, wq, bq, wk, wv, bv):
    rows, width = x.shape
    local = wq.shape[1]
    size = min(512, rows)
    args = [x] + [v.reshape(1, -1) if v.ndim == 1 else v for v in (gain, bias, wq, bq, wk, wv, bv)]
    tall = pl.BlockSpec((size, width), lambda i: (i, 0))
    thin = pl.BlockSpec((size, local), lambda i: (i, 0))
    shape = jax.ShapeDtypeStruct((rows, local), BF16)
    return pl.pallas_call(
        project_kernel,
        grid=(rows // size,),
        in_specs=[tall] + [whole_spec(a) for a in args[1:]],
        out_specs=[tall] + [thin] * 3,
        out_shape=[jax.ShapeDtypeStruct(x.shape, BF16)] + [shape] * 3,
        compiler_params=pltpu.CompilerParams(vmem_limit_bytes=56 * 2**20),
        cost_estimate=cost(6 * rows * width * local),
    )(*args)


def middle_kernel(
    steps, here_ref, near, far, wo, x, bo, gain, bias, wup, bup, d_hid, wup_rows,
    own_mid, low_out, hidden, d_up, term, mid, low, d_low,
):
    first, second = steps
    step = pl.program_id(0)
    block = wo.shape[1]
    here, side = here_ref[0], here_ref[1]
    half = near.shape[1]

    @pl.when(step < first)
    def _():
        offset = pl.multiple_of(side * half, half)
        other = pl.multiple_of((1 - side) * half, half)
        branch = mm(near[...], wo[pl.ds(offset, half), :])
        branch = branch + mm(far[...], wo[pl.ds(other, half), :])
        values = x[...].reshape(branch.shape).astype(F32)
        columns = pl.ds(pl.multiple_of(step * block, block), block)
        mid[:, columns] = values + (branch + bo[...])

    @pl.when(step == first)
    def _():
        low[...] = norm_rows(mid[...], gain[...], bias[...]).astype(BF16)
        part = own_mid.shape[0]
        own_mid[...] = mid[pl.ds(pl.multiple_of(here * part, part), part), :]

    @pl.when((step >= first) & (step < first + second))
    def _():
        piece = 256
        for start in range(0, wup.shape[1], piece):
            columns = slice(start, start + piece)
            up_value = mm(low[...], wup[:, columns]) + bup[:, columns]
            below = 0.5 + 0.5 * lax.erf(up_value * (0.5**0.5))
            density = jnp.exp(-0.5 * up_value * up_value) * 0.3989422804014327
            hidden[:, columns] = (up_value * below).astype(BF16)
            slope = ((below + up_value * density) * d_hid[:, columns].astype(F32)).astype(BF16)
            d_up[:, columns] = slope
            place = pl.multiple_of((step - first) * wup.shape[1] + start, piece)
            d_low[:, pl.ds(place, piece)] = slope

    @pl.when(step >= first + second)
    def _():
        term[...] = times_trans(d_low[...], wup_rows[...]).astype(BF16)
        columns = pl.ds(pl.multiple_of((step - first - second) * block, block), block)
        low_out[...] = low[:, columns]


def middle_call(c, here, near, far, wo, x, bo, gain, bias, wup, bup, d_hid):
    groups, _, part, width = x.shape
    rows = groups * part
    hidden = wup.shape[1]
    block = 512
    first, second = width // block, hidden // block
    bo, gain, bias, bup = (v.reshape(1, -1) for v in (bo, gain, bias, bup))

    def at(index, low, count):
        return jnp.clip(index - low, 0, count - 1)

    def columns(tall, low, count):
        return pl.BlockSpec((tall, block), lambda i, h: (0, at(i, low, count)))

    third = first + second
    return pl.pallas_call(
        functools.partial(middle_kernel, (first, second)),
        grid_spec=pltpu.PrefetchScalarGridSpec(
            num_scalar_prefetch=1,
            grid=(first + second + first,),
            in_specs=[
                whole_spec(near),
                whole_spec(far),
                columns(width, 0, first),
                pl.BlockSpec(
                    (groups, None, part, block), lambda i, h: (0, c, 0, at(i, 0, first))
                ),
                columns(1, 0, first),
                whole_spec(gain),
                whole_spec(bias),
                columns(width, first, second),
                columns(1, first, second),
                pl.BlockSpec((None, rows, block), lambda i, h: (c, 0, at(i, first, second))),
                pl.BlockSpec((block, hidden), lambda i, h: (at(i, third, first), 0)),
            ],
            out_specs=[
                pl.BlockSpec((part, width), lambda i, h: (0, 0)),
                columns(rows, third, first),
                columns(rows, first, second),
                columns(rows, first, second),
                columns(rows, third, first),
            ],
            scratch_shapes=[
                pltpu.VMEM((rows, width), F32),
                pltpu.VMEM((rows, width), BF16),
                pltpu.VMEM((rows, hidden), BF16),
            ],
        ),
        out_shape=[
            jax.ShapeDtypeStruct((part, width), F32),
            jax.ShapeDtypeStruct((rows, width), BF16),
            jax.ShapeDtypeStruct((rows, hidden), BF16),
            jax.ShapeDtypeStruct((rows, hidden), BF16),
            jax.ShapeDtypeStruct((rows, width), BF16),
        ],
        compiler_params=pltpu.CompilerParams(vmem_limit_bytes=56 * 2**20),
        cost_estimate=cost(2 * rows * width * (width + 2 * hidden)),
    )(here, near, far, wo, x, bo, gain, bias, wup, bup, d_hid, wup)


def middle_back_kernel(count, here_ref, *refs):
    pieces, (mid, cot, gain, wo), outs = refs[:count], refs[count : count + 4], refs[count + 4 :]
    d_mid, d_branch, sums, d_att = outs

    @pl.when(pl.program_id(0) == 0)
    def _():
        d_normed = pieces[0][...].astype(F32)
        for piece in pieces[1:]:
            d_normed = d_normed + piece[...].astype(F32)
        values = mid[...]
        centred = values - jnp.mean(values, axis=-1, keepdims=True)
        inverse = lax.rsqrt(jnp.mean(centred * centred, axis=-1, keepdims=True) + EPSILON)
        xhat = centred * inverse
        total = cot[...].astype(F32) + norm_back(d_normed, gain[...], xhat, inverse)
        low = total.astype(BF16)
        d_mid[...] = total
        d_branch[...] = low
        sums[0:1, :] = jnp.sum(d_normed * xhat, axis=0, keepdims=True)
        sums[1:2, :] = jnp.sum(d_normed, axis=0, keepdims=True)
        sums[2:3, :] = jnp.sum(low.astype(F32), axis=0, keepdims=True)

    d_att[...] = times_trans(d_branch[...], wo[...]).astype(BF16)


def middle_back(c, me, pieces, mid, cotangent, gain, wo):
    part, width = mid.shape
    block = 512
    whole_rows = pl.BlockSpec((part, width), lambda j, m: (0, 0))
    specs = []
    for array, which in pieces:
        if which is None:
            specs.append(whole_rows)
        else:
            specs.append(
                pl.BlockSpec((None, part, width), lambda j, m, which=which: (which(m), 0, 0))
            )
    cot_spec = pl.BlockSpec((part, width), lambda j, m: (m[1] * PARTS + c, 0))
    return pl.pallas_call(
        functools.partial(middle_back_kernel, len(pieces)),
        grid_spec=pltpu.PrefetchScalarGridSpec(
            num_scalar_prefetch=1,
            grid=(width // block,),
            in_specs=specs
            + [whole_rows, cot_spec, pl.BlockSpec((1, width), lambda j, m: (0, 0))]
            + [pl.BlockSpec((block, width), lambda j, m: (j, 0))],
            out_specs=[
                whole_rows,
                whole_rows,
                pl.BlockSpec((8, width), lambda j, m: (0, 0)),
                pl.BlockSpec((part, block), lambda j, m: (0, j)),
            ],
        ),
        out_shape=[
            jax.ShapeDtypeStruct((part, width), F32),
            jax.ShapeDtypeStruct((part, width), BF16),
            jax.ShapeDtypeStruct((8, width), F32),
            jax.ShapeDtypeStruct((part, width), BF16),
        ],
        compiler_params=pltpu.CompilerParams(vmem_limit_bytes=48 * 2**20),
        cost_estimate=cost(2 * part * width * width),
    )(me, *[array for array, _ in pieces], mid, cotangent, gain.reshape(1, -1), wo)


def gradient_terms(pairs, me, blocks, core_only=False):
    half = blocks // 2
    bits = place_bits(blocks)
    lefts = [left for pair in pairs for left in pair[0]]
    part_of = [left[1] if isinstance(left, tuple) else None for left in lefts]
    lefts = [left[0] if isinstance(left, tuple) else left for left in lefts]
    rights = [right for pair in pairs for right in pair[1]]
    width = lefts[0].shape[-1] // blocks
    total = sum(pair[1][0].shape[1] for pair in pairs)

    def source(j, m):
        if core_only:
            return 2 * (j % half) + ((m[0] & 1) ^ (j < half).astype(jnp.int32))
        return xor_source(jnp.where(j < half, j + half, j - half), m[0], bits)

    def left_spec(left, c):
        if c is None:
            return pl.BlockSpec((left.shape[0], width), lambda j, m: (0, source(j, m)))
        shape = (left.shape[0], None, left.shape[2], width)
        return pl.BlockSpec(shape, lambda j, m: (0, c, 0, source(j, m)))

    def kernel(me_ref, *refs):
        left_refs, right_refs = refs[: len(lefts)], refs[len(lefts) : len(lefts) + len(rights)]
        send, keep = refs[-2:]
        step = pl.program_id(0)

        def fill(target):
            place = at = 0
            for ls, rs in pairs:
                count = len(ls)
                value = None
                for i in range(count):
                    left = left_refs[at + i][...].reshape(-1, width)
                    more = trans_times(left, right_refs[at + i][...])
                    value = more if value is None else value + more
                columns = value.shape[1]
                target[:, place : place + columns] = value.astype(BF16)
                place += columns
                at += count

        @pl.when(step < half)
        def _():
            fill(send)

        @pl.when(step >= half)
        def _():
            fill(keep)

    shape = jax.ShapeDtypeStruct((half, width, total), BF16)
    return pl.pallas_call(
        kernel,
        grid_spec=pltpu.PrefetchScalarGridSpec(
            num_scalar_prefetch=1,
            grid=(blocks,),
            in_specs=[left_spec(left, c) for left, c in zip(lefts, part_of)]
            + [whole_spec(right) for right in rights],
            out_specs=[
                pl.BlockSpec((None, width, total), lambda j, m: (jnp.minimum(j, half - 1), 0, 0)),
                pl.BlockSpec((None, width, total), lambda j, m: (jnp.maximum(j - half, 0), 0, 0)),
            ],
        ),
        out_shape=[shape, shape],
        compiler_params=pltpu.CompilerParams(vmem_limit_bytes=56 * 2**20),
        cost_estimate=cost(2 * blocks * width * sum(r.size for r in rights)),
    )(me, *lefts, *rights)


def normed_back_kernel(dq, dk, dv, wq, wk, wv, x, terms, gain_sum, bias_sum):
    total = times_trans(dq[...], wq[...]) + times_trans(dk[...], wk[...])
    total = total + times_trans(dv[...], wv[...])
    terms[...] = total.astype(BF16)
    values = x[...].astype(F32)
    centred = values - jnp.mean(values, axis=-1, keepdims=True)
    inverse = lax.rsqrt(jnp.mean(centred * centred, axis=-1, keepdims=True) + EPSILON)

    @pl.when(pl.program_id(0) == 0)
    def _():
        gain_sum[...] = jnp.zeros_like(gain_sum)
        bias_sum[...] = jnp.zeros_like(bias_sum)

    gain_sum[...] += jnp.sum(total * (centred * inverse), axis=0, keepdims=True)
    bias_sum[...] += jnp.sum(total, axis=0, keepdims=True)


def normed_back(dq, dk, dv, wq, wk, wv, x):
    rows, width = x.shape
    size = min(512, rows)
    thin = pl.BlockSpec((size, dq.shape[1]), lambda i: (i, 0))
    tall = pl.BlockSpec((size, width), lambda i: (i, 0))
    line = pl.BlockSpec((1, width), lambda i: (0, 0))
    return pl.pallas_call(
        normed_back_kernel,
        grid=(rows // size,),
        in_specs=[thin] * 3 + [whole_spec(w) for w in (wq, wk, wv)] + [tall],
        out_specs=[tall, line, line],
        out_shape=[
            jax.ShapeDtypeStruct((rows, width), BF16),
            jax.ShapeDtypeStruct((1, width), F32),
            jax.ShapeDtypeStruct((1, width), F32),
        ],
        compiler_params=pltpu.CompilerParams(vmem_limit_bytes=56 * 2**20),
        cost_estimate=cost(6 * rows * width * dq.shape[1]),
    )(dq, dk, dv, wq, wk, wv, x)


def both_parts(lefts, weight, transposed, columns):
    block = min(512, columns)
    part_of = [left[1] if isinstance(left, tuple) else None for left in lefts]
    lefts = [left[0] if isinstance(left, tuple) else left for left in lefts]
    depth = lefts[0].shape[-1]
    rows = lefts[0].shape[0] * (1 if part_of[0] is None else lefts[0].shape[2])

    def kernel(*refs):
        weight_ref, out = refs[-2:]
        for c in range(len(lefts)):
            left = refs[c][...].reshape(-1, depth)
            product = times_trans if transposed else mm
            out[c] = product(left, weight_ref[...]).astype(BF16)

    def left_spec(left, c):
        if c is None:
            return whole_spec(left)
        return pl.BlockSpec((left.shape[0], None) + left.shape[2:], lambda j: (0, c, 0, 0))

    if transposed:
        weight_spec = pl.BlockSpec((block, depth), lambda j: (j, 0))
    else:
        weight_spec = pl.BlockSpec((depth, block), lambda j: (0, j))
    return pl.pallas_call(
        kernel,
        grid=(columns // block,),
        in_specs=[left_spec(left, c) for left, c in zip(lefts, part_of)] + [weight_spec],
        out_specs=pl.BlockSpec((len(lefts), rows, block), lambda j: (0, 0, j)),
        out_shape=jax.ShapeDtypeStruct((len(lefts), rows, columns), BF16),
        compiler_params=pltpu.CompilerParams(vmem_limit_bytes=56 * 2**20),
        cost_estimate=cost(2 * len(lefts) * rows * depth * columns),
    )(*lefts, weight)


def swap_bit(values, axis, bit):
    size = lax.axis_size(axis)
    return lax.ppermute(values, axis, [(i, i ^ (1 << bit)) for i in range(size)])


def third(k, steps):
    return range((k - 1) * steps // 3 + 1, k * steps // 3 + 1)


def fence(things, arrays=()):
    lists = [thing.live for thing in things]
    flat = lax.optimization_barrier(tuple(v for values in lists for v in values) + tuple(arrays))
    place = 0
    for thing, values in zip(things, lists):
        thing.live = list(flat[place : place + len(values)])
        place += len(values)
    return flat[place:]


class Gather:
    def __init__(self, own):
        self.live = [own]
        self.size = lax.axis_size("tensor")
        self.here = lax.axis_index("tensor")

    def advance(self, k):
        if self.size != 4:
            if k == 1:
                every = lax.all_gather(self.live[0], "tensor", axis=1, tiled=True)
                half = every.shape[1] // 2
                side = self.here // (self.size // 2)
                self.live = [
                    lax.dynamic_slice_in_dim(every, where * half, half, 1)
                    for where in (side, 1 - side)
                ]
            return
        if k == 1:
            self.live.append(swap_bit(self.live[0], "tensor", 0))
        elif k == 2:
            own, other = self.live
            even = self.here % 2 == 0
            pair = [jnp.where(even, own, other), jnp.where(even, other, own)]
            near = jnp.concatenate(pair, axis=1)
            self.live = [near, lax.ppermute(near, "tensor", [(1, 2), (2, 1)])]
        else:
            near, far = self.live
            last = lax.ppermute(far, "tensor", [(1, 0), (2, 3)])
            self.live = [near, far, last]

    def pair(self):
        if self.size != 4:
            return self.live
        near, far, last = self.live
        inner = (self.here == 1) | (self.here == 2)
        return [near, jnp.where(inner, far, last)]


class PairReduce:
    def __init__(self, parts):
        self.live = [parts]
        self.size = lax.axis_size("tensor")
        self.here = lax.axis_index("tensor")

    def advance(self, k):
        parts = self.live[0]
        if self.size != 4:
            if k == 1:
                self.live = [lax.psum_scatter(parts, "tensor", scatter_dimension=0)]
            return
        side = self.here // 2
        away = lax.dynamic_slice_in_dim(parts, 2 - 2 * side, 2, 0)
        if k == 1:
            self.live.append(lax.ppermute(away, "tensor", [(0, 1), (3, 2)]))
        elif k == 2:
            total = (self.live[1].astype(F32) + away.astype(F32)).astype(BF16)
            self.live[1] = lax.ppermute(total, "tensor", [(1, 2), (2, 1)])
        else:
            got = self.live[1]
            other = lax.dynamic_index_in_dim(parts, self.here ^ 1, 0, False).astype(F32)
            more = lax.dynamic_index_in_dim(got, 1 - self.here % 2, 0, False).astype(F32)
            self.live.append(swap_bit((other + more).astype(BF16), "tensor", 0))

    def pieces(self):
        if self.size != 4:
            return [(self.live[0], None)]
        parts, got, last = self.live
        return [(parts, lambda m: m[1]), (got, lambda m: m[1] % 2), (last, None)]


class LineReduce:
    def __init__(self, parts, axis=0):
        self.live = [parts]
        self.axis = axis
        self.size = lax.axis_size("tensor")
        self.here = lax.axis_index("tensor")

    def term(self, which):
        which = jnp.clip(which, 0, self.size - 1)
        return lax.dynamic_index_in_dim(self.live[0], which, self.axis, keepdims=False)

    def advance(self, k):
        size = self.size
        for step in third(k, size - 1):
            ahead = self.term(self.here + size - step)
            behind = self.term(self.here - size + step)
            if step > 1:
                ahead = (self.live[1].astype(F32) + ahead.astype(F32)).astype(BF16)
                behind = (self.live[2].astype(F32) + behind.astype(F32)).astype(BF16)
            up = lax.ppermute(ahead, "tensor", [(i, i + 1) for i in range(step)])
            down = lax.ppermute(behind, "tensor", [(i, i - 1) for i in range(size - step, size)])
            self.live[1:] = [up, down]

    def total(self):
        own = self.term(self.here).astype(F32)
        return own + self.live[1].astype(F32) + self.live[2].astype(F32)


class DpSum:
    def __init__(self, send, keep, cuts):
        self.base = [send, keep]
        self.bits = place_bits(lax.axis_size("dp"))
        self.edges = [keep.shape[-1] * c // cuts for c in range(cuts + 1)]
        self.state = [[] for _ in range(cuts)]
        self.left = [list(range(1, self.bits)) for _ in range(cuts)]

    @property
    def live(self):
        return self.base + [v for values in self.state for v in values]

    @live.setter
    def live(self, values):
        values = list(values)
        self.base = [values.pop(0) for _ in self.base]
        self.state = [[values.pop(0) for _ in state] for state in self.state]

    def core(self):
        self.base = [self.base[1], swap_bit(self.base[0], "dp", 0)]

    def move(self, values, cut):
        left = self.left[cut]
        bit = left[0] if cut % 2 == 0 else left[-1]
        dim = left.index(bit)
        keep = lax.index_in_dim(values, 0, dim, keepdims=False)
        send = lax.index_in_dim(values, 1, dim, keepdims=False)
        left.remove(bit)
        self.state[cut] = [keep, swap_bit(send, "dp", bit)]

    def first(self, *cuts):
        keep, got = self.base
        for cut in cuts:
            columns = slice(self.edges[cut], self.edges[cut + 1])
            total = keep[..., columns].astype(F32) + got[..., columns].astype(F32)
            total = total.astype(BF16).reshape((2,) * (self.bits - 1) + keep.shape[1:-1] + (-1,))
            self.move(total, cut)
        if all(self.state):
            self.base = []

    def second(self, *cuts):
        for cut in cuts:
            while self.left[cut]:
                self.move(self.sum(cut).astype(BF16), cut)

    def sum(self, cut):
        keep, got = self.state[cut]
        return keep.astype(F32) + got.astype(F32)

    def total(self):
        return [self.sum(cut) for cut in range(len(self.state))]


class WeightGather:
    def __init__(self, own, me):
        self.blocks = lax.axis_size("dp")
        self.size = lax.axis_size("tensor")
        self.usual = (self.size, self.blocks) == (4, 8)
        self.me = me
        share = own.shape[1 if self.usual else 0] // self.blocks
        axis = 1 if self.usual else 0
        self.live = [lax.dynamic_slice_in_dim(own, me[0] * share, share, axis)]

    def advance(self, k):
        if not self.usual:
            if k == 0:
                self.live = [lax.all_gather(self.live[0], ("tensor", "dp"), axis=0, tiled=True)]
            return
        if k == 0:
            own = self.live[0]
            self.live += [
                lax.ppermute(own, "tensor", [(i, (i + m) % self.size) for i in range(self.size)])
                for m in range(1, self.size)
            ]
        elif k == 1:
            own, one, two, three = self.live
            even = lax.axis_index("tensor") % 2 == 0
            near = jnp.concatenate([jnp.where(even, own, one), jnp.where(even, three, own)])
            far = jnp.concatenate([jnp.where(even, two, three), jnp.where(even, one, two)])
            self.live = [near, swap_bit(near, "dp", 1), far, swap_bit(far, "dp", 2)]
            self.live += [swap_bit(near, "dp", 0), swap_bit(far, "dp", 0)]
        elif k == 2:
            near, near_one, far, far_one, near_core, far_core = self.live
            self.live = [jnp.stack([near, near_one]), jnp.stack([far, far_one])]
            self.live += [swap_bit(self.live[0], "dp", 2), swap_bit(self.live[1], "dp", 1)]
            self.live += [near_core[None], far_core[None], far_one]
            self.live += [swap_bit(near_one, "dp", 0)[None]]
        else:
            near, far, near_two, far_two, near_core, far_core, far_one, near_one_core = self.live
            self.half = self.place([near, near_two, far, far_two], 0, None)
            self.live = [near_core, near_one_core, swap_bit(near_two, "dp", 0)]
            self.live += [far_core, swap_bit(far_one, "dp", 0)[None], swap_bit(far_two, "dp", 0)]
            self.live += [self.half]

    def place(self, arrays, core, half):
        rows, width = arrays[0].shape[1:]
        starts = [0]
        for array in arrays:
            starts.append(starts[-1] + array.shape[0])

        def kernel(me_ref, *refs):
            step = pl.program_id(0)
            for q in range(len(arrays)):

                @pl.when((step >= starts[q]) & (step < starts[q + 1]))
                def _():
                    refs[-1][...] = refs[q][...]

        def source(q):
            last = arrays[q].shape[0] - 1
            return pl.BlockSpec(
                (None, rows, width), lambda s, m: (jnp.clip(s - starts[q], 0, last), 0, 0)
            )

        def target(s, m):
            one, two = s & 1, (s >> 1) & 1
            low = jnp.where(s < 4, 2 * one + 4 * two, 4 * one + 2 * two)
            return (jnp.where(s < 4, m[2], 1 - m[2]), (low + core) ^ m[0])

        more = [] if half is None else [half]
        return pl.pallas_call(
            kernel,
            grid_spec=pltpu.PrefetchScalarGridSpec(
                num_scalar_prefetch=1,
                grid=(8,),
                in_specs=[source(q) for q in range(len(arrays))]
                + [pl.BlockSpec(memory_space=pl.ANY)] * len(more),
                out_specs=pl.BlockSpec((rows, width), target),
            ),
            out_shape=jax.ShapeDtypeStruct((2 * rows, 8 * width), BF16),
            input_output_aliases={1 + len(arrays): 0} if more else {},
            compiler_params=pltpu.CompilerParams(vmem_limit_bytes=32 * 2**20),
            cost_estimate=cost(2**20),
        )(self.me, *arrays, *more)

    def whole(self):
        if not self.usual:
            return self.live[0]
        return self.place(self.live[:6], 1, self.live[6])


class SmallSum:
    def __init__(self, vectors, me):
        self.vectors = vectors
        self.blocks = blocks = lax.axis_size("dp")
        self.bits = place_bits(blocks)
        places = jnp.stack([xor_source(p, me, self.bits) for p in range(blocks)]).reshape(-1)
        self.ordered = sorted(range(len(vectors)), key=lambda i: not vectors[i][1])
        wide = [vectors[i][0].reshape(blocks, -1) for i in self.ordered]
        wide = jnp.take(jnp.concatenate(wide, axis=1), places, axis=0)
        self.live = [wide.reshape((2,) * self.bits + wide.shape[1:])]

    def move(self):
        values = self.live[0]
        self.live = [values[0] + swap_bit(values[1], "dp", self.bits - values.ndim + 1)]

    def finish(self):
        while self.live[0].ndim > 1:
            self.move()
        values = self.live[0]
        both = sum(v[0].shape[0] // self.blocks for v in self.vectors if v[1])
        summed, alone = values[:both], values[both:]
        for bit in range(place_bits(lax.axis_size("tensor"))):
            summed = summed + swap_bit(summed, "tensor", bit)
        self.live = [jnp.concatenate([summed, alone])]

    def total(self):
        out, start = [None] * len(self.vectors), 0
        for i in self.ordered:
            size = self.vectors[i][0].shape[0] // self.blocks
            out[i] = self.live[0][start : start + size]
            start += size
        return out


def on_device(
    inputs,
    segments,
    cotangent,
    norm1_gain,
    norm1_bias,
    query_weight,
    query_bias,
    key_weight,
    value_weight,
    value_bias,
    output_weight,
    output_bias,
    norm2_gain,
    norm2_bias,
    up_weight,
    up_bias,
    down_weight,
    down_bias,
):
    groups = lax.axis_size("tensor")
    blocks = lax.axis_size("dp")
    here = lax.axis_index("tensor").astype(jnp.int32)
    side = here // (groups // 2)
    me = lax.axis_index("dp").astype(jnp.int32)
    me = jnp.stack([me, here, side])
    place = jnp.stack([here, side])
    rows, width = inputs.shape
    share = rows // groups
    part = share // PARTS
    local = query_weight.shape[1]
    size = width // blocks

    def by_part(values):
        return values.reshape(groups, PARTS, part, values.shape[1])

    def own(values):
        return lax.dynamic_slice_in_dim(values, here * share, share, 0)

    def own_heads(values):
        values = values.reshape(groups, part, values.shape[1])
        return lax.dynamic_index_in_dim(values, here, 0, keepdims=False)

    def all_to_all(d_att):
        got = []
        for m in range(groups):
            to = (here - m) % groups
            piece = lax.dynamic_slice_in_dim(d_att, to * local, local, 1)
            if m > 0:
                ring = [(i, (i - m) % groups) for i in range(groups)]
                piece = lax.ppermute(piece, "tensor", ring)
            got.append(piece)
        return got

    weight = WeightGather(output_weight, me)
    weight.advance(0)
    normed, query, key, value = project(
        inputs,
        norm1_gain,
        norm1_bias,
        query_weight,
        query_bias,
        key_weight,
        value_weight,
        value_bias,
    )
    attended = attend(segments, query, key, value)
    gather = [
        Gather(by_part(attended)[:, c].reshape(groups * part, local)) for c in range(PARTS)
    ]
    (cot,) = fence([weight] + gather, (cotangent,))

    gather[0].advance(1)
    weight.advance(1)
    cot_parts = by_part(cot)
    cots = [(cot_parts, c) for c in range(PARTS)]
    d_hidden = both_parts(cots, down_weight, True, down_weight.shape[0])
    (d_hidden, cot) = fence([weight] + gather, (d_hidden, cot))

    gather[0].advance(2)
    gather[1].advance(1)
    weight.advance(2)
    cot_sum = column_sums(cot)
    (cot_sum,) = fence([weight] + gather, (cot_sum,))

    gather[0].advance(3)
    gather[1].advance(2)
    weight.advance(3)
    fence([weight] + gather)

    own_mid, low, hidden, d_up, pairs, heads = ([None] * PARTS for _ in range(6))

    def middle(c):
        pairs[c] = gather[c].pair()
        own_mid[c], low[c], hidden[c], d_up[c], terms = middle_call(
            c,
            place,
            *pairs[c],
            whole,
            by_part(inputs),
            output_bias,
            norm2_gain,
            norm2_bias,
            up_weight,
            up_bias,
            d_hidden,
        )
        return PairReduce(terms.reshape(groups, part, width))

    gather[1].advance(3)
    whole = weight.whole()
    reduce_up = [middle(0), None]
    (whole,) = fence([gather[1], reduce_up[0]], (whole,))

    reduce_up[0].advance(1)
    reduce_up[1] = middle(1)
    hidden[0], hidden[1], d_up[0], d_up[1], *heads = fence(
        reduce_up, (*hidden, *d_up, *pairs[0], *pairs[1])
    )

    reduce_up[0].advance(2)
    reduce_up[1].advance(1)
    out_terms = both_parts(hidden, down_weight, False, width)
    reduce_out = LineReduce(out_terms.reshape(PARTS, groups, part, width), 1)
    heads = [own_heads(v) for v in heads]
    attended_own = [jnp.concatenate(heads[k::2], axis=0) for k in range(2)]
    d_up[0], d_up[1], *attended_own = fence(reduce_up + [reduce_out], (*d_up, *attended_own))

    reduce_up[0].advance(3)
    reduce_up[1].advance(2)
    reduce_out.advance(1)
    mlp_terms = gradient_terms([(low, d_up), (cots, hidden)], me, blocks, True)
    up_sum = column_sums(d_up[0]) + column_sums(d_up[1])
    *mlp_terms, up_sum = fence(reduce_up + [reduce_out], (*mlp_terms, up_sum))

    d_mids, d_branches, sums, got = ([None] * PARTS for _ in range(4))
    reduce_up[1].advance(3)
    mlp_got = swap_bit(mlp_terms[0], "dp", 0)

    def back(c):
        d_mids[c], d_branches[c], sums[c], d_att = middle_back(
            c, me, reduce_up[c].pieces(), own_mid[c], cotangent, norm2_gain, whole
        )
        got[c] = all_to_all(d_att)

    back(0)
    *got[0], d_branches[0], mlp_got = fence(
        [reduce_up[1], reduce_out], (*got[0], d_branches[0], mlp_got)
    )

    back(1)
    reduce_out.advance(2)
    mlp_sum = (mlp_terms[1].astype(F32) + mlp_got.astype(F32)).astype(BF16)
    wo_sum = DpSum(
        *gradient_terms(
            [([d_branches[c] for c in range(PARTS)], [v[c * part : (c + 1) * part] for c in range(PARTS)]) for v in attended_own],
            me,
            blocks,
        ),
        2,
    )
    *got[1], mlp_sum = fence([reduce_out, wo_sum], (*got[1], mlp_sum))

    reduce_out.advance(3)
    wo_sum.core()
    same_core = [list(range(c, blocks, 2)) for c in range(2)]
    mlp_sum = lax.psum_scatter(
        mlp_sum, "dp", scatter_dimension=0, axis_index_groups=same_core
    )
    d_query, d_key, d_value = attend_back(segments, query, key, value, got, me)
    d_query, d_key, d_value = fence([reduce_out, wo_sum], (d_query, d_key, d_value))

    wo_sum.first(0, 1)
    terms_in, gain1, bias1 = normed_back(
        d_query, d_key, d_value, query_weight, key_weight, value_weight, inputs
    )
    reduce_in = LineReduce(terms_in.reshape(groups, share, width))
    d_query, d_key, d_value, normed, gain1, bias1 = fence(
        [reduce_in, wo_sum], (d_query, d_key, d_value, normed, gain1, bias1)
    )

    reduce_in.advance(1)
    wo_sum.second(0, 1)
    qkv_sum = DpSum(
        *gradient_terms([([normed], [d]) for d in (d_query, d_key, d_value)], me, blocks), 2
    )
    two = sums[0] + sums[1]
    small = SmallSum(
        [
            (gain1[0], True),
            (bias1[0], True),
            (two[0], True),
            (two[1], True),
            (two[2], True),
            (cot_sum, False),
            (column_sums(d_query), False),
            (column_sums(d_value), False),
            (up_sum, False),
        ],
        me[:1],
    )
    fence([reduce_in, wo_sum, qkv_sum, small])

    reduce_in.advance(2)
    qkv_sum.core()
    small.move()
    total = reduce_out.total()
    outputs = [(own_mid[c] + (total[c] + down_bias)).astype(BF16) for c in range(PARTS)]
    output = jnp.concatenate(outputs, axis=0)
    average, inverse = row_stats(own(inputs).astype(F32))
    wo_terms = jnp.concatenate(wo_sum.total(), axis=1).T
    wo_terms = wo_terms.astype(BF16).reshape(groups, local, size)
    wo_terms, output, average, inverse = fence(
        [reduce_in, qkv_sum, small], (wo_terms, output, average, inverse)
    )

    reduce_in.advance(3)
    qkv_sum.first(0, 1)
    small.move()
    (mlp_sum,) = fence([reduce_in, qkv_sum, small], (mlp_sum,))

    qkv_sum.second(0, 1)
    small.finish()
    output_weight_grad = 0.0
    for m in range(groups):
        to = (here - m) % groups
        away = jnp.where(to // (groups // 2) == side, 0, groups // 2)
        piece = lax.dynamic_index_in_dim(wo_terms, away + to % (groups // 2), 0, keepdims=False)
        if m > 0:
            ring = [(i, (i - m) % groups) for i in range(groups)]
            piece = lax.ppermute(piece, "tensor", ring)
        output_weight_grad = output_weight_grad + piece.astype(F32)
    xhat = (own(inputs).astype(F32) - average) * inverse
    d_mid = jnp.concatenate(d_mids, axis=0)
    input_grad = d_mid + norm_back(reduce_in.total(), norm1_gain, xhat, inverse)
    hidden_width = up_weight.shape[1]
    mlp_sum = mlp_sum.astype(F32)
    qkv_grad = jnp.concatenate(qkv_sum.total(), axis=1)
    (
        norm1_gain_grad,
        norm1_bias_grad,
        norm2_gain_grad,
        norm2_bias_grad,
        output_bias_grad,
        down_bias_grad,
        query_bias_grad,
        value_bias_grad,
        up_bias_grad,
    ) = small.total()
    return (
        output,
        input_grad,
        norm1_gain_grad,
        norm1_bias_grad,
        qkv_grad[:, :local],
        query_bias_grad,
        qkv_grad[:, local : 2 * local],
        qkv_grad[:, 2 * local :],
        value_bias_grad,
        output_weight_grad,
        output_bias_grad,
        norm2_gain_grad,
        norm2_bias_grad,
        mlp_sum[:, :hidden_width],
        up_bias_grad,
        mlp_sum[:, hidden_width:].T,
        down_bias_grad,
    )


def solution(mesh):
    return jax.shard_map(
        on_device,
        mesh=mesh,
        in_specs=(
            P("dp", None),
            P("dp", None),
            P("dp", None),
            P(),
            P(),
            P(None, "tensor"),
            P("tensor"),
            P(None, "tensor"),
            P(None, "tensor"),
            P("tensor"),
            P("tensor", None),
            P(),
            P(),
            P(),
            P(None, "tensor"),
            P("tensor"),
            P("tensor", None),
            P(),
        ),
        out_specs=(
            P(("dp", "tensor"), None),
            P(("dp", "tensor"), None),
            P("dp"),
            P("dp"),
            P("dp", "tensor"),
            P(("tensor", "dp")),
            P("dp", "tensor"),
            P("dp", "tensor"),
            P(("tensor", "dp")),
            P("tensor", "dp"),
            P("dp"),
            P("dp"),
            P("dp"),
            P("dp", "tensor"),
            P(("tensor", "dp")),
            P("tensor", "dp"),
            P("dp"),
        ),
        check_vma=False,
    )
```

```python
import functools

import jax
import jax.numpy as jnp
from jax import lax
from jax.experimental import pallas as pl
from jax.experimental.pallas import tpu as pltpu
from jax.sharding import PartitionSpec as P

HEAD_DIM = 128
LONGEST = 512
EPSILON = 1e-05
MASKED_SCORE = -1e30
SCALING = HEAD_DIM ** (-0.5)
F32 = jnp.float32
BF16 = jnp.bfloat16
PARTS = 2
COST = 0
VMEM = 60 * 2**20


def mm(left_side, right_side):
    return lax.dot_general(
        left_side, right_side, (((1,), (0,)), ((), ())), preferred_element_type=F32
    )


def times_trans(left_side, right_side):
    return lax.dot_general(
        left_side, right_side, (((1,), (1,)), ((), ())), preferred_element_type=F32
    )


def trans_times(left_side, right_side):
    return lax.dot_general(
        left_side, right_side, (((0,), (0,)), ((), ())), preferred_element_type=F32
    )


def column_sums(values):
    return jnp.sum(values.astype(F32), axis=0)


def row_stats(rows):
    average = jnp.mean(rows, axis=-1, keepdims=True)
    centred = rows - average
    spread = jnp.mean(centred * centred, axis=-1, keepdims=True)
    return average, lax.rsqrt(spread + EPSILON)


def norm_back(d_normed, gain, xhat, inverse):
    scaled = d_normed * gain
    first = jnp.mean(scaled, axis=-1, keepdims=True)
    second = jnp.mean(scaled * xhat, axis=-1, keepdims=True)
    return inverse * (scaled - first - xhat * second)


def cost(flops):
    return pl.CostEstimate(flops=COST and flops, bytes_accessed=2**10, transcendentals=0)


def key_start(block, size):
    return max(0, (block * size - (LONGEST - 1)) // size * size)


def probabilities(seg_row, seg_col, query, keys, block, size):
    low, high = key_start(block, size), (block + 1) * size
    scores = times_trans(keys[low:high, :], query)
    shape = (high - low, size)
    key_place = lax.broadcasted_iota(jnp.int32, shape, 0) + low
    query_place = lax.broadcasted_iota(jnp.int32, shape, 1) + block * size
    same = seg_col[low:high, :] == seg_row[:, block * size : high]
    scores = jnp.where(same & (key_place <= query_place), scores, MASKED_SCORE)
    weights = jnp.exp(scores - jnp.max(scores, axis=0, keepdims=True))
    return weights * (1.0 / jnp.sum(weights, axis=0, keepdims=True))


def forward_kernel(size, seg_row, seg_col, query, key, value, *outs):
    part = outs[0].shape[1]
    for block in range(query.shape[0] // size):
        low, high = key_start(block, size), (block + 1) * size
        rows = slice(block * size, high)
        probs = probabilities(seg_row, seg_col, query[rows, :], key, block, size)
        attended = trans_times(probs.astype(BF16), value[low:high, :]).astype(BF16)
        for piece in range(size // part):
            share, c = divmod(block * (size // part) + piece, PARTS)
            outs[c][share] = attended[piece * part : (piece + 1) * part, :]


def backward_kernel(size, seg_row, seg_col, query, key, value, got, *refs):
    d_query, d_key, d_value, d_attended, key_sum, value_sum = refs
    groups, parts, part = got.shape[:3]
    for t in range(groups):
        for c in range(parts):
            start = (t * parts + c) * part
            d_attended[start : start + part, :] = got[t, c]
    key_sum[...] = jnp.zeros_like(key_sum)
    value_sum[...] = jnp.zeros_like(value_sum)
    for block in range(query.shape[0] // size):
        low, high = key_start(block, size), (block + 1) * size
        rows = slice(block * size, high)
        probs = probabilities(seg_row, seg_col, query[rows, :], key, block, size)
        value_sum[low:high, :] += mm(probs.astype(BF16), d_attended[rows, :])
        d_probs = times_trans(value[low:high, :], d_attended[rows, :])
        inner = jnp.sum(probs * d_probs, axis=0, keepdims=True)
        d_scores = (probs * (d_probs - inner)).astype(BF16)
        d_query[rows, :] = (trans_times(d_scores, key[low:high, :]) * SCALING).astype(BF16)
        key_sum[low:high, :] += mm(d_scores, query[rows, :])
    d_key[...] = key_sum[...].astype(BF16)
    d_value[...] = value_sum[...].astype(BF16)


def segment_views(segments):
    seqs, length = segments.shape
    return segments.reshape(seqs, 1, length), segments.reshape(seqs, length, 1)


def attend(segments, query, key, value, groups):
    length, local = query.shape
    part = length // groups // PARTS
    tall = pl.BlockSpec((length, HEAD_DIM), lambda h: (0, h))
    out = jax.ShapeDtypeStruct((groups, part, local), BF16)
    return pl.pallas_call(
        functools.partial(forward_kernel, min(256, length)),
        grid=(local // HEAD_DIM,),
        in_specs=[
            pl.BlockSpec((None, 1, length), lambda h: (0, 0, 0)),
            pl.BlockSpec((None, length, 1), lambda h: (0, 0, 0)),
        ]
        + [tall] * 3,
        out_specs=[pl.BlockSpec((groups, part, HEAD_DIM), lambda h: (0, 0, h))] * PARTS,
        out_shape=[out] * PARTS,
        compiler_params=pltpu.CompilerParams(vmem_limit_bytes=VMEM),
        cost_estimate=cost(4 * length * length * local),
    )(*segment_views(segments), query, key, value)


def attend_back(segments, query, key, value, got):
    length = query.shape[0]
    tall = pl.BlockSpec((length, HEAD_DIM), lambda h: (0, h))
    return pl.pallas_call(
        functools.partial(backward_kernel, min(256, length)),
        grid=(query.shape[1] // HEAD_DIM,),
        in_specs=[
            pl.BlockSpec((None, 1, length), lambda h: (0, 0, 0)),
            pl.BlockSpec((None, length, 1), lambda h: (0, 0, 0)),
        ]
        + [tall] * 3
        + [pl.BlockSpec(got.shape[:3] + (HEAD_DIM,), lambda h: (0, 0, 0, h))],
        out_specs=[tall] * 3,
        scratch_shapes=[
            pltpu.VMEM((length, HEAD_DIM), BF16),
            pltpu.VMEM((length, HEAD_DIM), F32),
            pltpu.VMEM((length, HEAD_DIM), F32),
        ],
        out_shape=[jax.ShapeDtypeStruct(query.shape, BF16)] * 3,
        compiler_params=pltpu.CompilerParams(vmem_limit_bytes=VMEM),
        cost_estimate=cost(10 * query.shape[0] * length * query.shape[1]),
    )(*segment_views(segments), query, key, value, got)


def place_bits(blocks):
    return blocks.bit_length() - 1


def xor_source(place, me, bits):
    distance = 0
    for bit in range(bits):
        distance = distance + (((place >> (bits - 1 - bit)) & 1) << bit)
    return distance ^ me


def norm_rows(values, gain, bias):
    average = jnp.mean(values, axis=-1, keepdims=True)
    centred = values - average
    inverse = lax.rsqrt(jnp.mean(centred * centred, axis=-1, keepdims=True) + EPSILON)
    return centred * inverse * gain + bias


def project_kernel(x, gain, bias, wq, bq, wk, wv, bv, normed, query, key, value):
    low = norm_rows(x[...].astype(F32), gain[...], bias[...]).astype(BF16)
    normed[...] = low
    query[...] = ((mm(low, wq[...]) + bq[...]) * SCALING).astype(BF16)
    key[...] = mm(low, wk[...]).astype(BF16)
    value[...] = (mm(low, wv[...]) + bv[...]).astype(BF16)


def whole_spec(array):
    return pl.BlockSpec(array.shape, lambda *_: (0,) * array.ndim)


def project(x, gain, bias, wq, bq, wk, wv, bv):
    rows, width = x.shape
    local = wq.shape[1]
    size = min(512, rows)
    args = [x] + [v.reshape(1, -1) if v.ndim == 1 else v for v in (gain, bias, wq, bq, wk, wv, bv)]
    tall = pl.BlockSpec((size, width), lambda i: (i, 0))
    thin = pl.BlockSpec((size, local), lambda i: (i, 0))
    shape = jax.ShapeDtypeStruct((rows, local), BF16)
    return pl.pallas_call(
        project_kernel,
        grid=(rows // size,),
        in_specs=[tall] + [whole_spec(a) for a in args[1:]],
        out_specs=[tall] + [thin] * 3,
        out_shape=[jax.ShapeDtypeStruct(x.shape, BF16)] + [shape] * 3,
        compiler_params=pltpu.CompilerParams(vmem_limit_bytes=VMEM),
        cost_estimate=cost(6 * rows * width * local),
    )(*args)


def middle_kernel(
    steps, here_ref, heads, wo, x, bo, gain, bias, wup, bup, d_hid, wup_rows,
    own_mid, low_out, hidden, d_up, *rest,
):
    first, second = steps
    *terms, mid, low, d_low = rest
    step = pl.program_id(0)
    block = wo.shape[1]
    here = here_ref[1]
    local = heads.shape[2]

    @pl.when(step == 0)
    def _():
        for t in range(heads.shape[0]):
            low[:, t * local : (t + 1) * local] = heads[t]

    @pl.when(step < first)
    def _():
        branch = mm(low[...], wo[...])
        values = x[...].reshape(branch.shape).astype(F32)
        columns = pl.ds(pl.multiple_of(step * block, block), block)
        mid[:, columns] = values + (branch + bo[...])

    @pl.when(step == first)
    def _():
        low[...] = norm_rows(mid[...], gain[...], bias[...]).astype(BF16)
        part = own_mid.shape[0]
        own_mid[...] = mid[pl.ds(pl.multiple_of(here * part, part), part), :]

    @pl.when((step >= first) & (step < first + second))
    def _():
        piece = 256
        for start in range(0, wup.shape[1], piece):
            columns = slice(start, start + piece)
            up_value = mm(low[...], wup[:, columns]) + bup[:, columns]
            below = 0.5 + 0.5 * lax.erf(up_value * (0.5**0.5))
            density = jnp.exp(-0.5 * up_value * up_value) * 0.3989422804014327
            hidden[:, columns] = (up_value * below).astype(BF16)
            slope = ((below + up_value * density) * d_hid[:, columns].astype(F32)).astype(BF16)
            d_up[:, columns] = slope
            place = pl.multiple_of((step - first) * wup.shape[1] + start, piece)
            d_low[:, pl.ds(place, piece)] = slope

    @pl.when(step >= first + second)
    def _():
        value = times_trans(d_low[...], wup_rows[...]).astype(BF16)

        for k, term in enumerate(terms):
            start = first + second + k * first // len(terms)

            @pl.when((step >= start) & (step < start + first // len(terms)))
            def _():
                term[...] = value

        columns = pl.ds(pl.multiple_of((step - first - second) * block, block), block)
        low_out[...] = low[:, columns]


def middle_call(split, c, here, heads, wo, x, bo, gain, bias, wup, bup, d_hid):
    groups, _, part, width = x.shape
    rows = groups * part
    hidden = wup.shape[1]
    block = 512
    first, second = width // block, hidden // block
    bo, gain, bias, bup = (v.reshape(1, -1) for v in (bo, gain, bias, bup))

    def at(index, low, count):
        return jnp.clip(index - low, 0, count - 1)

    def columns(tall, low, count):
        return pl.BlockSpec((tall, block), lambda i, h: (0, at(i, low, count)))

    third = first + second
    return pl.pallas_call(
        functools.partial(middle_kernel, (first, second)),
        grid_spec=pltpu.PrefetchScalarGridSpec(
            num_scalar_prefetch=1,
            grid=(first + second + first,),
            in_specs=[
                whole_spec(heads),
                columns(width, 0, first),
                pl.BlockSpec(
                    (groups, None, part, block), lambda i, h: (0, c, 0, at(i, 0, first))
                ),
                columns(1, 0, first),
                whole_spec(gain),
                whole_spec(bias),
                columns(width, first, second),
                columns(1, first, second),
                pl.BlockSpec((None, rows, block), lambda i, h: (c, 0, at(i, first, second))),
                pl.BlockSpec((block, hidden), lambda i, h: (at(i, third, first), 0)),
            ],
            out_specs=[
                pl.BlockSpec((part, width), lambda i, h: (0, 0)),
                columns(rows, third, first),
                columns(rows, first, second),
                columns(rows, first, second),
            ]
            + [columns(rows, third + k * first // split, first // split) for k in range(split)],
            scratch_shapes=[
                pltpu.VMEM((rows, width), F32),
                pltpu.VMEM((rows, width), BF16),
                pltpu.VMEM((rows, hidden), BF16),
            ],
        ),
        out_shape=[
            jax.ShapeDtypeStruct((part, width), F32),
            jax.ShapeDtypeStruct((rows, width), BF16),
            jax.ShapeDtypeStruct((rows, hidden), BF16),
            jax.ShapeDtypeStruct((rows, hidden), BF16),
        ]
        + [jax.ShapeDtypeStruct((rows, width // split), BF16)] * split,
        compiler_params=pltpu.CompilerParams(vmem_limit_bytes=VMEM),
        cost_estimate=cost(2 * rows * width * (width + 2 * hidden)),
    )(here, heads, wo, x, bo, gain, bias, wup, bup, d_hid, wup)


def middle_back_kernel(count, *refs):
    (terms, mid, cot, gain, wo), before = refs[:5], refs[5 : 5 + count]
    d_mid, d_branch, sums, d_att = refs[5 + count :]

    @pl.when(pl.program_id(0) == 0)
    def _():
        d_normed = terms[...].astype(F32)
        values = mid[...]
        centred = values - jnp.mean(values, axis=-1, keepdims=True)
        inverse = lax.rsqrt(jnp.mean(centred * centred, axis=-1, keepdims=True) + EPSILON)
        xhat = centred * inverse
        total = cot[...].astype(F32) + norm_back(d_normed, gain[...], xhat, inverse)
        low = total.astype(BF16)
        d_mid[...] = total
        d_branch[...] = low
        sums[0:1, :] = jnp.sum(d_normed * xhat, axis=0, keepdims=True)
        sums[1:2, :] = jnp.sum(d_normed, axis=0, keepdims=True)
        sums[2:3, :] = jnp.sum(low.astype(F32), axis=0, keepdims=True)

    for c in range(count):
        d_att[c] = before[c][...]
    d_att[count] = times_trans(d_branch[...], wo[...]).astype(BF16)


def middle_back(terms, mid, cot, gain, wo, before):
    part, width = mid.shape
    groups = lax.axis_size("tensor")
    block = width // groups
    count = len(before) + 1
    rows = pl.BlockSpec((part, width), lambda j: (0, 0))
    return pl.pallas_call(
        functools.partial(middle_back_kernel, len(before)),
        grid=(groups,),
        in_specs=[
            rows,
            rows,
            rows,
            pl.BlockSpec((1, width), lambda j: (0, 0)),
            pl.BlockSpec((block, width), lambda j: (j, 0)),
        ]
        + [pl.BlockSpec((None, None, part, block), lambda j: (j, 0, 0, 0))] * len(before),
        out_specs=[
            rows,
            rows,
            pl.BlockSpec((8, width), lambda j: (0, 0)),
            pl.BlockSpec((None, count, part, block), lambda j: (j, 0, 0, 0)),
        ],
        out_shape=[
            jax.ShapeDtypeStruct((part, width), F32),
            jax.ShapeDtypeStruct((part, width), BF16),
            jax.ShapeDtypeStruct((8, width), F32),
            jax.ShapeDtypeStruct((groups, count, part, block), BF16),
        ],
        compiler_params=pltpu.CompilerParams(vmem_limit_bytes=VMEM),
        cost_estimate=cost(2 * part * width * width),
    )(terms, mid, cot, gain.reshape(1, -1), wo, *before)


def gradient_terms(lefts, groups, me, blocks):
    half = blocks // 2
    bits = place_bits(blocks)
    part_of = [left[1] if isinstance(left, tuple) else None for left in lefts]
    lefts = [left[0] if isinstance(left, tuple) else left for left in lefts]
    count = len(lefts)
    rights = [right for group in groups for right in group]
    entry_of = [right[1] if isinstance(right, tuple) else None for right in rights]
    rights = [right[0] if isinstance(right, tuple) else right for right in rights]
    width = lefts[0].shape[-1] // blocks
    total = sum(right.shape[-1] for right in rights[::count])

    def source(j, m):
        return xor_source(jnp.where(j < half, j + half, j - half), m[0], bits)

    def right_spec(right, t):
        if t is None:
            return whole_spec(right)
        return pl.BlockSpec((None, None) + right.shape[2:], lambda j, m: (t, m[1], 0, 0))

    def left_spec(left, c):
        if c is None:
            return pl.BlockSpec((left.shape[0], width), lambda j, m: (0, source(j, m)))
        shape = (left.shape[0], None, left.shape[2], width)
        return pl.BlockSpec(shape, lambda j, m: (0, c, 0, source(j, m)))

    def kernel(me_ref, *refs):
        left_refs, right_refs = refs[:count], refs[count:]
        send, keep = refs[-2:]
        step = pl.program_id(0)

        def fill(target):
            place = 0
            turned = [ref[...].reshape(-1, width).T for ref in left_refs]
            for g in range(len(groups)):
                value = None
                for i in range(count):
                    more = mm(turned[i], right_refs[g * count + i][...])
                    value = more if value is None else value + more
                columns = value.shape[1]
                target[:, place : place + columns] = value.astype(BF16)
                place += columns

        @pl.when(step < half)
        def _():
            fill(send)

        @pl.when(step >= half)
        def _():
            fill(keep)

    shape = jax.ShapeDtypeStruct((half, width, total), BF16)
    return pl.pallas_call(
        kernel,
        grid_spec=pltpu.PrefetchScalarGridSpec(
            num_scalar_prefetch=1,
            grid=(blocks,),
            in_specs=[left_spec(left, c) for left, c in zip(lefts, part_of)]
            + [right_spec(right, t) for right, t in zip(rights, entry_of)],
            out_specs=[
                pl.BlockSpec((None, width, total), lambda j, m: (jnp.minimum(j, half - 1), 0, 0)),
                pl.BlockSpec((None, width, total), lambda j, m: (jnp.maximum(j - half, 0), 0, 0)),
            ],
        ),
        out_shape=[shape, shape],
        compiler_params=pltpu.CompilerParams(vmem_limit_bytes=VMEM),
        cost_estimate=cost(2**20),
    )(me, *lefts, *rights)


def normed_back_kernel(dq, dk, dv, wq, wk, wv, x, terms, gain_sum, bias_sum):
    total = times_trans(dq[...], wq[...]) + times_trans(dk[...], wk[...])
    total = total + times_trans(dv[...], wv[...])
    terms[...] = total.astype(BF16)
    values = x[...].astype(F32)
    centred = values - jnp.mean(values, axis=-1, keepdims=True)
    inverse = lax.rsqrt(jnp.mean(centred * centred, axis=-1, keepdims=True) + EPSILON)

    @pl.when(pl.program_id(0) == 0)
    def _():
        gain_sum[...] = jnp.zeros_like(gain_sum)
        bias_sum[...] = jnp.zeros_like(bias_sum)

    gain_sum[...] += jnp.sum(total * (centred * inverse), axis=0, keepdims=True)
    bias_sum[...] += jnp.sum(total, axis=0, keepdims=True)


def normed_back(dq, dk, dv, wq, wk, wv, x):
    rows, width = x.shape
    size = min(512, rows)
    thin = pl.BlockSpec((size, dq.shape[1]), lambda i: (i, 0))
    tall = pl.BlockSpec((size, width), lambda i: (i, 0))
    line = pl.BlockSpec((1, width), lambda i: (0, 0))
    return pl.pallas_call(
        normed_back_kernel,
        grid=(rows // size,),
        in_specs=[thin] * 3 + [whole_spec(w) for w in (wq, wk, wv)] + [tall],
        out_specs=[tall, line, line],
        out_shape=[
            jax.ShapeDtypeStruct((rows, width), BF16),
            jax.ShapeDtypeStruct((1, width), F32),
            jax.ShapeDtypeStruct((1, width), F32),
        ],
        compiler_params=pltpu.CompilerParams(vmem_limit_bytes=VMEM),
        cost_estimate=cost(6 * rows * width * dq.shape[1]),
    )(dq, dk, dv, wq, wk, wv, x)


def input_back(d_normed, x, d_mid, gain):
    rows, width = x.shape
    size = min(64, rows)

    def kernel(terms, x_ref, mid, gain_ref, out):
        values = x_ref[...].astype(F32)
        centred = values - jnp.mean(values, axis=-1, keepdims=True)
        inverse = lax.rsqrt(jnp.mean(centred * centred, axis=-1, keepdims=True) + EPSILON)
        back = norm_back(terms[...].astype(F32), gain_ref[...], centred * inverse, inverse)
        out[...] = mid[...] + back

    tall = pl.BlockSpec((size, width), lambda i: (i, 0))
    return pl.pallas_call(
        kernel,
        grid=(rows // size,),
        in_specs=[tall, tall, tall, pl.BlockSpec((1, width), lambda i: (0, 0))],
        out_specs=tall,
        out_shape=jax.ShapeDtypeStruct((rows, width), F32),
        compiler_params=pltpu.CompilerParams(vmem_limit_bytes=VMEM),
        cost_estimate=cost(2**20),
    )(d_normed, x, d_mid, gain.reshape(1, -1))


def both_parts(lefts, weight, transposed, columns, groups=None):
    block = min(512, columns)
    part_of = [left[1] if isinstance(left, tuple) else None for left in lefts]
    lefts = [left[0] if isinstance(left, tuple) else left for left in lefts]
    depth = lefts[0].shape[-1]
    rows = lefts[0].shape[0] * (1 if part_of[0] is None else lefts[0].shape[2])

    def kernel(*refs):
        weight_ref, out = refs[-2:]
        for c in range(len(lefts)):
            left = refs[c][...].reshape(-1, depth)
            product = times_trans if transposed else mm
            value = product(left, weight_ref[...]).astype(BF16)
            if groups is None:
                out[c] = value
            else:
                out[:, c] = value.reshape(groups, rows // groups, block)

    def left_spec(left, c):
        if c is None:
            return whole_spec(left)
        return pl.BlockSpec((left.shape[0], None) + left.shape[2:], lambda j: (0, c, 0, 0))

    shape = (len(lefts), rows)
    if groups is not None:
        shape = (groups, len(lefts), rows // groups)
    if transposed:
        weight_spec = pl.BlockSpec((block, depth), lambda j: (j, 0))
    else:
        weight_spec = pl.BlockSpec((depth, block), lambda j: (0, j))
    return pl.pallas_call(
        kernel,
        grid=(columns // block,),
        in_specs=[left_spec(left, c) for left, c in zip(lefts, part_of)] + [weight_spec],
        out_specs=pl.BlockSpec(shape + (block,), lambda j: (0,) * len(shape) + (j,)),
        out_shape=jax.ShapeDtypeStruct(shape + (columns,), BF16),
        compiler_params=pltpu.CompilerParams(vmem_limit_bytes=VMEM),
        cost_estimate=cost(2 * len(lefts) * rows * depth * columns),
    )(*lefts, weight)


def swap_bit(values, axis, bit):
    size = lax.axis_size(axis)
    return lax.ppermute(values, axis, [(i, i ^ (1 << bit)) for i in range(size)])


def third(k, steps):
    return range((k - 1) * steps // 3 + 1, k * steps // 3 + 1)


def fence(things, arrays=()):
    lists = [thing.live for thing in things]
    flat = lax.optimization_barrier(tuple(v for values in lists for v in values) + tuple(arrays))
    place = 0
    for thing, values in zip(things, lists):
        thing.live = list(flat[place : place + len(values)])
        place += len(values)
    return flat[place:]


def exchange(values):
    return lax.all_to_all(values, "tensor", 0, 0)


def add_and_split(sources, outs, dims):
    places = 2**dims
    rows = sources[0][0].shape[1]
    size = min(64, rows)
    widths = [sum(stop - start for _, start, stop in picks) for picks, _ in outs]

    def kernel(*refs):
        target = 2 * len(sources)
        for picks, dim in outs:
            shift = dims - 1 - dim
            for half in range(2):
                chosen = [p for p in range(places) if (p >> shift) & 1 == half]
                at = 0
                for source, start, stop in picks:
                    keep, got = refs[2 * source : 2 * source + 2]
                    for q, p in enumerate(chosen):
                        value = keep[p, :, start:stop].astype(F32) + got[p, :, start:stop].astype(F32)
                        refs[target][q, :, at : at + stop - start] = value.astype(BF16)
                    at += stop - start
                target += 1

    def block(count, columns):
        return pl.BlockSpec((count, size, columns), lambda i: (0, i, 0))

    flat = [v for pair in sources for v in pair]
    return pl.pallas_call(
        kernel,
        grid=(rows // size,),
        in_specs=[block(places, v.shape[2]) for v in flat],
        out_specs=[block(places // 2, w) for w in widths for _ in range(2)],
        out_shape=[
            jax.ShapeDtypeStruct((places // 2, rows, w), BF16) for w in widths for _ in range(2)
        ],
        compiler_params=pltpu.CompilerParams(vmem_limit_bytes=VMEM),
        cost_estimate=cost(2**20),
    )(*flat)


class DpSum:
    def __init__(self, send, keep, cuts):
        self.live = [send, keep]
        self.cuts = cuts
        self.rest = place_bits(lax.axis_size("dp")) - 1
        self.width = keep.shape[-1] // cuts
        self.left = [list(range(1, self.rest + 1)) for _ in range(2)]

    def core(self):
        self.live = [self.live[1], swap_bit(self.live[0], "dp", 0)]

    def dim(self, odd):
        return len(self.left[odd]) - 1 if odd else 0

    def split(self):
        outs = [
            ([(0, c * self.width, (c + 1) * self.width)], self.dim(c % 2)) for c in range(self.cuts)
        ]
        self.live = list(add_and_split([tuple(self.live)], outs, self.rest))

    def first(self, *cuts):
        for c in cuts:
            values = self.live[2 * c + 1]
            self.live[2 * c + 1] = swap_bit(values, "dp", self.left[c % 2][self.dim(c % 2)])

    def add(self):
        bits = [left[self.dim(odd)] for odd, left in enumerate(self.left)]
        for odd in range(2):
            self.left[odd].remove(bits[odd])
        count = len(self.live) // 2
        sources = [(self.live[2 * k], self.live[2 * k + 1]) for k in range(count)]
        outs = [
            ([(k, 0, sources[k][0].shape[2]) for k in range(odd, count, 2)], self.dim(odd))
            for odd in range(2)
        ]
        self.live = list(add_and_split(sources, outs, len(self.left[0])))

    def send(self):
        for odd in range(2):
            bit = self.left[odd][self.dim(odd)]
            self.live[2 * odd + 1] = swap_bit(self.live[2 * odd + 1], "dp", bit)
        while len(self.left[0]) > 1:
            self.add()
            self.send()

    def total(self):
        sums = [
            self.live[2 * odd][0].astype(F32) + self.live[2 * odd + 1][0].astype(F32)
            for odd in range(2)
        ]
        size = self.width
        return [
            sums[c % 2][:, c // 2 * size : (c // 2 + 1) * size] for c in range(self.cuts)
        ]


class WeightGather:
    def __init__(self, own, me):
        self.blocks = lax.axis_size("dp")
        self.size = lax.axis_size("tensor")
        self.usual = (self.size, self.blocks) == (4, 8)
        self.me = me
        share = own.shape[1 if self.usual else 0] // self.blocks
        axis = 1 if self.usual else 0
        self.live = [lax.dynamic_slice_in_dim(own, me[0] * share, share, axis)]

    def advance(self, k):
        if not self.usual:
            if k == 0:
                self.live = [lax.all_gather(self.live[0], ("tensor", "dp"), axis=0, tiled=True)]
            return
        if k == 0:
            own = self.live[0]
            self.live += [
                lax.ppermute(own, "tensor", [(i, (i + m) % self.size) for i in range(self.size)])
                for m in range(1, self.size)
            ]
        elif k == 1:
            own, one, two, three = self.live
            even = lax.axis_index("tensor") % 2 == 0
            near = jnp.concatenate([jnp.where(even, own, one), jnp.where(even, three, own)])
            far = jnp.concatenate([jnp.where(even, two, three), jnp.where(even, one, two)])
            self.live = [near, swap_bit(near, "dp", 1), far, swap_bit(far, "dp", 2)]
            self.live += [swap_bit(near, "dp", 0), swap_bit(far, "dp", 0)]
        elif k == 2:
            near, near_one, far, far_one, near_core, far_core = self.live
            near, far = jnp.stack([near, near_one]), jnp.stack([far, far_one])
            self.live = [near, far, near_core[None], far_core[None]]
            self.live += [swap_bit(near, "dp", 2), swap_bit(far, "dp", 1)]
            self.live += [swap_bit(near_one, "dp", 0)[None], swap_bit(far_one, "dp", 0)[None]]
        elif k == 3:
            near, far, near_core, far_core, near_two, far_two, near_one_core, far_one_core = self.live
            own = [(near, 0), (near, 1), (far, 0), (far, 1)]
            other = [(v, 0) for v in (near_core, near_one_core, far_core, far_one_core)]
            self.live = [near_two, far_two, self.place(own, other, 0, None)]
        else:
            near_two, far_two, half = self.live
            self.live = [near_two, swap_bit(near_two, "dp", 0)]
            self.live += [far_two, swap_bit(far_two, "dp", 0), half]

    def place(self, own, other, late, half):
        rows, width = own[0][0].shape[1:]
        blocks = own + other

        def kernel(me_ref, *refs):
            out = refs[-1]
            step, odd = pl.program_id(0), me_ref[0] & 1
            for k in range(4):
                for flip in range(2):

                    @pl.when((step == k) & (odd == flip))
                    def _():
                        out[:, flip * width : (flip + 1) * width] = refs[k][...]
                        out[:, (1 - flip) * width : (2 - flip) * width] = refs[k + 4][...]

        def source(entry):
            return pl.BlockSpec((None, rows, width), lambda s, m: (entry, 0, 0))

        def target(s, m):
            top, one = s < 2, s & 1
            low = jnp.where(top, 2 * one + 4 * late, 4 * one + 2 * late)
            return (jnp.where(top, m[2], 1 - m[2]), (low ^ m[0]) >> 1)

        more = [] if half is None else [half]
        return pl.pallas_call(
            kernel,
            grid_spec=pltpu.PrefetchScalarGridSpec(
                num_scalar_prefetch=1,
                grid=(4,),
                in_specs=[source(entry) for _, entry in blocks]
                + [pl.BlockSpec(memory_space=pl.ANY)] * len(more),
                out_specs=pl.BlockSpec((rows, 2 * width), target),
            ),
            out_shape=jax.ShapeDtypeStruct((2 * rows, 8 * width), BF16),
            input_output_aliases={9: 0} if more else {},
            compiler_params=pltpu.CompilerParams(vmem_limit_bytes=VMEM),
            cost_estimate=cost(2**20),
        )(self.me, *[array for array, _ in blocks], *more)

    def whole(self):
        if not self.usual:
            return self.live[0]
        near, near_core, far, far_core, half = self.live
        own = [(near, 0), (near, 1), (far, 0), (far, 1)]
        other = [(near_core, 0), (near_core, 1), (far_core, 0), (far_core, 1)]
        return self.place(own, other, 1, half)


class SmallSum:
    def __init__(self, vectors, me):
        self.vectors = vectors
        self.blocks = blocks = lax.axis_size("dp")
        self.bits = place_bits(blocks)
        places = jnp.stack([xor_source(p, me, self.bits) for p in range(blocks)]).reshape(-1)
        self.ordered = sorted(range(len(vectors)), key=lambda i: not vectors[i][1])
        wide = [vectors[i][0].reshape(blocks, -1) for i in self.ordered]
        wide = jnp.take(jnp.concatenate(wide, axis=1), places, axis=0)
        self.live = [wide.reshape((2,) * self.bits + wide.shape[1:])]

    def move(self):
        self.steps = getattr(self, "steps", 0) + 1
        while self.live[0].ndim > 1:
            values = self.live[0]
            self.live = [values[0] + swap_bit(values[1], "dp", self.bits - values.ndim + 1)]
            if self.steps < 3:
                return

    def tensor(self):
        values = self.live[0]
        both = sum(v[0].shape[0] // self.blocks for v in self.vectors if v[1])
        summed, alone = values[..., :both], values[..., both:]
        for bit in range(place_bits(lax.axis_size("tensor"))):
            summed = summed + swap_bit(summed, "tensor", bit)
        self.live = [jnp.concatenate([summed, alone], axis=-1)]

    def total(self):
        out, start = [None] * len(self.vectors), 0
        for i in self.ordered:
            size = self.vectors[i][0].shape[0] // self.blocks
            out[i] = self.live[0][start : start + size]
            start += size
        return out


def on_device(
    inputs,
    segments,
    cotangent,
    norm1_gain,
    norm1_bias,
    query_weight,
    query_bias,
    key_weight,
    value_weight,
    value_bias,
    output_weight,
    output_bias,
    norm2_gain,
    norm2_bias,
    up_weight,
    up_bias,
    down_weight,
    down_bias,
):
    groups = lax.axis_size("tensor")
    blocks = lax.axis_size("dp")
    here = lax.axis_index("tensor").astype(jnp.int32)
    side = here // (groups // 2)
    me = lax.axis_index("dp").astype(jnp.int32)
    me = jnp.stack([me, here, side])
    rows, width = inputs.shape
    share = rows // groups
    part = share // PARTS
    local = query_weight.shape[1]
    size = width // blocks

    def by_part(values):
        return values.reshape(groups, PARTS, part, values.shape[1])

    def own(values):
        return lax.dynamic_slice_in_dim(values, here * share, share, 0)

    weight = WeightGather(output_weight, me)
    weight.advance(0)
    normed, query, key, value = project(
        inputs,
        norm1_gain,
        norm1_bias,
        query_weight,
        query_bias,
        key_weight,
        value_weight,
        value_bias,
    )
    heads = attend(segments, query, key, value, groups)
    heads = [h.reshape(groups * part, local) for h in heads]
    cot, *heads = fence([weight], (cotangent, *heads))

    heads[0] = lax.all_gather(heads[0], "tensor", axis=0)
    weight.advance(1)
    cot, heads[1] = fence([weight], (cot, heads[1]))
    heads[1] = lax.all_gather(heads[1], "tensor", axis=0)
    weight.advance(2)
    cot_parts = by_part(cot)
    cots = [(cot_parts, c) for c in range(PARTS)]
    d_hidden = both_parts(cots, down_weight, True, down_weight.shape[0])
    d_hidden, cot = fence([], (d_hidden, cot))
    weight.advance(3)
    d_hidden, cot = fence([weight], (d_hidden, cot))
    weight.advance(4)
    fence([weight])
    whole = weight.whole()
    whole, heads[0] = fence([], (whole, heads[0]))

    own_mid, low, hidden, d_up, terms = ([None] * PARTS for _ in range(5))

    def middle(c):
        own_mid[c], low[c], hidden[c], d_up[c], *term = middle_call(
            1,
            c,
            me,
            heads[c],
            whole,
            by_part(inputs),
            output_bias,
            norm2_gain,
            norm2_bias,
            up_weight,
            up_bias,
            d_hidden,
        )
        terms[c] = term[0].reshape(groups, part, width)

    middle(0)
    terms[0], heads[1] = fence([], (terms[0], heads[1]))

    terms[0] = lax.psum_scatter(terms[0], "tensor", scatter_dimension=0)
    middle(1)
    cot_own = own(cot)
    terms[1], cot_own, low[0], low[1], d_up[0], d_up[1] = fence(
        [], (terms[1], cot_own, *low, *d_up)
    )

    terms[1] = lax.psum_scatter(terms[1], "tensor", scatter_dimension=0)
    up_terms = gradient_terms(low, [d_up], me, blocks)
    d_mids, d_branches, sums = ([None] * PARTS for _ in range(3))

    def back(c, before):
        d_mids[c], d_branches[c], sums[c], d_att = middle_back(
            terms[c], own_mid[c], cot_own[c * part : (c + 1) * part], norm2_gain, whole, before
        )
        return d_att

    terms[0], hidden[0], hidden[1], *up_terms = fence([], (terms[0], *hidden, *up_terms))
    d_att = back(0, [])
    d_att, hidden[0], hidden[1] = fence([], (d_att, *hidden))
    out_terms = both_parts(hidden, down_weight, False, width, groups)
    out_terms, hidden[0], hidden[1] = fence([], (out_terms, *hidden))
    down_terms = gradient_terms(cots, [hidden], me, blocks)
    cot_sum = column_sums(cot)
    up_bias_sum = column_sums(d_up[0]) + column_sums(d_up[1])
    up_sum = DpSum(*up_terms, 2)
    down_sum = DpSum(*down_terms, 2)
    terms[1], out_terms, d_branches[0], cot_sum, up_bias_sum, d_att = fence(
        [up_sum, down_sum], (terms[1], out_terms, d_branches[0], cot_sum, up_bias_sum, d_att)
    )

    d_att = back(1, [d_att])
    d_att, *d_branches = fence([up_sum, down_sum], (d_att, *d_branches))
    d_att = exchange(d_att)
    up_sum.core()
    down_sum.core()
    views = [h.reshape(groups, groups, part, local) for h in heads]
    wo_terms = gradient_terms(d_branches, [[(v, t) for v in views] for t in range(groups)], me, blocks)
    wo_sum = DpSum(*wo_terms, 2)
    up_sum.split()
    d_att, out_terms = fence([wo_sum, up_sum, down_sum], (d_att, out_terms))

    out_sum = lax.psum_scatter(out_terms, "tensor", scatter_dimension=0)
    up_sum.first(0, 1)
    wo_sum.core()
    d_query, d_key, d_value = attend_back(segments, query, key, value, d_att)
    wo_sum.split()
    d_query, d_key, d_value = fence([up_sum, wo_sum, down_sum], (d_query, d_key, d_value))
    wo_sum.first(0, 1)
    qkv_sum = DpSum(
        *gradient_terms([normed], [[d] for d in (d_query, d_key, d_value)], me, blocks), 2
    )
    down_sum.split()
    d_query, d_key, d_value = fence([wo_sum, qkv_sum, down_sum], (d_query, d_key, d_value))
    qkv_sum.core()
    down_sum.first(0, 1)
    terms_in, gain1, bias1 = normed_back(
        d_query, d_key, d_value, query_weight, key_weight, value_weight, inputs
    )
    gain1, bias1, terms_in, d_query, d_value = fence(
        [qkv_sum, wo_sum], (gain1, bias1, terms_in, d_query, d_value)
    )

    d_normed = lax.psum_scatter(
        terms_in.reshape(groups, share, width), "tensor", scatter_dimension=0
    )
    qkv_sum.split()
    wo_sum.add()
    gain1, bias1, d_query, d_value = fence(
        [qkv_sum, wo_sum, down_sum], (gain1, bias1, d_query, d_value)
    )
    qkv_sum.first(0, 1)
    wo_sum.send()
    two = sums[0] + sums[1]
    small = SmallSum(
        [
            (gain1[0], True),
            (bias1[0], True),
            (two[0], True),
            (two[1], True),
            (two[2], True),
            (cot_sum, False),
            (column_sums(d_query), False),
            (column_sums(d_value), False),
            (up_bias_sum, False),
        ],
        me[:1],
    )
    down_sum.add()
    out_sum, *_ = fence([qkv_sum, wo_sum, down_sum, small, up_sum], (out_sum,))
    qkv_sum.add()
    qkv_sum.send()
    down_sum.send()
    small.tensor()
    wo_terms = jnp.concatenate(wo_sum.total(), axis=1).T
    wo_terms = wo_terms.astype(BF16).reshape(groups, local, size)
    to_all = [
        lax.dynamic_index_in_dim(wo_terms, (here - m) % groups, 0, keepdims=False)
        for m in range(groups)
    ]
    up_sum.add()
    out_sum, *to_all = fence([qkv_sum, small, down_sum, up_sum], (out_sum, *to_all))
    output_weight_grad = to_all[0].astype(F32)
    for m in range(1, groups):
        ring = [(i, (i - m) % groups) for i in range(groups)]
        output_weight_grad = output_weight_grad + lax.ppermute(to_all[m], "tensor", ring).astype(F32)
    up_sum.send()
    small.move()
    small.move()
    small.move()
    total = [own_mid[c] + (out_sum[c].astype(F32) + down_bias) for c in range(PARTS)]
    output = jnp.concatenate([t.astype(BF16) for t in total], axis=0)
    qkv_grad = jnp.concatenate(qkv_sum.total(), axis=1)
    up_weight_grad = jnp.concatenate(up_sum.total(), axis=1)
    down_weight_grad = jnp.concatenate(down_sum.total(), axis=1).T
    up_weight_grad, down_weight_grad, qkv_grad, output_weight_grad = fence(
        [small], (up_weight_grad, down_weight_grad, qkv_grad, output_weight_grad)
    )
    (d_normed,) = fence([small], (d_normed,))
    input_grad = input_back(d_normed, own(inputs), jnp.concatenate(d_mids, axis=0), norm1_gain)
    (
        norm1_gain_grad,
        norm1_bias_grad,
        norm2_gain_grad,
        norm2_bias_grad,
        output_bias_grad,
        down_bias_grad,
        query_bias_grad,
        value_bias_grad,
        up_bias_grad,
    ) = small.total()
    return (
        output,
        input_grad,
        norm1_gain_grad,
        norm1_bias_grad,
        qkv_grad[:, :local],
        query_bias_grad,
        qkv_grad[:, local : 2 * local],
        qkv_grad[:, 2 * local :],
        value_bias_grad,
        output_weight_grad,
        output_bias_grad,
        norm2_gain_grad,
        norm2_bias_grad,
        up_weight_grad,
        up_bias_grad,
        down_weight_grad,
        down_bias_grad,
    )


def solution(mesh):
    return jax.shard_map(
        on_device,
        mesh=mesh,
        in_specs=(
            P("dp", None),
            P("dp", None),
            P("dp", None),
            P(),
            P(),
            P(None, "tensor"),
            P("tensor"),
            P(None, "tensor"),
            P(None, "tensor"),
            P("tensor"),
            P("tensor", None),
            P(),
            P(),
            P(),
            P(None, "tensor"),
            P("tensor"),
            P("tensor", None),
            P(),
        ),
        out_specs=(
            P(("dp", "tensor"), None),
            P(("dp", "tensor"), None),
            P("dp"),
            P("dp"),
            P("dp", "tensor"),
            P(("tensor", "dp")),
            P("dp", "tensor"),
            P("dp", "tensor"),
            P(("tensor", "dp")),
            P("tensor", "dp"),
            P("dp"),
            P("dp"),
            P("dp"),
            P("dp", "tensor"),
            P(("tensor", "dp")),
            P("tensor", "dp"),
            P("dp"),
        ),
        check_vma=False,
    )
```

```python
import functools

import jax
import jax.numpy as jnp
from jax import lax
from jax.experimental import pallas as pl
from jax.experimental.pallas import tpu as pltpu
from jax.sharding import PartitionSpec as P

HEAD_DIM = 128
LONGEST = 512
EPSILON = 1e-05
MASKED_SCORE = -1e30
SCALING = HEAD_DIM ** (-0.5)
F32 = jnp.float32
BF16 = jnp.bfloat16
PARTS = 2
COST = 0
VMEM = 60 * 2**20


def mm(left_side, right_side):
    return lax.dot_general(
        left_side, right_side, (((1,), (0,)), ((), ())), preferred_element_type=F32
    )


def times_trans(left_side, right_side):
    return lax.dot_general(
        left_side, right_side, (((1,), (1,)), ((), ())), preferred_element_type=F32
    )


def trans_times(left_side, right_side):
    return lax.dot_general(
        left_side, right_side, (((0,), (0,)), ((), ())), preferred_element_type=F32
    )


def column_sums(values):
    return jnp.sum(values.astype(F32), axis=0)


def row_stats(rows):
    average = jnp.mean(rows, axis=-1, keepdims=True)
    centred = rows - average
    spread = jnp.mean(centred * centred, axis=-1, keepdims=True)
    return average, lax.rsqrt(spread + EPSILON)


def norm_back(d_normed, gain, xhat, inverse):
    scaled = d_normed * gain
    first = jnp.mean(scaled, axis=-1, keepdims=True)
    second = jnp.mean(scaled * xhat, axis=-1, keepdims=True)
    return inverse * (scaled - first - xhat * second)


def cost(flops):
    return pl.CostEstimate(flops=COST and flops, bytes_accessed=2**10, transcendentals=0)


def key_start(first):
    return max(0, (first - (LONGEST - 1)) // 256 * 256)


def segment_column(seg_row):
    length = seg_row.shape[1]
    return jnp.broadcast_to(seg_row[...], (128, length)).T[:, :1]


def probabilities(seg_row, seg_col, query, keys, first, last):
    low, high = key_start(first), last
    scores = times_trans(keys[low:high, :], query)
    shape = (high - low, last - first)
    key_place = lax.broadcasted_iota(jnp.int32, shape, 0) + low
    query_place = lax.broadcasted_iota(jnp.int32, shape, 1) + first
    same = seg_col[low:high, :] == seg_row[:, first:last]
    scores = jnp.where(same & (key_place <= query_place), scores, MASKED_SCORE)
    weights = jnp.exp(scores - jnp.max(scores, axis=0, keepdims=True))
    return weights * (1.0 / jnp.sum(weights, axis=0, keepdims=True))


def forward_kernel(c, seg_row, query, key, value, out):
    groups, part = out.shape[:2]
    seg_col = segment_column(seg_row)
    for t in range(groups):
        first = (t * PARTS + c) * part
        last = first + part
        low = key_start(first)
        probs = probabilities(seg_row, seg_col, query[first:last, :], key, first, last)
        out[t] = trans_times(probs.astype(BF16), value[low:last, :]).astype(BF16)


def backward_kernel(size, seg_row, query, key, value, got, *refs):
    d_query, d_key, d_value, d_attended, key_sum, value_sum = refs
    groups, parts, part = got.shape[:3]
    for t in range(groups):
        for c in range(parts):
            start = (t * parts + c) * part
            d_attended[start : start + part, :] = got[t, c]
    seg_col = segment_column(seg_row)
    key_sum[...] = jnp.zeros_like(key_sum)
    value_sum[...] = jnp.zeros_like(value_sum)
    for block in range(query.shape[0] // size):
        low, high = key_start(block * size), (block + 1) * size
        rows = slice(block * size, high)
        probs = probabilities(seg_row, seg_col, query[rows, :], key, block * size, high)
        value_sum[low:high, :] += mm(probs.astype(BF16), d_attended[rows, :])
        d_probs = times_trans(value[low:high, :], d_attended[rows, :])
        inner = jnp.sum(probs * d_probs, axis=0, keepdims=True)
        d_scores = (probs * (d_probs - inner)).astype(BF16)
        d_query[rows, :] = (trans_times(d_scores, key[low:high, :]) * SCALING).astype(BF16)
        key_sum[low:high, :] += mm(d_scores, query[rows, :])
    d_key[...] = key_sum[...].astype(BF16)
    d_value[...] = value_sum[...].astype(BF16)


def attend(c, segments, query, key, value, groups):
    length, local = query.shape
    part = length // groups // PARTS
    tall = pl.BlockSpec((length, HEAD_DIM), lambda h: (0, h))
    return pl.pallas_call(
        functools.partial(forward_kernel, c),
        grid=(local // HEAD_DIM,),
        in_specs=[pl.BlockSpec((1, length), lambda h: (0, 0))] + [tall] * 3,
        out_specs=pl.BlockSpec((groups, part, HEAD_DIM), lambda h: (0, 0, h)),
        out_shape=jax.ShapeDtypeStruct((groups, part, local), BF16),
        compiler_params=pltpu.CompilerParams(vmem_limit_bytes=VMEM),
        cost_estimate=cost(2**20),
    )(segments, query, key, value)


def attend_back(segments, query, key, value, got):
    length = query.shape[0]
    tall = pl.BlockSpec((length, HEAD_DIM), lambda h: (0, h))
    return pl.pallas_call(
        functools.partial(backward_kernel, min(256, length)),
        grid=(query.shape[1] // HEAD_DIM,),
        in_specs=[pl.BlockSpec((1, length), lambda h: (0, 0))]
        + [tall] * 3
        + [pl.BlockSpec(got.shape[:3] + (HEAD_DIM,), lambda h: (0, 0, 0, h))],
        out_specs=[tall] * 3,
        scratch_shapes=[
            pltpu.VMEM((length, HEAD_DIM), BF16),
            pltpu.VMEM((length, HEAD_DIM), F32),
            pltpu.VMEM((length, HEAD_DIM), F32),
        ],
        out_shape=[jax.ShapeDtypeStruct(query.shape, BF16)] * 3,
        compiler_params=pltpu.CompilerParams(vmem_limit_bytes=VMEM),
        cost_estimate=cost(10 * query.shape[0] * length * query.shape[1]),
    )(segments, query, key, value, got)


def place_bits(blocks):
    return blocks.bit_length() - 1


def xor_source(place, me, bits):
    distance = 0
    for bit in range(bits):
        distance = distance + (((place >> (bits - 1 - bit)) & 1) << bit)
    return distance ^ me


def norm_rows(values, gain, bias):
    average = jnp.mean(values, axis=-1, keepdims=True)
    centred = values - average
    inverse = lax.rsqrt(jnp.mean(centred * centred, axis=-1, keepdims=True) + EPSILON)
    return centred * inverse * gain + bias


def project_kernel(x, gain, bias, wq, bq, wk, wv, bv, normed, query, key, value):
    low = norm_rows(x[...].astype(F32), gain[...], bias[...]).astype(BF16)
    normed[...] = low
    query[...] = ((mm(low, wq[...]) + bq[...]) * SCALING).astype(BF16)
    key[...] = mm(low, wk[...]).astype(BF16)
    value[...] = (mm(low, wv[...]) + bv[...]).astype(BF16)


def whole_spec(array):
    return pl.BlockSpec(array.shape, lambda *_: (0,) * array.ndim)


def project(x, gain, bias, wq, bq, wk, wv, bv):
    rows, width = x.shape
    local = wq.shape[1]
    size = min(512, rows)
    args = [x] + [v.reshape(1, -1) if v.ndim == 1 else v for v in (gain, bias, wq, bq, wk, wv, bv)]
    tall = pl.BlockSpec((size, width), lambda i: (i, 0))
    thin = pl.BlockSpec((size, local), lambda i: (i, 0))
    shape = jax.ShapeDtypeStruct((rows, local), BF16)
    return pl.pallas_call(
        project_kernel,
        grid=(rows // size,),
        in_specs=[tall] + [whole_spec(a) for a in args[1:]],
        out_specs=[tall] + [thin] * 3,
        out_shape=[jax.ShapeDtypeStruct(x.shape, BF16)] + [shape] * 3,
        compiler_params=pltpu.CompilerParams(vmem_limit_bytes=VMEM),
        cost_estimate=cost(6 * rows * width * local),
    )(*args)


def middle_kernel(
    steps, here_ref, heads, wo, x, bo, gain, bias, wup, bup, d_hid, wup_rows,
    own_mid, low_out, hidden, d_up, *rest,
):
    first, second = steps
    *terms, mid, low, d_low = rest
    step = pl.program_id(0)
    block = wo.shape[1]
    here = here_ref[1]
    local = heads.shape[2]

    @pl.when(step == 0)
    def _():
        for t in range(heads.shape[0]):
            low[:, t * local : (t + 1) * local] = heads[t]

    @pl.when(step < first)
    def _():
        branch = mm(low[...], wo[...])
        values = x[...].reshape(branch.shape).astype(F32)
        columns = pl.ds(pl.multiple_of(step * block, block), block)
        mid[:, columns] = values + (branch + bo[...])

    @pl.when(step == first)
    def _():
        low[...] = norm_rows(mid[...], gain[...], bias[...]).astype(BF16)
        part = own_mid.shape[0]
        own_mid[...] = mid[pl.ds(pl.multiple_of(here * part, part), part), :]

    @pl.when((step >= first) & (step < first + second))
    def _():
        piece = 256
        for start in range(0, wup.shape[1], piece):
            columns = slice(start, start + piece)
            up_value = mm(low[...], wup[:, columns]) + bup[:, columns]
            below = 0.5 + 0.5 * lax.erf(up_value * (0.5**0.5))
            density = jnp.exp(-0.5 * up_value * up_value) * 0.3989422804014327
            hidden[:, columns] = (up_value * below).astype(BF16)
            slope = ((below + up_value * density) * d_hid[:, columns].astype(F32)).astype(BF16)
            d_up[:, columns] = slope
            place = pl.multiple_of((step - first) * wup.shape[1] + start, piece)
            d_low[:, pl.ds(place, piece)] = slope

    @pl.when(step >= first + second)
    def _():
        value = times_trans(d_low[...], wup_rows[...]).astype(BF16)

        for k, term in enumerate(terms):
            start = first + second + k * first // len(terms)

            @pl.when((step >= start) & (step < start + first // len(terms)))
            def _():
                term[...] = value

        columns = pl.ds(pl.multiple_of((step - first - second) * block, block), block)
        low_out[...] = low[:, columns]


def middle_call(split, c, here, heads, wo, x, bo, gain, bias, wup, bup, d_hid):
    groups, _, part, width = x.shape
    rows = groups * part
    hidden = wup.shape[1]
    block = 512
    first, second = width // block, hidden // block
    bo, gain, bias, bup = (v.reshape(1, -1) for v in (bo, gain, bias, bup))

    def at(index, low, count):
        return jnp.clip(index - low, 0, count - 1)

    def columns(tall, low, count):
        return pl.BlockSpec((tall, block), lambda i, h: (0, at(i, low, count)))

    third = first + second
    return pl.pallas_call(
        functools.partial(middle_kernel, (first, second)),
        grid_spec=pltpu.PrefetchScalarGridSpec(
            num_scalar_prefetch=1,
            grid=(first + second + first,),
            in_specs=[
                whole_spec(heads),
                columns(width, 0, first),
                pl.BlockSpec(
                    (groups, None, part, block), lambda i, h: (0, c, 0, at(i, 0, first))
                ),
                columns(1, 0, first),
                whole_spec(gain),
                whole_spec(bias),
                columns(width, first, second),
                columns(1, first, second),
                pl.BlockSpec((None, rows, block), lambda i, h: (c, 0, at(i, first, second))),
                pl.BlockSpec((block, hidden), lambda i, h: (at(i, third, first), 0)),
            ],
            out_specs=[
                pl.BlockSpec((part, width), lambda i, h: (0, 0)),
                columns(rows, third, first),
                columns(rows, first, second),
                columns(rows, first, second),
            ]
            + [columns(rows, third + k * first // split, first // split) for k in range(split)],
            scratch_shapes=[
                pltpu.VMEM((rows, width), F32),
                pltpu.VMEM((rows, width), BF16),
                pltpu.VMEM((rows, hidden), BF16),
            ],
        ),
        out_shape=[
            jax.ShapeDtypeStruct((part, width), F32),
            jax.ShapeDtypeStruct((rows, width), BF16),
            jax.ShapeDtypeStruct((rows, hidden), BF16),
            jax.ShapeDtypeStruct((rows, hidden), BF16),
        ]
        + [jax.ShapeDtypeStruct((rows, width // split), BF16)] * split,
        compiler_params=pltpu.CompilerParams(vmem_limit_bytes=VMEM),
        cost_estimate=cost(2 * rows * width * (width + 2 * hidden)),
    )(here, heads, wo, x, bo, gain, bias, wup, bup, d_hid, wup)


def middle_back_kernel(count, *refs):
    (terms, mid, cot, gain, wo), before = refs[:5], refs[5 : 5 + count]
    d_mid, d_branch, sums, d_att = refs[5 + count :]

    @pl.when(pl.program_id(0) == 0)
    def _():
        d_normed = terms[...].astype(F32)
        values = mid[...]
        centred = values - jnp.mean(values, axis=-1, keepdims=True)
        inverse = lax.rsqrt(jnp.mean(centred * centred, axis=-1, keepdims=True) + EPSILON)
        xhat = centred * inverse
        total = cot[...].astype(F32) + norm_back(d_normed, gain[...], xhat, inverse)
        low = total.astype(BF16)
        d_mid[...] = total
        d_branch[...] = low
        sums[0:1, :] = jnp.sum(d_normed * xhat, axis=0, keepdims=True)
        sums[1:2, :] = jnp.sum(d_normed, axis=0, keepdims=True)
        sums[2:3, :] = jnp.sum(low.astype(F32), axis=0, keepdims=True)

    for c in range(count):
        d_att[c] = before[c][...]
    d_att[count] = times_trans(d_branch[...], wo[...]).astype(BF16)


def middle_back(terms, mid, cot, gain, wo, before):
    part, width = mid.shape
    groups = lax.axis_size("tensor")
    block = width // groups
    count = len(before) + 1
    rows = pl.BlockSpec((part, width), lambda j: (0, 0))
    return pl.pallas_call(
        functools.partial(middle_back_kernel, len(before)),
        grid=(groups,),
        in_specs=[
            rows,
            rows,
            rows,
            pl.BlockSpec((1, width), lambda j: (0, 0)),
            pl.BlockSpec((block, width), lambda j: (j, 0)),
        ]
        + [pl.BlockSpec((None, None, part, block), lambda j: (j, 0, 0, 0))] * len(before),
        out_specs=[
            rows,
            rows,
            pl.BlockSpec((8, width), lambda j: (0, 0)),
            pl.BlockSpec((None, count, part, block), lambda j: (j, 0, 0, 0)),
        ],
        out_shape=[
            jax.ShapeDtypeStruct((part, width), F32),
            jax.ShapeDtypeStruct((part, width), BF16),
            jax.ShapeDtypeStruct((8, width), F32),
            jax.ShapeDtypeStruct((groups, count, part, block), BF16),
        ],
        compiler_params=pltpu.CompilerParams(vmem_limit_bytes=VMEM),
        cost_estimate=cost(2 * part * width * width),
    )(terms, mid, cot, gain.reshape(1, -1), wo, *before)


def gradient_terms(lefts, groups, me, blocks):
    half = blocks // 2
    bits = place_bits(blocks)
    part_of = [left[1] if isinstance(left, tuple) else None for left in lefts]
    lefts = [left[0] if isinstance(left, tuple) else left for left in lefts]
    count = len(lefts)
    rights = [right for group in groups for right in group]
    entry_of = [right[1] if isinstance(right, tuple) else None for right in rights]
    rights = [right[0] if isinstance(right, tuple) else right for right in rights]
    width = lefts[0].shape[-1] // blocks
    total = sum(right.shape[-1] for right in rights[::count])

    def source(j, m):
        return xor_source(jnp.where(j < half, j + half, j - half), m[0], bits)

    def right_spec(right, t):
        if t is None:
            return whole_spec(right)
        return pl.BlockSpec((None, None) + right.shape[2:], lambda j, m: (t, m[1], 0, 0))

    def left_spec(left, c):
        if c is None:
            return pl.BlockSpec((left.shape[0], width), lambda j, m: (0, source(j, m)))
        shape = (left.shape[0], None, left.shape[2], width)
        return pl.BlockSpec(shape, lambda j, m: (0, c, 0, source(j, m)))

    def kernel(me_ref, *refs):
        left_refs, right_refs = refs[:count], refs[count:]
        send, keep = refs[-2:]
        step = pl.program_id(0)

        def fill(target):
            place = 0
            turned = [ref[...].reshape(-1, width).T for ref in left_refs]
            for g in range(len(groups)):
                value = None
                for i in range(count):
                    more = mm(turned[i], right_refs[g * count + i][...])
                    value = more if value is None else value + more
                columns = value.shape[1]
                target[:, place : place + columns] = value.astype(BF16)
                place += columns

        @pl.when(step < half)
        def _():
            fill(send)

        @pl.when(step >= half)
        def _():
            fill(keep)

    shape = jax.ShapeDtypeStruct((half, width, total), BF16)
    return pl.pallas_call(
        kernel,
        grid_spec=pltpu.PrefetchScalarGridSpec(
            num_scalar_prefetch=1,
            grid=(blocks,),
            in_specs=[left_spec(left, c) for left, c in zip(lefts, part_of)]
            + [right_spec(right, t) for right, t in zip(rights, entry_of)],
            out_specs=[
                pl.BlockSpec((None, width, total), lambda j, m: (jnp.minimum(j, half - 1), 0, 0)),
                pl.BlockSpec((None, width, total), lambda j, m: (jnp.maximum(j - half, 0), 0, 0)),
            ],
        ),
        out_shape=[shape, shape],
        compiler_params=pltpu.CompilerParams(vmem_limit_bytes=VMEM),
        cost_estimate=cost(2**20),
    )(me, *lefts, *rights)


def normed_back_kernel(dq, dk, dv, wq, wk, wv, x, terms, gain_sum, bias_sum):
    total = times_trans(dq[...], wq[...]) + times_trans(dk[...], wk[...])
    total = total + times_trans(dv[...], wv[...])
    terms[...] = total.astype(BF16)
    values = x[...].astype(F32)
    centred = values - jnp.mean(values, axis=-1, keepdims=True)
    inverse = lax.rsqrt(jnp.mean(centred * centred, axis=-1, keepdims=True) + EPSILON)

    @pl.when(pl.program_id(0) == 0)
    def _():
        gain_sum[...] = jnp.zeros_like(gain_sum)
        bias_sum[...] = jnp.zeros_like(bias_sum)

    gain_sum[...] += jnp.sum(total * (centred * inverse), axis=0, keepdims=True)
    bias_sum[...] += jnp.sum(total, axis=0, keepdims=True)


def normed_back(dq, dk, dv, wq, wk, wv, x):
    rows, width = x.shape
    size = min(512, rows)
    thin = pl.BlockSpec((size, dq.shape[1]), lambda i: (i, 0))
    tall = pl.BlockSpec((size, width), lambda i: (i, 0))
    line = pl.BlockSpec((1, width), lambda i: (0, 0))
    return pl.pallas_call(
        normed_back_kernel,
        grid=(rows // size,),
        in_specs=[thin] * 3 + [whole_spec(w) for w in (wq, wk, wv)] + [tall],
        out_specs=[tall, line, line],
        out_shape=[
            jax.ShapeDtypeStruct((rows, width), BF16),
            jax.ShapeDtypeStruct((1, width), F32),
            jax.ShapeDtypeStruct((1, width), F32),
        ],
        compiler_params=pltpu.CompilerParams(vmem_limit_bytes=VMEM),
        cost_estimate=cost(6 * rows * width * dq.shape[1]),
    )(dq, dk, dv, wq, wk, wv, x)


def input_back(d_normed, x, d_mid, gain):
    rows, width = x.shape
    size = min(128, rows)

    def kernel(terms, x_ref, mid, gain_ref, out):
        values = x_ref[...].astype(F32)
        centred = values - jnp.mean(values, axis=-1, keepdims=True)
        inverse = lax.rsqrt(jnp.mean(centred * centred, axis=-1, keepdims=True) + EPSILON)
        back = norm_back(terms[...].astype(F32), gain_ref[...], centred * inverse, inverse)
        out[...] = mid[...] + back

    tall = pl.BlockSpec((size, width), lambda i: (i, 0))
    return pl.pallas_call(
        kernel,
        grid=(rows // size,),
        in_specs=[tall, tall, tall, pl.BlockSpec((1, width), lambda i: (0, 0))],
        out_specs=tall,
        out_shape=jax.ShapeDtypeStruct((rows, width), F32),
        compiler_params=pltpu.CompilerParams(vmem_limit_bytes=VMEM),
        cost_estimate=cost(2**20),
    )(d_normed, x, d_mid, gain.reshape(1, -1))


def both_parts(lefts, weight, transposed, columns, groups=None):
    block = min(512, columns)
    part_of = [left[1] if isinstance(left, tuple) else None for left in lefts]
    lefts = [left[0] if isinstance(left, tuple) else left for left in lefts]
    depth = lefts[0].shape[-1]
    rows = lefts[0].shape[0] * (1 if part_of[0] is None else lefts[0].shape[2])

    def kernel(*refs):
        weight_ref, out = refs[-2:]
        for c in range(len(lefts)):
            left = refs[c][...].reshape(-1, depth)
            product = times_trans if transposed else mm
            value = product(left, weight_ref[...]).astype(BF16)
            if groups is None:
                out[c] = value
            else:
                out[:, c] = value.reshape(groups, rows // groups, block)

    def left_spec(left, c):
        if c is None:
            return whole_spec(left)
        return pl.BlockSpec((left.shape[0], None) + left.shape[2:], lambda j: (0, c, 0, 0))

    shape = (len(lefts), rows)
    if groups is not None:
        shape = (groups, len(lefts), rows // groups)
    if transposed:
        weight_spec = pl.BlockSpec((block, depth), lambda j: (j, 0))
    else:
        weight_spec = pl.BlockSpec((depth, block), lambda j: (0, j))
    return pl.pallas_call(
        kernel,
        grid=(columns // block,),
        in_specs=[left_spec(left, c) for left, c in zip(lefts, part_of)] + [weight_spec],
        out_specs=pl.BlockSpec(shape + (block,), lambda j: (0,) * len(shape) + (j,)),
        out_shape=jax.ShapeDtypeStruct(shape + (columns,), BF16),
        compiler_params=pltpu.CompilerParams(vmem_limit_bytes=VMEM),
        cost_estimate=cost(2 * len(lefts) * rows * depth * columns),
    )(*lefts, weight)


def swap_bit(values, axis, bit):
    size = lax.axis_size(axis)
    return lax.ppermute(values, axis, [(i, i ^ (1 << bit)) for i in range(size)])


def third(k, steps):
    return range((k - 1) * steps // 3 + 1, k * steps // 3 + 1)


def fence(things, arrays=()):
    lists = [thing.live for thing in things]
    flat = lax.optimization_barrier(tuple(v for values in lists for v in values) + tuple(arrays))
    place = 0
    for thing, values in zip(things, lists):
        thing.live = list(flat[place : place + len(values)])
        place += len(values)
    return flat[place:]


def exchange(values):
    return lax.all_to_all(values, "tensor", 0, 0)


def add_and_split(sources, outs, dims):
    places = 2**dims
    rows = sources[0][0].shape[1]
    size = min(64, rows)
    widths = [sum(stop - start for _, start, stop in picks) for picks, _ in outs]

    def kernel(*refs):
        target = 2 * len(sources)
        for picks, dim in outs:
            shift = dims - 1 - dim
            for half in range(2):
                chosen = [p for p in range(places) if (p >> shift) & 1 == half]
                at = 0
                for source, start, stop in picks:
                    keep, got = refs[2 * source : 2 * source + 2]
                    for q, p in enumerate(chosen):
                        value = keep[p, :, start:stop].astype(F32) + got[p, :, start:stop].astype(F32)
                        refs[target][q, :, at : at + stop - start] = value.astype(BF16)
                    at += stop - start
                target += 1

    def block(count, columns):
        return pl.BlockSpec((count, size, columns), lambda i: (0, i, 0))

    flat = [v for pair in sources for v in pair]
    return pl.pallas_call(
        kernel,
        grid=(rows // size,),
        in_specs=[block(places, v.shape[2]) for v in flat],
        out_specs=[block(places // 2, w) for w in widths for _ in range(2)],
        out_shape=[
            jax.ShapeDtypeStruct((places // 2, rows, w), BF16) for w in widths for _ in range(2)
        ],
        compiler_params=pltpu.CompilerParams(vmem_limit_bytes=VMEM),
        cost_estimate=cost(2**20),
    )(*flat)


def finish_sum(live, width, cuts, turned, kind):
    rows, columns = live[0].shape[1:]
    count = columns // width
    total = 2 * columns

    def kernel(*refs):
        sums = []
        for c in range(2 * count):
            keep, got = refs[2 * (c % 2) : 2 * (c % 2) + 2]
            place = slice(c // 2 * width, (c // 2 + 1) * width)
            sums.append(keep[0, :, place].astype(F32) + got[0, :, place].astype(F32))
        value = jnp.concatenate(sums, axis=1)
        if turned:
            refs[4][...] = value.T.astype(kind)
            return
        for k in range(cuts):
            refs[4 + k][...] = value[:, k * total // cuts : (k + 1) * total // cuts].astype(kind)

    size = rows if turned else min(64, rows)
    shape = (total, rows) if turned else (rows, total // cuts)
    block = (total, rows) if turned else (size, total // cuts)
    return pl.pallas_call(
        kernel,
        grid=(rows // size,),
        in_specs=[pl.BlockSpec((1, size, columns), lambda i: (0, i, 0))] * 4,
        out_specs=[pl.BlockSpec(block, lambda i: (i, 0) if not turned else (0, 0))] * cuts,
        out_shape=[jax.ShapeDtypeStruct(shape, kind)] * cuts,
        compiler_params=pltpu.CompilerParams(vmem_limit_bytes=VMEM),
        cost_estimate=cost(2**20),
    )(*live)


class DpSum:
    def __init__(self, send, keep, cuts):
        self.live = [send, keep]
        self.cuts = cuts
        self.rest = place_bits(lax.axis_size("dp")) - 1
        self.width = keep.shape[-1] // cuts
        self.left = [list(range(1, self.rest + 1)) for _ in range(2)]

    def core(self):
        self.live = [self.live[1], swap_bit(self.live[0], "dp", 0)]

    def dim(self, odd):
        return len(self.left[odd]) - 1 if odd else 0

    def split(self):
        outs = [
            ([(0, c * self.width, (c + 1) * self.width)], self.dim(c % 2)) for c in range(self.cuts)
        ]
        self.live = list(add_and_split([tuple(self.live)], outs, self.rest))

    def first(self, *cuts):
        for c in cuts:
            values = self.live[2 * c + 1]
            self.live[2 * c + 1] = swap_bit(values, "dp", self.left[c % 2][self.dim(c % 2)])

    def add(self):
        bits = [left[self.dim(odd)] for odd, left in enumerate(self.left)]
        for odd in range(2):
            self.left[odd].remove(bits[odd])
        count = len(self.live) // 2
        sources = [(self.live[2 * k], self.live[2 * k + 1]) for k in range(count)]
        outs = [
            ([(k, 0, sources[k][0].shape[2]) for k in range(odd, count, 2)], self.dim(odd))
            for odd in range(2)
        ]
        self.live = list(add_and_split(sources, outs, len(self.left[0])))

    def send(self):
        for odd in range(2):
            bit = self.left[odd][self.dim(odd)]
            self.live[2 * odd + 1] = swap_bit(self.live[2 * odd + 1], "dp", bit)
        while len(self.left[0]) > 1:
            self.add()
            self.send()

    def total(self, cuts=1, turned=False, kind=F32):
        return finish_sum(self.live, self.width, cuts, turned, kind)


class WeightGather:
    def __init__(self, own, me):
        self.blocks = lax.axis_size("dp")
        self.size = lax.axis_size("tensor")
        self.usual = (self.size, self.blocks) == (4, 8)
        self.me = me
        share = own.shape[1 if self.usual else 0] // self.blocks
        axis = 1 if self.usual else 0
        self.live = [lax.dynamic_slice_in_dim(own, me[0] * share, share, axis)]

    def advance(self, k):
        if not self.usual:
            if k == 0:
                self.live = [lax.all_gather(self.live[0], ("tensor", "dp"), axis=0, tiled=True)]
            return
        if k == 0:
            own = self.live[0]
            self.live += [
                lax.ppermute(own, "tensor", [(i, (i + m) % self.size) for i in range(self.size)])
                for m in range(1, self.size)
            ]
        elif k == 1:
            own, one, two, three = self.live
            even = lax.axis_index("tensor") % 2 == 0
            near = jnp.concatenate([jnp.where(even, own, one), jnp.where(even, three, own)])
            far = jnp.concatenate([jnp.where(even, two, three), jnp.where(even, one, two)])
            self.live = [near, swap_bit(near, "dp", 1), far, swap_bit(far, "dp", 2)]
            self.live += [swap_bit(near, "dp", 0), swap_bit(far, "dp", 0)]
        elif k == 2:
            near, near_one, far, far_one, near_core, far_core = self.live
            near, far = jnp.stack([near, near_one]), jnp.stack([far, far_one])
            self.live = [near, far, near_core[None], far_core[None]]
            self.live += [swap_bit(near, "dp", 2), swap_bit(far, "dp", 1)]
            self.live += [swap_bit(near_one, "dp", 0)[None], swap_bit(far_one, "dp", 0)[None]]
        elif k == 3:
            near, far, near_core, far_core, near_two, far_two, near_one_core, far_one_core = self.live
            own = [(near, 0), (near, 1), (far, 0), (far, 1)]
            other = [(v, 0) for v in (near_core, near_one_core, far_core, far_one_core)]
            self.live = [near_two, far_two, self.place(own, other, 0, None)]
        else:
            near_two, far_two, half = self.live
            self.live = [near_two, swap_bit(near_two, "dp", 0)]
            self.live += [far_two, swap_bit(far_two, "dp", 0), half]

    def place(self, own, other, late, half):
        rows, width = own[0][0].shape[1:]
        blocks = own + other

        def kernel(me_ref, *refs):
            out = refs[-1]
            step, odd = pl.program_id(0), me_ref[0] & 1
            for k in range(4):
                for flip in range(2):

                    @pl.when((step == k) & (odd == flip))
                    def _():
                        out[:, flip * width : (flip + 1) * width] = refs[k][...]
                        out[:, (1 - flip) * width : (2 - flip) * width] = refs[k + 4][...]

        def source(entry):
            return pl.BlockSpec((None, rows, width), lambda s, m: (entry, 0, 0))

        def target(s, m):
            top, one = s < 2, s & 1
            low = jnp.where(top, 2 * one + 4 * late, 4 * one + 2 * late)
            return (jnp.where(top, m[2], 1 - m[2]), (low ^ m[0]) >> 1)

        more = [] if half is None else [half]
        return pl.pallas_call(
            kernel,
            grid_spec=pltpu.PrefetchScalarGridSpec(
                num_scalar_prefetch=1,
                grid=(4,),
                in_specs=[source(entry) for _, entry in blocks]
                + [pl.BlockSpec(memory_space=pl.ANY)] * len(more),
                out_specs=pl.BlockSpec((rows, 2 * width), target),
            ),
            out_shape=jax.ShapeDtypeStruct((2 * rows, 8 * width), BF16),
            input_output_aliases={9: 0} if more else {},
            compiler_params=pltpu.CompilerParams(vmem_limit_bytes=VMEM),
            cost_estimate=cost(2**20),
        )(self.me, *[array for array, _ in blocks], *more)

    def whole(self):
        if not self.usual:
            return self.live[0]
        near, near_core, far, far_core, half = self.live
        own = [(near, 0), (near, 1), (far, 0), (far, 1)]
        other = [(near_core, 0), (near_core, 1), (far_core, 0), (far_core, 1)]
        return self.place(own, other, 1, half)


class SmallSum:
    def __init__(self, vectors, me):
        self.vectors = vectors
        self.blocks = blocks = lax.axis_size("dp")
        self.bits = place_bits(blocks)
        places = jnp.stack([xor_source(p, me, self.bits) for p in range(blocks)]).reshape(-1)
        self.ordered = sorted(range(len(vectors)), key=lambda i: not vectors[i][1])
        wide = [vectors[i][0].reshape(blocks, -1) for i in self.ordered]
        wide = jnp.take(jnp.concatenate(wide, axis=1), places, axis=0)
        self.live = [wide.reshape((2,) * self.bits + wide.shape[1:])]

    def move(self):
        self.steps = getattr(self, "steps", 0) + 1
        while self.live[0].ndim > 1:
            values = self.live[0]
            self.live = [values[0] + swap_bit(values[1], "dp", self.bits - values.ndim + 1)]
            if self.steps < 3:
                return

    def tensor(self):
        values = self.live[0]
        both = sum(v[0].shape[0] // self.blocks for v in self.vectors if v[1])
        summed, alone = values[..., :both], values[..., both:]
        for bit in range(place_bits(lax.axis_size("tensor"))):
            summed = summed + swap_bit(summed, "tensor", bit)
        self.live = [jnp.concatenate([summed, alone], axis=-1)]

    def total(self):
        out, start = [None] * len(self.vectors), 0
        for i in self.ordered:
            size = self.vectors[i][0].shape[0] // self.blocks
            out[i] = self.live[0][start : start + size]
            start += size
        return out


def on_device(
    inputs,
    segments,
    cotangent,
    norm1_gain,
    norm1_bias,
    query_weight,
    query_bias,
    key_weight,
    value_weight,
    value_bias,
    output_weight,
    output_bias,
    norm2_gain,
    norm2_bias,
    up_weight,
    up_bias,
    down_weight,
    down_bias,
):
    groups = lax.axis_size("tensor")
    blocks = lax.axis_size("dp")
    here = lax.axis_index("tensor").astype(jnp.int32)
    side = here // (groups // 2)
    me = lax.axis_index("dp").astype(jnp.int32)
    me = jnp.stack([me, here, side])
    rows, width = inputs.shape
    share = rows // groups
    part = share // PARTS
    local = query_weight.shape[1]
    size = width // blocks

    def by_part(values):
        return values.reshape(groups, PARTS, part, values.shape[1])

    def own(values):
        return lax.dynamic_slice_in_dim(values, here * share, share, 0)

    weight = WeightGather(output_weight, me)
    weight.advance(0)
    normed, query, key, value = project(
        inputs,
        norm1_gain,
        norm1_bias,
        query_weight,
        query_bias,
        key_weight,
        value_weight,
        value_bias,
    )
    heads = [None] * PARTS
    heads[0] = attend(0, segments, query, key, value, groups)
    cot, heads[0], query, key, value = fence([weight], (cotangent, heads[0], query, key, value))

    heads[0] = lax.all_gather(heads[0].reshape(groups * part, local), "tensor", axis=0)
    weight.advance(1)
    heads[1] = attend(1, segments, query, key, value, groups)
    cot, heads[1] = fence([weight], (cot, heads[1]))
    heads[1] = lax.all_gather(heads[1].reshape(groups * part, local), "tensor", axis=0)
    weight.advance(2)
    cot_parts = by_part(cot)
    cots = [(cot_parts, c) for c in range(PARTS)]
    d_hidden = both_parts(cots, down_weight, True, down_weight.shape[0])
    d_hidden, cot = fence([], (d_hidden, cot))
    weight.advance(3)
    d_hidden, cot = fence([weight], (d_hidden, cot))
    weight.advance(4)
    fence([weight])
    whole = weight.whole()
    whole, heads[0] = fence([], (whole, heads[0]))

    own_mid, low, hidden, d_up, terms = ([None] * PARTS for _ in range(5))

    def middle(c):
        own_mid[c], low[c], hidden[c], d_up[c], *term = middle_call(
            1,
            c,
            me,
            heads[c],
            whole,
            by_part(inputs),
            output_bias,
            norm2_gain,
            norm2_bias,
            up_weight,
            up_bias,
            d_hidden,
        )
        terms[c] = term[0].reshape(groups, part, width)

    middle(0)
    terms[0], heads[1] = fence([], (terms[0], heads[1]))

    terms[0] = lax.psum_scatter(terms[0], "tensor", scatter_dimension=0)
    middle(1)
    cot_own = own(cot)
    terms[1], cot_own, low[0], low[1], d_up[0], d_up[1] = fence(
        [], (terms[1], cot_own, *low, *d_up)
    )

    terms[1] = lax.psum_scatter(terms[1], "tensor", scatter_dimension=0)
    up_terms = gradient_terms(low, [d_up], me, blocks)
    d_mids, d_branches, sums = ([None] * PARTS for _ in range(3))

    def back(c, before):
        d_mids[c], d_branches[c], sums[c], d_att = middle_back(
            terms[c], own_mid[c], cot_own[c * part : (c + 1) * part], norm2_gain, whole, before
        )
        return d_att

    terms[0], hidden[0], hidden[1], *up_terms = fence([], (terms[0], *hidden, *up_terms))
    d_att = back(0, [])
    d_att, hidden[0], hidden[1] = fence([], (d_att, *hidden))
    out_terms = both_parts(hidden, down_weight, False, width, groups)
    out_terms, hidden[0], hidden[1] = fence([], (out_terms, *hidden))
    down_terms = gradient_terms(cots, [hidden], me, blocks)
    cot_sum = column_sums(cot)
    up_bias_sum = column_sums(d_up[0]) + column_sums(d_up[1])
    up_sum = DpSum(*up_terms, 2)
    down_sum = DpSum(*down_terms, 2)
    terms[1], out_terms, d_branches[0], cot_sum, up_bias_sum, d_att = fence(
        [up_sum, down_sum], (terms[1], out_terms, d_branches[0], cot_sum, up_bias_sum, d_att)
    )

    d_att = back(1, [d_att])
    d_att, *d_branches = fence([up_sum, down_sum], (d_att, *d_branches))
    d_att = exchange(d_att)
    up_sum.core()
    down_sum.core()
    views = [h.reshape(groups, groups, part, local) for h in heads]
    wo_terms = gradient_terms(d_branches, [[(v, t) for v in views] for t in range(groups)], me, blocks)
    wo_sum = DpSum(*wo_terms, 2)
    up_sum.split()
    d_att, out_terms = fence([wo_sum, up_sum, down_sum], (d_att, out_terms))

    out_sum = lax.psum_scatter(out_terms, "tensor", scatter_dimension=0)
    up_sum.first(0, 1)
    wo_sum.core()
    d_query, d_key, d_value = attend_back(segments, query, key, value, d_att)
    wo_sum.split()
    d_query, d_key, d_value = fence([up_sum, wo_sum, down_sum], (d_query, d_key, d_value))
    wo_sum.first(0, 1)
    qkv_sum = DpSum(
        *gradient_terms([normed], [[d] for d in (d_query, d_key, d_value)], me, blocks), 2
    )
    down_sum.split()
    d_query, d_key, d_value = fence([wo_sum, qkv_sum, down_sum], (d_query, d_key, d_value))
    qkv_sum.core()
    down_sum.first(0, 1)
    terms_in, gain1, bias1 = normed_back(
        d_query, d_key, d_value, query_weight, key_weight, value_weight, inputs
    )
    qkv_sum.split()
    wo_sum.add()
    gain1, bias1, terms_in, d_query, d_value = fence(
        [qkv_sum, wo_sum, down_sum], (gain1, bias1, terms_in, d_query, d_value)
    )

    d_normed = lax.psum_scatter(
        terms_in.reshape(groups, share, width), "tensor", scatter_dimension=0
    )
    qkv_sum.first(0, 1)
    wo_sum.send()
    two = sums[0] + sums[1]
    small = SmallSum(
        [
            (gain1[0], True),
            (bias1[0], True),
            (two[0], True),
            (two[1], True),
            (two[2], True),
            (cot_sum, False),
            (column_sums(d_query), False),
            (column_sums(d_value), False),
            (up_bias_sum, False),
        ],
        me[:1],
    )
    small.tensor()
    down_sum.add()
    out_sum, *_ = fence([qkv_sum, wo_sum, down_sum, small, up_sum], (out_sum,))
    down_sum.send()
    qkv_sum.add()
    qkv_sum.send()
    small.move()
    small.move()
    small.move()
    wo_terms = wo_sum.total(turned=True, kind=BF16)[0].reshape(groups, local, size)
    to_all = [
        lax.dynamic_index_in_dim(wo_terms, (here - m) % groups, 0, keepdims=False)
        for m in range(groups)
    ]
    up_sum.add()
    out_sum, *to_all = fence([qkv_sum, small, down_sum, up_sum], (out_sum, *to_all))
    wo_got = [to_all[0]]
    for m in range(1, groups):
        ring = [(i, (i - m) % groups) for i in range(groups)]
        wo_got.append(lax.ppermute(to_all[m], "tensor", ring))
    up_sum.send()
    total = [own_mid[c] + (out_sum[c].astype(F32) + down_bias) for c in range(PARTS)]
    output = jnp.concatenate([t.astype(BF16) for t in total], axis=0)
    qkv_grads = qkv_sum.total(3)
    (up_weight_grad,) = up_sum.total()
    (down_weight_grad,) = down_sum.total(turned=True)
    d_mid = jnp.concatenate(d_mids, axis=0)
    rows_own = own(inputs)
    small_sums = small.total()
    up_weight_grad, down_weight_grad, output, d_mid, rows_own, *others = fence(
        [],
        (up_weight_grad, down_weight_grad, output, d_mid, rows_own, *qkv_grads, *small_sums),
    )
    qkv_grads, small_sums = others[:3], others[3:]
    input_grad = input_back(d_normed, rows_own, d_mid, norm1_gain)
    input_grad, *wo_got = fence([], (input_grad, *wo_got))
    output_weight_grad = sum(g.astype(F32) for g in wo_got)
    (
        norm1_gain_grad,
        norm1_bias_grad,
        norm2_gain_grad,
        norm2_bias_grad,
        output_bias_grad,
        down_bias_grad,
        query_bias_grad,
        value_bias_grad,
        up_bias_grad,
    ) = small_sums
    return (
        output,
        input_grad,
        norm1_gain_grad,
        norm1_bias_grad,
        qkv_grads[0],
        query_bias_grad,
        qkv_grads[1],
        qkv_grads[2],
        value_bias_grad,
        output_weight_grad,
        output_bias_grad,
        norm2_gain_grad,
        norm2_bias_grad,
        up_weight_grad,
        up_bias_grad,
        down_weight_grad,
        down_bias_grad,
    )


def solution(mesh):
    return jax.shard_map(
        on_device,
        mesh=mesh,
        in_specs=(
            P("dp", None),
            P("dp", None),
            P("dp", None),
            P(),
            P(),
            P(None, "tensor"),
            P("tensor"),
            P(None, "tensor"),
            P(None, "tensor"),
            P("tensor"),
            P("tensor", None),
            P(),
            P(),
            P(),
            P(None, "tensor"),
            P("tensor"),
            P("tensor", None),
            P(),
        ),
        out_specs=(
            P(("dp", "tensor"), None),
            P(("dp", "tensor"), None),
            P("dp"),
            P("dp"),
            P("dp", "tensor"),
            P(("tensor", "dp")),
            P("dp", "tensor"),
            P("dp", "tensor"),
            P(("tensor", "dp")),
            P("tensor", "dp"),
            P("dp"),
            P("dp"),
            P("dp"),
            P("dp", "tensor"),
            P(("tensor", "dp")),
            P("tensor", "dp"),
            P("dp"),
        ),
        check_vma=False,
    )
```

```python
import functools

import jax
import jax.numpy as jnp
from jax import lax
from jax.experimental import pallas as pl
from jax.experimental.pallas import tpu as pltpu
from jax.sharding import PartitionSpec as P

HEAD_DIM = 128
LONGEST = 512
EPSILON = 1e-05
MASKED_SCORE = -1e30
SCALING = HEAD_DIM ** (-0.5)
F32 = jnp.float32
BF16 = jnp.bfloat16
PARTS = 2
COST = 0
VMEM = 60 * 2**20


def mm(left_side, right_side):
    return lax.dot_general(
        left_side, right_side, (((1,), (0,)), ((), ())), preferred_element_type=F32
    )


def times_trans(left_side, right_side):
    return lax.dot_general(
        left_side, right_side, (((1,), (1,)), ((), ())), preferred_element_type=F32
    )


def trans_times(left_side, right_side):
    return lax.dot_general(
        left_side, right_side, (((0,), (0,)), ((), ())), preferred_element_type=F32
    )


def column_sums(values):
    return jnp.sum(values.astype(F32), axis=0)


def row_stats(rows):
    average = jnp.mean(rows, axis=-1, keepdims=True)
    centred = rows - average
    spread = jnp.mean(centred * centred, axis=-1, keepdims=True)
    return average, lax.rsqrt(spread + EPSILON)


def norm_back(d_normed, gain, xhat, inverse):
    scaled = d_normed * gain
    first = jnp.mean(scaled, axis=-1, keepdims=True)
    second = jnp.mean(scaled * xhat, axis=-1, keepdims=True)
    return inverse * (scaled - first - xhat * second)


def cost(flops):
    return pl.CostEstimate(flops=COST and flops, bytes_accessed=2**10, transcendentals=0)


def key_start(first):
    return max(0, (first - (LONGEST - 1)) // 256 * 256)


def segment_column(seg_row):
    length = seg_row.shape[1]
    return jnp.broadcast_to(seg_row[...], (128, length)).T[:, :1]


def probabilities(seg_row, seg_col, query, keys, first, last):
    low, high = key_start(first), last
    scores = times_trans(keys[low:high, :], query)
    shape = (high - low, last - first)
    key_place = lax.broadcasted_iota(jnp.int32, shape, 0) + low
    query_place = lax.broadcasted_iota(jnp.int32, shape, 1) + first
    same = seg_col[low:high, :] == seg_row[:, first:last]
    scores = jnp.where(same & (key_place <= query_place), scores, MASKED_SCORE)
    weights = jnp.exp(scores - jnp.max(scores, axis=0, keepdims=True))
    return weights * (1.0 / jnp.sum(weights, axis=0, keepdims=True))


def forward_kernel(c, seg_row, query, key, value, out):
    groups, part = out.shape[:2]
    seg_col = segment_column(seg_row)
    for t in range(groups):
        first = (t * PARTS + c) * part
        last = first + part
        low = key_start(first)
        probs = probabilities(seg_row, seg_col, query[first:last, :], key, first, last)
        out[t] = trans_times(probs.astype(BF16), value[low:last, :]).astype(BF16)


def backward_kernel(size, seg_row, query, key, value, *refs):
    got = refs[:PARTS]
    d_query, d_key, d_value, d_attended, key_sum, value_sum = refs[PARTS:]
    groups, part = got[0].shape[:2]
    for t in range(groups):
        for c in range(PARTS):
            start = (t * PARTS + c) * part
            d_attended[start : start + part, :] = got[c][t]
    seg_col = segment_column(seg_row)
    key_sum[...] = jnp.zeros_like(key_sum)
    value_sum[...] = jnp.zeros_like(value_sum)
    for block in range(query.shape[0] // size):
        low, high = key_start(block * size), (block + 1) * size
        rows = slice(block * size, high)
        probs = probabilities(seg_row, seg_col, query[rows, :], key, block * size, high)
        value_sum[low:high, :] += mm(probs.astype(BF16), d_attended[rows, :])
        d_probs = times_trans(value[low:high, :], d_attended[rows, :])
        inner = jnp.sum(probs * d_probs, axis=0, keepdims=True)
        d_scores = (probs * (d_probs - inner)).astype(BF16)
        d_query[rows, :] = (trans_times(d_scores, key[low:high, :]) * SCALING).astype(BF16)
        key_sum[low:high, :] += mm(d_scores, query[rows, :])
    d_key[...] = key_sum[...].astype(BF16)
    d_value[...] = value_sum[...].astype(BF16)


def attend(c, segments, query, key, value, groups):
    length, local = query.shape
    part = length // groups // PARTS
    tall = pl.BlockSpec((length, HEAD_DIM), lambda h: (0, h))
    return pl.pallas_call(
        functools.partial(forward_kernel, c),
        grid=(local // HEAD_DIM,),
        in_specs=[pl.BlockSpec((1, length), lambda h: (0, 0))] + [tall] * 3,
        out_specs=pl.BlockSpec((groups, part, HEAD_DIM), lambda h: (0, 0, h)),
        out_shape=jax.ShapeDtypeStruct((groups, part, local), BF16),
        compiler_params=pltpu.CompilerParams(vmem_limit_bytes=VMEM),
        cost_estimate=cost(2**20),
    )(segments, query, key, value)


def attend_back(segments, query, key, value, got):
    length = query.shape[0]
    tall = pl.BlockSpec((length, HEAD_DIM), lambda h: (0, h))
    return pl.pallas_call(
        functools.partial(backward_kernel, min(256, length)),
        grid=(query.shape[1] // HEAD_DIM,),
        in_specs=[pl.BlockSpec((1, length), lambda h: (0, 0))]
        + [tall] * 3
        + [pl.BlockSpec(g.shape[:2] + (HEAD_DIM,), lambda h: (0, 0, h)) for g in got],
        out_specs=[tall] * 3,
        scratch_shapes=[
            pltpu.VMEM((length, HEAD_DIM), BF16),
            pltpu.VMEM((length, HEAD_DIM), F32),
            pltpu.VMEM((length, HEAD_DIM), F32),
        ],
        out_shape=[jax.ShapeDtypeStruct(query.shape, BF16)] * 3,
        compiler_params=pltpu.CompilerParams(vmem_limit_bytes=VMEM),
        cost_estimate=cost(10 * query.shape[0] * length * query.shape[1]),
    )(segments, query, key, value, *got)


def place_bits(blocks):
    return blocks.bit_length() - 1


def xor_source(place, me, bits):
    distance = 0
    for bit in range(bits):
        distance = distance + (((place >> (bits - 1 - bit)) & 1) << bit)
    return distance ^ me


def norm_rows(values, gain, bias):
    average = jnp.mean(values, axis=-1, keepdims=True)
    centred = values - average
    inverse = lax.rsqrt(jnp.mean(centred * centred, axis=-1, keepdims=True) + EPSILON)
    return centred * inverse * gain + bias


def project_kernel(x, gain, bias, wq, bq, wk, wv, bv, normed, query, key, value):
    low = norm_rows(x[...].astype(F32), gain[...], bias[...]).astype(BF16)
    normed[...] = low
    query[...] = ((mm(low, wq[...]) + bq[...]) * SCALING).astype(BF16)
    key[...] = mm(low, wk[...]).astype(BF16)
    value[...] = (mm(low, wv[...]) + bv[...]).astype(BF16)


def whole_spec(array):
    return pl.BlockSpec(array.shape, lambda *_: (0,) * array.ndim)


def project(x, gain, bias, wq, bq, wk, wv, bv):
    rows, width = x.shape
    local = wq.shape[1]
    size = min(512, rows)
    args = [x] + [v.reshape(1, -1) if v.ndim == 1 else v for v in (gain, bias, wq, bq, wk, wv, bv)]
    tall = pl.BlockSpec((size, width), lambda i: (i, 0))
    thin = pl.BlockSpec((size, local), lambda i: (i, 0))
    shape = jax.ShapeDtypeStruct((rows, local), BF16)
    return pl.pallas_call(
        project_kernel,
        grid=(rows // size,),
        in_specs=[tall] + [whole_spec(a) for a in args[1:]],
        out_specs=[tall] + [thin] * 3,
        out_shape=[jax.ShapeDtypeStruct(x.shape, BF16)] + [shape] * 3,
        compiler_params=pltpu.CompilerParams(vmem_limit_bytes=VMEM),
        cost_estimate=cost(6 * rows * width * local),
    )(*args)


def middle_kernel(
    steps, here_ref, heads, wo, x, bo, gain, bias, wup, bup, d_hid, wup_rows,
    own_mid, low_out, hidden, d_up, *rest,
):
    first, second = steps
    *terms, mid, low, d_low = rest
    step = pl.program_id(0)
    block = wo.shape[1]
    here = here_ref[1]
    local = heads.shape[2]

    @pl.when(step == 0)
    def _():
        for t in range(heads.shape[0]):
            low[:, t * local : (t + 1) * local] = heads[t]

    @pl.when(step < first)
    def _():
        branch = mm(low[...], wo[...])
        values = x[...].reshape(branch.shape).astype(F32)
        columns = pl.ds(pl.multiple_of(step * block, block), block)
        mid[:, columns] = values + (branch + bo[...])

    @pl.when(step == first)
    def _():
        low[...] = norm_rows(mid[...], gain[...], bias[...]).astype(BF16)
        part = own_mid.shape[0]
        own_mid[...] = mid[pl.ds(pl.multiple_of(here * part, part), part), :]

    @pl.when((step >= first) & (step < first + second))
    def _():
        piece = 256
        for start in range(0, wup.shape[1], piece):
            columns = slice(start, start + piece)
            up_value = mm(low[...], wup[:, columns]) + bup[:, columns]
            below = 0.5 + 0.5 * lax.erf(up_value * (0.5**0.5))
            density = jnp.exp(-0.5 * up_value * up_value) * 0.3989422804014327
            hidden[:, columns] = (up_value * below).astype(BF16)
            slope = ((below + up_value * density) * d_hid[:, columns].astype(F32)).astype(BF16)
            d_up[:, columns] = slope
            place = pl.multiple_of((step - first) * wup.shape[1] + start, piece)
            d_low[:, pl.ds(place, piece)] = slope

    @pl.when(step >= first + second)
    def _():
        value = times_trans(d_low[...], wup_rows[...]).astype(BF16)

        for k, term in enumerate(terms):
            start = first + second + k * first // len(terms)

            @pl.when((step >= start) & (step < start + first // len(terms)))
            def _():
                term[...] = value

        columns = pl.ds(pl.multiple_of((step - first - second) * block, block), block)
        low_out[...] = low[:, columns]


def middle_call(split, c, here, heads, wo, x, bo, gain, bias, wup, bup, d_hid):
    groups, _, part, width = x.shape
    rows = groups * part
    hidden = wup.shape[1]
    block = 512
    first, second = width // block, hidden // block
    bo, gain, bias, bup = (v.reshape(1, -1) for v in (bo, gain, bias, bup))

    def at(index, low, count):
        return jnp.clip(index - low, 0, count - 1)

    def columns(tall, low, count):
        return pl.BlockSpec((tall, block), lambda i, h: (0, at(i, low, count)))

    third = first + second
    return pl.pallas_call(
        functools.partial(middle_kernel, (first, second)),
        grid_spec=pltpu.PrefetchScalarGridSpec(
            num_scalar_prefetch=1,
            grid=(first + second + first,),
            in_specs=[
                whole_spec(heads),
                columns(width, 0, first),
                pl.BlockSpec(
                    (groups, None, part, block), lambda i, h: (0, c, 0, at(i, 0, first))
                ),
                columns(1, 0, first),
                whole_spec(gain),
                whole_spec(bias),
                columns(width, first, second),
                columns(1, first, second),
                pl.BlockSpec((None, rows, block), lambda i, h: (c, 0, at(i, first, second))),
                pl.BlockSpec((block, hidden), lambda i, h: (at(i, third, first), 0)),
            ],
            out_specs=[
                pl.BlockSpec((part, width), lambda i, h: (0, 0)),
                columns(rows, third, first),
                columns(rows, first, second),
                columns(rows, first, second),
            ]
            + [columns(rows, third + k * first // split, first // split) for k in range(split)],
            scratch_shapes=[
                pltpu.VMEM((rows, width), F32),
                pltpu.VMEM((rows, width), BF16),
                pltpu.VMEM((rows, hidden), BF16),
            ],
        ),
        out_shape=[
            jax.ShapeDtypeStruct((part, width), F32),
            jax.ShapeDtypeStruct((rows, width), BF16),
            jax.ShapeDtypeStruct((rows, hidden), BF16),
            jax.ShapeDtypeStruct((rows, hidden), BF16),
        ]
        + [jax.ShapeDtypeStruct((rows, width // split), BF16)] * split,
        compiler_params=pltpu.CompilerParams(vmem_limit_bytes=VMEM),
        cost_estimate=cost(2 * rows * width * (width + 2 * hidden)),
    )(here, heads, wo, x, bo, gain, bias, wup, bup, d_hid, wup)


def middle_back_kernel(terms, mid, cot, gain, wo, d_mid, d_branch, sums, d_att):

    @pl.when(pl.program_id(0) == 0)
    def _():
        d_normed = terms[...].astype(F32)
        values = mid[...]
        centred = values - jnp.mean(values, axis=-1, keepdims=True)
        inverse = lax.rsqrt(jnp.mean(centred * centred, axis=-1, keepdims=True) + EPSILON)
        xhat = centred * inverse
        total = cot[...].astype(F32) + norm_back(d_normed, gain[...], xhat, inverse)
        low = total.astype(BF16)
        d_mid[...] = total
        d_branch[...] = low
        sums[0:1, :] = jnp.sum(d_normed * xhat, axis=0, keepdims=True)
        sums[1:2, :] = jnp.sum(d_normed, axis=0, keepdims=True)
        sums[2:3, :] = jnp.sum(low.astype(F32), axis=0, keepdims=True)

    d_att[...] = times_trans(d_branch[...], wo[...]).astype(BF16)


def middle_back(terms, mid, cot, gain, wo):
    part, width = mid.shape
    groups = lax.axis_size("tensor")
    block = width // groups
    rows = pl.BlockSpec((part, width), lambda j: (0, 0))
    return pl.pallas_call(
        middle_back_kernel,
        grid=(groups,),
        in_specs=[
            rows,
            rows,
            rows,
            pl.BlockSpec((1, width), lambda j: (0, 0)),
            pl.BlockSpec((block, width), lambda j: (j, 0)),
        ],
        out_specs=[
            rows,
            rows,
            pl.BlockSpec((8, width), lambda j: (0, 0)),
            pl.BlockSpec((None, part, block), lambda j: (j, 0, 0)),
        ],
        out_shape=[
            jax.ShapeDtypeStruct((part, width), F32),
            jax.ShapeDtypeStruct((part, width), BF16),
            jax.ShapeDtypeStruct((8, width), F32),
            jax.ShapeDtypeStruct((groups, part, block), BF16),
        ],
        compiler_params=pltpu.CompilerParams(vmem_limit_bytes=VMEM),
        cost_estimate=cost(2 * part * width * width),
    )(terms, mid, cot, gain.reshape(1, -1), wo)


def gradient_terms(lefts, groups, me, blocks):
    half = blocks // 2
    bits = place_bits(blocks)
    part_of = [left[1] if isinstance(left, tuple) else None for left in lefts]
    lefts = [left[0] if isinstance(left, tuple) else left for left in lefts]
    count = len(lefts)
    rights = [right for group in groups for right in group]
    entry_of = [right[1] if isinstance(right, tuple) else None for right in rights]
    rights = [right[0] if isinstance(right, tuple) else right for right in rights]
    width = lefts[0].shape[-1] // blocks
    total = sum(right.shape[-1] for right in rights[::count])

    def source(j, m):
        return xor_source(jnp.where(j < half, j + half, j - half), m[0], bits)

    def right_spec(right, t):
        if t is None:
            return whole_spec(right)
        return pl.BlockSpec((None, None) + right.shape[2:], lambda j, m: (t, m[1], 0, 0))

    def left_spec(left, c):
        if c is None:
            return pl.BlockSpec((left.shape[0], width), lambda j, m: (0, source(j, m)))
        shape = (left.shape[0], None, left.shape[2], width)
        return pl.BlockSpec(shape, lambda j, m: (0, c, 0, source(j, m)))

    def kernel(me_ref, *refs):
        left_refs, right_refs = refs[:count], refs[count:]
        send, keep = refs[-2:]
        step = pl.program_id(0)

        def fill(target):
            place = 0
            turned = [ref[...].reshape(-1, width).T for ref in left_refs]
            for g in range(len(groups)):
                value = None
                for i in range(count):
                    more = mm(turned[i], right_refs[g * count + i][...])
                    value = more if value is None else value + more
                columns = value.shape[1]
                target[:, place : place + columns] = value.astype(BF16)
                place += columns

        @pl.when(step < half)
        def _():
            fill(send)

        @pl.when(step >= half)
        def _():
            fill(keep)

    shape = jax.ShapeDtypeStruct((half, width, total), BF16)
    return pl.pallas_call(
        kernel,
        grid_spec=pltpu.PrefetchScalarGridSpec(
            num_scalar_prefetch=1,
            grid=(blocks,),
            in_specs=[left_spec(left, c) for left, c in zip(lefts, part_of)]
            + [right_spec(right, t) for right, t in zip(rights, entry_of)],
            out_specs=[
                pl.BlockSpec((None, width, total), lambda j, m: (jnp.minimum(j, half - 1), 0, 0)),
                pl.BlockSpec((None, width, total), lambda j, m: (jnp.maximum(j - half, 0), 0, 0)),
            ],
        ),
        out_shape=[shape, shape],
        compiler_params=pltpu.CompilerParams(vmem_limit_bytes=VMEM),
        cost_estimate=cost(2**20),
    )(me, *lefts, *rights)


def normed_back_kernel(dq, dk, dv, wq, wk, wv, x, terms, gain_sum, bias_sum):
    total = times_trans(dq[...], wq[...]) + times_trans(dk[...], wk[...])
    total = total + times_trans(dv[...], wv[...])
    terms[...] = total.astype(BF16)
    values = x[...].astype(F32)
    centred = values - jnp.mean(values, axis=-1, keepdims=True)
    inverse = lax.rsqrt(jnp.mean(centred * centred, axis=-1, keepdims=True) + EPSILON)

    @pl.when(pl.program_id(0) == 0)
    def _():
        gain_sum[...] = jnp.zeros_like(gain_sum)
        bias_sum[...] = jnp.zeros_like(bias_sum)

    gain_sum[...] += jnp.sum(total * (centred * inverse), axis=0, keepdims=True)
    bias_sum[...] += jnp.sum(total, axis=0, keepdims=True)


def normed_back(dq, dk, dv, wq, wk, wv, x):
    rows, width = x.shape
    size = min(512, rows)
    thin = pl.BlockSpec((size, dq.shape[1]), lambda i: (i, 0))
    tall = pl.BlockSpec((size, width), lambda i: (i, 0))
    line = pl.BlockSpec((1, width), lambda i: (0, 0))
    return pl.pallas_call(
        normed_back_kernel,
        grid=(rows // size,),
        in_specs=[thin] * 3 + [whole_spec(w) for w in (wq, wk, wv)] + [tall],
        out_specs=[tall, line, line],
        out_shape=[
            jax.ShapeDtypeStruct((rows, width), BF16),
            jax.ShapeDtypeStruct((1, width), F32),
            jax.ShapeDtypeStruct((1, width), F32),
        ],
        compiler_params=pltpu.CompilerParams(vmem_limit_bytes=VMEM),
        cost_estimate=cost(6 * rows * width * dq.shape[1]),
    )(dq, dk, dv, wq, wk, wv, x)


def input_back(d_normed, x, d_mid, gain):
    rows, width = x.shape
    size = min(128, rows)

    def kernel(terms, x_ref, mid, gain_ref, out):
        values = x_ref[...].astype(F32)
        centred = values - jnp.mean(values, axis=-1, keepdims=True)
        inverse = lax.rsqrt(jnp.mean(centred * centred, axis=-1, keepdims=True) + EPSILON)
        back = norm_back(terms[...].astype(F32), gain_ref[...], centred * inverse, inverse)
        out[...] = mid[...] + back

    tall = pl.BlockSpec((size, width), lambda i: (i, 0))
    return pl.pallas_call(
        kernel,
        grid=(rows // size,),
        in_specs=[tall, tall, tall, pl.BlockSpec((1, width), lambda i: (0, 0))],
        out_specs=tall,
        out_shape=jax.ShapeDtypeStruct((rows, width), F32),
        compiler_params=pltpu.CompilerParams(vmem_limit_bytes=VMEM),
        cost_estimate=cost(2**20),
    )(d_normed, x, d_mid, gain.reshape(1, -1))


def both_parts(lefts, weight, transposed, columns, groups=None):
    block = min(512, columns)
    part_of = [left[1] if isinstance(left, tuple) else None for left in lefts]
    lefts = [left[0] if isinstance(left, tuple) else left for left in lefts]
    depth = lefts[0].shape[-1]
    rows = lefts[0].shape[0] * (1 if part_of[0] is None else lefts[0].shape[2])

    def kernel(*refs):
        weight_ref, out = refs[-2:]
        for c in range(len(lefts)):
            left = refs[c][...].reshape(-1, depth)
            product = times_trans if transposed else mm
            value = product(left, weight_ref[...]).astype(BF16)
            if groups is None:
                out[c] = value
            else:
                out[:, c] = value.reshape(groups, rows // groups, block)

    def left_spec(left, c):
        if c is None:
            return whole_spec(left)
        return pl.BlockSpec((left.shape[0], None) + left.shape[2:], lambda j: (0, c, 0, 0))

    shape = (len(lefts), rows)
    if groups is not None:
        shape = (groups, len(lefts), rows // groups)
    if transposed:
        weight_spec = pl.BlockSpec((block, depth), lambda j: (j, 0))
    else:
        weight_spec = pl.BlockSpec((depth, block), lambda j: (0, j))
    return pl.pallas_call(
        kernel,
        grid=(columns // block,),
        in_specs=[left_spec(left, c) for left, c in zip(lefts, part_of)] + [weight_spec],
        out_specs=pl.BlockSpec(shape + (block,), lambda j: (0,) * len(shape) + (j,)),
        out_shape=jax.ShapeDtypeStruct(shape + (columns,), BF16),
        compiler_params=pltpu.CompilerParams(vmem_limit_bytes=VMEM),
        cost_estimate=cost(2 * len(lefts) * rows * depth * columns),
    )(*lefts, weight)


def swap_bit(values, axis, bit):
    size = lax.axis_size(axis)
    return lax.ppermute(values, axis, [(i, i ^ (1 << bit)) for i in range(size)])


def third(k, steps):
    return range((k - 1) * steps // 3 + 1, k * steps // 3 + 1)


def fence(things, arrays=()):
    lists = [thing.live for thing in things]
    flat = lax.optimization_barrier(tuple(v for values in lists for v in values) + tuple(arrays))
    place = 0
    for thing, values in zip(things, lists):
        thing.live = list(flat[place : place + len(values)])
        place += len(values)
    return flat[place:]


def exchange(values):
    return lax.all_to_all(values, "tensor", 0, 0)


def add_and_split(sources, outs, dims):
    places = 2**dims
    rows = sources[0][0].shape[1]
    size = min(64, rows)
    widths = [sum(stop - start for _, start, stop in picks) for picks, _ in outs]

    def kernel(*refs):
        target = 2 * len(sources)
        for picks, dim in outs:
            shift = dims - 1 - dim
            for half in range(2):
                chosen = [p for p in range(places) if (p >> shift) & 1 == half]
                at = 0
                for source, start, stop in picks:
                    keep, got = refs[2 * source : 2 * source + 2]
                    for q, p in enumerate(chosen):
                        value = keep[p, :, start:stop].astype(F32) + got[p, :, start:stop].astype(F32)
                        refs[target][q, :, at : at + stop - start] = value.astype(BF16)
                    at += stop - start
                target += 1

    def block(count, columns):
        return pl.BlockSpec((count, size, columns), lambda i: (0, i, 0))

    flat = [v for pair in sources for v in pair]
    return pl.pallas_call(
        kernel,
        grid=(rows // size,),
        in_specs=[block(places, v.shape[2]) for v in flat],
        out_specs=[block(places // 2, w) for w in widths for _ in range(2)],
        out_shape=[
            jax.ShapeDtypeStruct((places // 2, rows, w), BF16) for w in widths for _ in range(2)
        ],
        compiler_params=pltpu.CompilerParams(vmem_limit_bytes=VMEM),
        cost_estimate=cost(2**20),
    )(*flat)


def finish_sum(live, width, cuts, turned, kind):
    rows, columns = live[0].shape[1:]
    count = columns // width
    total = 2 * columns

    def kernel(*refs):
        sums = []
        for c in range(2 * count):
            keep, got = refs[2 * (c % 2) : 2 * (c % 2) + 2]
            place = slice(c // 2 * width, (c // 2 + 1) * width)
            sums.append(keep[0, :, place].astype(F32) + got[0, :, place].astype(F32))
        value = jnp.concatenate(sums, axis=1)
        if turned:
            refs[4][...] = value.T.astype(kind)
            return
        for k in range(cuts):
            refs[4 + k][...] = value[:, k * total // cuts : (k + 1) * total // cuts].astype(kind)

    size = rows if turned else min(64, rows)
    shape = (total, rows) if turned else (rows, total // cuts)
    block = (total, rows) if turned else (size, total // cuts)
    return pl.pallas_call(
        kernel,
        grid=(rows // size,),
        in_specs=[pl.BlockSpec((1, size, columns), lambda i: (0, i, 0))] * 4,
        out_specs=[pl.BlockSpec(block, lambda i: (i, 0) if not turned else (0, 0))] * cuts,
        out_shape=[jax.ShapeDtypeStruct(shape, kind)] * cuts,
        compiler_params=pltpu.CompilerParams(vmem_limit_bytes=VMEM),
        cost_estimate=cost(2**20),
    )(*live)


class DpSum:
    def __init__(self, send, keep, cuts):
        self.live = [send, keep]
        self.cuts = cuts
        self.rest = place_bits(lax.axis_size("dp")) - 1
        self.width = keep.shape[-1] // cuts
        self.left = [list(range(1, self.rest + 1)) for _ in range(2)]

    def core(self):
        self.live = [self.live[1], swap_bit(self.live[0], "dp", 0)]

    def dim(self, odd):
        return len(self.left[odd]) - 1 if odd else 0

    def split(self):
        outs = [
            ([(0, c * self.width, (c + 1) * self.width)], self.dim(c % 2)) for c in range(self.cuts)
        ]
        self.live = list(add_and_split([tuple(self.live)], outs, self.rest))

    def first(self, *cuts):
        for c in cuts:
            values = self.live[2 * c + 1]
            self.live[2 * c + 1] = swap_bit(values, "dp", self.left[c % 2][self.dim(c % 2)])

    def add(self):
        bits = [left[self.dim(odd)] for odd, left in enumerate(self.left)]
        for odd in range(2):
            self.left[odd].remove(bits[odd])
        count = len(self.live) // 2
        sources = [(self.live[2 * k], self.live[2 * k + 1]) for k in range(count)]
        outs = [
            ([(k, 0, sources[k][0].shape[2]) for k in range(odd, count, 2)], self.dim(odd))
            for odd in range(2)
        ]
        self.live = list(add_and_split(sources, outs, len(self.left[0])))

    def send(self):
        for odd in range(2):
            bit = self.left[odd][self.dim(odd)]
            self.live[2 * odd + 1] = swap_bit(self.live[2 * odd + 1], "dp", bit)
        while len(self.left[0]) > 1:
            self.add()
            self.send()

    def total(self, cuts=1, turned=False, kind=F32):
        return finish_sum(self.live, self.width, cuts, turned, kind)


class WeightGather:
    def __init__(self, own, me):
        self.blocks = lax.axis_size("dp")
        self.size = lax.axis_size("tensor")
        self.usual = (self.size, self.blocks) == (4, 8)
        self.me = me
        share = own.shape[1 if self.usual else 0] // self.blocks
        axis = 1 if self.usual else 0
        self.live = [lax.dynamic_slice_in_dim(own, me[0] * share, share, axis)]

    def advance(self, k):
        if not self.usual:
            if k == 0:
                self.live = [lax.all_gather(self.live[0], ("tensor", "dp"), axis=0, tiled=True)]
            return
        if k == 0:
            own = self.live[0]
            self.live += [
                lax.ppermute(own, "tensor", [(i, (i + m) % self.size) for i in range(self.size)])
                for m in range(1, self.size)
            ]
        elif k == 1:
            own, one, two, three = self.live
            even = lax.axis_index("tensor") % 2 == 0
            near = jnp.concatenate([jnp.where(even, own, one), jnp.where(even, three, own)])
            far = jnp.concatenate([jnp.where(even, two, three), jnp.where(even, one, two)])
            self.live = [near, swap_bit(near, "dp", 1), far, swap_bit(far, "dp", 2)]
            self.live += [swap_bit(near, "dp", 0), swap_bit(far, "dp", 0)]
        elif k == 2:
            near, near_one, far, far_one, near_core, far_core = self.live
            near, far = jnp.stack([near, near_one]), jnp.stack([far, far_one])
            self.live = [near, far, near_core[None], far_core[None]]
            self.live += [swap_bit(near, "dp", 2), swap_bit(far, "dp", 1)]
            self.live += [swap_bit(near_one, "dp", 0)[None], swap_bit(far_one, "dp", 0)[None]]
        elif k == 3:
            near, far, near_core, far_core, near_two, far_two, near_one_core, far_one_core = self.live
            own = [(near, 0), (near, 1), (far, 0), (far, 1)]
            other = [(v, 0) for v in (near_core, near_one_core, far_core, far_one_core)]
            self.live = [near_two, far_two, self.place(own, other, 0, None)]
        else:
            near_two, far_two, half = self.live
            self.live = [near_two, swap_bit(near_two, "dp", 0)]
            self.live += [far_two, swap_bit(far_two, "dp", 0), half]

    def place(self, own, other, late, half):
        rows, width = own[0][0].shape[1:]
        blocks = own + other

        def kernel(me_ref, *refs):
            out = refs[-1]
            step, odd = pl.program_id(0), me_ref[0] & 1
            for k in range(4):
                for flip in range(2):

                    @pl.when((step == k) & (odd == flip))
                    def _():
                        out[:, flip * width : (flip + 1) * width] = refs[k][...]
                        out[:, (1 - flip) * width : (2 - flip) * width] = refs[k + 4][...]

        def source(entry):
            return pl.BlockSpec((None, rows, width), lambda s, m: (entry, 0, 0))

        def target(s, m):
            top, one = s < 2, s & 1
            low = jnp.where(top, 2 * one + 4 * late, 4 * one + 2 * late)
            return (jnp.where(top, m[2], 1 - m[2]), (low ^ m[0]) >> 1)

        more = [] if half is None else [half]
        return pl.pallas_call(
            kernel,
            grid_spec=pltpu.PrefetchScalarGridSpec(
                num_scalar_prefetch=1,
                grid=(4,),
                in_specs=[source(entry) for _, entry in blocks]
                + [pl.BlockSpec(memory_space=pl.ANY)] * len(more),
                out_specs=pl.BlockSpec((rows, 2 * width), target),
            ),
            out_shape=jax.ShapeDtypeStruct((2 * rows, 8 * width), BF16),
            input_output_aliases={9: 0} if more else {},
            compiler_params=pltpu.CompilerParams(vmem_limit_bytes=VMEM),
            cost_estimate=cost(2**20),
        )(self.me, *[array for array, _ in blocks], *more)

    def whole(self):
        if not self.usual:
            return self.live[0]
        near, near_core, far, far_core, half = self.live
        own = [(near, 0), (near, 1), (far, 0), (far, 1)]
        other = [(near_core, 0), (near_core, 1), (far_core, 0), (far_core, 1)]
        return self.place(own, other, 1, half)


class SmallSum:
    def __init__(self, vectors, me):
        self.vectors = vectors
        self.blocks = blocks = lax.axis_size("dp")
        self.bits = place_bits(blocks)
        places = jnp.stack([xor_source(p, me, self.bits) for p in range(blocks)]).reshape(-1)
        self.ordered = sorted(range(len(vectors)), key=lambda i: not vectors[i][1])
        wide = [vectors[i][0].reshape(blocks, -1) for i in self.ordered]
        wide = jnp.take(jnp.concatenate(wide, axis=1), places, axis=0)
        self.live = [wide.reshape((2,) * self.bits + wide.shape[1:])]

    def move(self):
        self.steps = getattr(self, "steps", 0) + 1
        while self.live[0].ndim > 1:
            values = self.live[0]
            self.live = [values[0] + swap_bit(values[1], "dp", self.bits - values.ndim + 1)]
            if self.steps < 3:
                return

    def tensor(self):
        values = self.live[0]
        both = sum(v[0].shape[0] // self.blocks for v in self.vectors if v[1])
        summed, alone = values[..., :both], values[..., both:]
        for bit in range(place_bits(lax.axis_size("tensor"))):
            summed = summed + swap_bit(summed, "tensor", bit)
        self.live = [jnp.concatenate([summed, alone], axis=-1)]

    def total(self):
        out, start = [None] * len(self.vectors), 0
        for i in self.ordered:
            size = self.vectors[i][0].shape[0] // self.blocks
            out[i] = self.live[0][start : start + size]
            start += size
        return out


def on_device(
    inputs,
    segments,
    cotangent,
    norm1_gain,
    norm1_bias,
    query_weight,
    query_bias,
    key_weight,
    value_weight,
    value_bias,
    output_weight,
    output_bias,
    norm2_gain,
    norm2_bias,
    up_weight,
    up_bias,
    down_weight,
    down_bias,
):
    groups = lax.axis_size("tensor")
    blocks = lax.axis_size("dp")
    here = lax.axis_index("tensor").astype(jnp.int32)
    side = here // (groups // 2)
    me = lax.axis_index("dp").astype(jnp.int32)
    me = jnp.stack([me, here, side])
    rows, width = inputs.shape
    share = rows // groups
    part = share // PARTS
    local = query_weight.shape[1]
    size = width // blocks

    def by_part(values):
        return values.reshape(groups, PARTS, part, values.shape[1])

    def own(values):
        return lax.dynamic_slice_in_dim(values, here * share, share, 0)

    weight = WeightGather(output_weight, me)
    weight.advance(0)
    normed, query, key, value = project(
        inputs,
        norm1_gain,
        norm1_bias,
        query_weight,
        query_bias,
        key_weight,
        value_weight,
        value_bias,
    )
    heads = [None] * PARTS
    heads[0] = attend(0, segments, query, key, value, groups)
    cot, heads[0], query, key, value = fence([weight], (cotangent, heads[0], query, key, value))

    heads[0] = lax.all_gather(heads[0].reshape(groups * part, local), "tensor", axis=0)
    weight.advance(1)
    heads[1] = attend(1, segments, query, key, value, groups)
    cot, heads[1] = fence([weight], (cot, heads[1]))
    heads[1] = lax.all_gather(heads[1].reshape(groups * part, local), "tensor", axis=0)
    weight.advance(2)
    cot_parts = by_part(cot)
    cots = [(cot_parts, c) for c in range(PARTS)]
    d_hidden = both_parts(cots, down_weight, True, down_weight.shape[0])
    d_hidden, cot = fence([], (d_hidden, cot))
    weight.advance(3)
    d_hidden, cot = fence([weight], (d_hidden, cot))
    weight.advance(4)
    fence([weight])
    whole = weight.whole()
    whole, heads[0] = fence([], (whole, heads[0]))

    own_mid, low, hidden, d_up, terms = ([None] * PARTS for _ in range(5))

    def middle(c):
        own_mid[c], low[c], hidden[c], d_up[c], *term = middle_call(
            1,
            c,
            me,
            heads[c],
            whole,
            by_part(inputs),
            output_bias,
            norm2_gain,
            norm2_bias,
            up_weight,
            up_bias,
            d_hidden,
        )
        terms[c] = term[0].reshape(groups, part, width)

    middle(0)
    terms[0], heads[1] = fence([], (terms[0], heads[1]))

    terms[0] = lax.psum_scatter(terms[0], "tensor", scatter_dimension=0)
    middle(1)
    cot_own = own(cot)
    terms[1], cot_own, low[0], low[1], d_up[0], d_up[1] = fence(
        [], (terms[1], cot_own, *low, *d_up)
    )

    terms[1] = lax.psum_scatter(terms[1], "tensor", scatter_dimension=0)
    up_terms = gradient_terms(low, [d_up], me, blocks)
    d_mids, d_branches, sums = ([None] * PARTS for _ in range(3))

    def back(c):
        d_mids[c], d_branches[c], sums[c], d_att = middle_back(
            terms[c], own_mid[c], cot_own[c * part : (c + 1) * part], norm2_gain, whole
        )
        return d_att

    terms[0], hidden[0], hidden[1], *up_terms = fence([], (terms[0], *hidden, *up_terms))
    d_att = back(0)
    d_att, hidden[0], hidden[1] = fence([], (d_att, *hidden))
    out_terms = both_parts(hidden, down_weight, False, width, groups)
    out_terms, hidden[0], hidden[1] = fence([], (out_terms, *hidden))
    down_terms = gradient_terms(cots, [hidden], me, blocks)
    d_att, *down_terms = fence([], (d_att, *down_terms))
    got = [exchange(d_att), None]
    cot_sum = column_sums(cot)
    up_bias_sum = column_sums(d_up[0]) + column_sums(d_up[1])
    up_sum = DpSum(*up_terms, 2)
    down_sum = DpSum(*down_terms, 2)
    terms[1], out_terms, d_branches[0], cot_sum, up_bias_sum = fence(
        [up_sum, down_sum], (terms[1], out_terms, d_branches[0], cot_sum, up_bias_sum)
    )

    d_att = back(1)
    d_att, got[0], *d_branches = fence([up_sum, down_sum], (d_att, got[0], *d_branches))
    got[1] = exchange(d_att)
    up_sum.core()
    down_sum.core()
    views = [h.reshape(groups, groups, part, local) for h in heads]
    wo_terms = gradient_terms(d_branches, [[(v, t) for v in views] for t in range(groups)], me, blocks)
    wo_sum = DpSum(*wo_terms, 2)
    got[1], out_terms = fence([wo_sum, up_sum, down_sum], (got[1], out_terms))

    out_sum = lax.psum_scatter(out_terms, "tensor", scatter_dimension=0)
    up_sum.split()
    up_sum.first(0, 1)
    wo_sum.core()
    d_query, d_key, d_value = attend_back(segments, query, key, value, got)
    wo_sum.split()
    d_query, d_key, d_value = fence([up_sum, wo_sum, down_sum], (d_query, d_key, d_value))
    wo_sum.first(0, 1)
    qkv_sum = DpSum(
        *gradient_terms([normed], [[d] for d in (d_query, d_key, d_value)], me, blocks), 2
    )
    down_sum.split()
    d_query, d_key, d_value = fence([wo_sum, qkv_sum, down_sum], (d_query, d_key, d_value))
    qkv_sum.core()
    down_sum.first(0, 1)
    terms_in, gain1, bias1 = normed_back(
        d_query, d_key, d_value, query_weight, key_weight, value_weight, inputs
    )
    qkv_sum.split()
    wo_sum.add()
    gain1, bias1, terms_in, d_query, d_value = fence(
        [qkv_sum, wo_sum, down_sum], (gain1, bias1, terms_in, d_query, d_value)
    )

    d_normed = lax.psum_scatter(
        terms_in.reshape(groups, share, width), "tensor", scatter_dimension=0
    )
    qkv_sum.first(0, 1)
    wo_sum.send()
    two = sums[0] + sums[1]
    small = SmallSum(
        [
            (gain1[0], True),
            (bias1[0], True),
            (two[0], True),
            (two[1], True),
            (two[2], True),
            (cot_sum, False),
            (column_sums(d_query), False),
            (column_sums(d_value), False),
            (up_bias_sum, False),
        ],
        me[:1],
    )
    small.tensor()
    down_sum.add()
    out_sum, *_ = fence([qkv_sum, wo_sum, down_sum, small, up_sum], (out_sum,))
    down_sum.send()
    qkv_sum.add()
    qkv_sum.send()
    small.move()
    small.move()
    small.move()
    wo_terms = wo_sum.total(turned=True, kind=BF16)[0].reshape(groups, local, size)
    to_all = [
        lax.dynamic_index_in_dim(wo_terms, (here - m) % groups, 0, keepdims=False)
        for m in range(groups)
    ]
    up_sum.add()
    out_sum, *to_all = fence([qkv_sum, small, down_sum, up_sum], (out_sum, *to_all))
    wo_got = [to_all[0]]
    for m in range(1, groups):
        ring = [(i, (i - m) % groups) for i in range(groups)]
        wo_got.append(lax.ppermute(to_all[m], "tensor", ring))
    up_sum.send()
    total = [own_mid[c] + (out_sum[c].astype(F32) + down_bias) for c in range(PARTS)]
    output = jnp.concatenate([t.astype(BF16) for t in total], axis=0)
    qkv_grads = qkv_sum.total(3)
    (up_weight_grad,) = up_sum.total()
    (down_weight_grad,) = down_sum.total(turned=True)
    d_mid = jnp.concatenate(d_mids, axis=0)
    rows_own = own(inputs)
    small_sums = small.total()
    up_weight_grad, down_weight_grad, output, d_mid, rows_own, *others = fence(
        [],
        (up_weight_grad, down_weight_grad, output, d_mid, rows_own, *qkv_grads, *small_sums),
    )
    qkv_grads, small_sums = others[:3], others[3:]
    input_grad = input_back(d_normed, rows_own, d_mid, norm1_gain)
    input_grad, *wo_got = fence([], (input_grad, *wo_got))
    output_weight_grad = sum(g.astype(F32) for g in wo_got)
    (
        norm1_gain_grad,
        norm1_bias_grad,
        norm2_gain_grad,
        norm2_bias_grad,
        output_bias_grad,
        down_bias_grad,
        query_bias_grad,
        value_bias_grad,
        up_bias_grad,
    ) = small_sums
    return (
        output,
        input_grad,
        norm1_gain_grad,
        norm1_bias_grad,
        qkv_grads[0],
        query_bias_grad,
        qkv_grads[1],
        qkv_grads[2],
        value_bias_grad,
        output_weight_grad,
        output_bias_grad,
        norm2_gain_grad,
        norm2_bias_grad,
        up_weight_grad,
        up_bias_grad,
        down_weight_grad,
        down_bias_grad,
    )


def solution(mesh):
    return jax.shard_map(
        on_device,
        mesh=mesh,
        in_specs=(
            P("dp", None),
            P("dp", None),
            P("dp", None),
            P(),
            P(),
            P(None, "tensor"),
            P("tensor"),
            P(None, "tensor"),
            P(None, "tensor"),
            P("tensor"),
            P("tensor", None),
            P(),
            P(),
            P(),
            P(None, "tensor"),
            P("tensor"),
            P("tensor", None),
            P(),
        ),
        out_specs=(
            P(("dp", "tensor"), None),
            P(("dp", "tensor"), None),
            P("dp"),
            P("dp"),
            P("dp", "tensor"),
            P(("tensor", "dp")),
            P("dp", "tensor"),
            P("dp", "tensor"),
            P(("tensor", "dp")),
            P("tensor", "dp"),
            P("dp"),
            P("dp"),
            P("dp"),
            P("dp", "tensor"),
            P(("tensor", "dp")),
            P("tensor", "dp"),
            P("dp"),
        ),
        check_vma=False,
    )
```

```python
import functools

import jax
import jax.numpy as jnp
from jax import lax
from jax.experimental import pallas as pl
from jax.experimental.pallas import tpu as pltpu
from jax.sharding import PartitionSpec as P

HEAD_DIM = 128
LONGEST = 512
EPSILON = 1e-05
MASKED_SCORE = -1e30
SCALING = HEAD_DIM ** (-0.5)
F32 = jnp.float32
BF16 = jnp.bfloat16
PARTS = 2
COST = 0
VMEM = 60 * 2**20


def mm(left_side, right_side):
    return lax.dot_general(
        left_side, right_side, (((1,), (0,)), ((), ())), preferred_element_type=F32
    )


def times_trans(left_side, right_side):
    return lax.dot_general(
        left_side, right_side, (((1,), (1,)), ((), ())), preferred_element_type=F32
    )


def trans_times(left_side, right_side):
    return lax.dot_general(
        left_side, right_side, (((0,), (0,)), ((), ())), preferred_element_type=F32
    )


def column_sums(values):
    return jnp.sum(values.astype(F32), axis=0)


def row_stats(rows):
    average = jnp.mean(rows, axis=-1, keepdims=True)
    centred = rows - average
    spread = jnp.mean(centred * centred, axis=-1, keepdims=True)
    return average, lax.rsqrt(spread + EPSILON)


def norm_back(d_normed, gain, xhat, inverse):
    scaled = d_normed * gain
    first = jnp.mean(scaled, axis=-1, keepdims=True)
    second = jnp.mean(scaled * xhat, axis=-1, keepdims=True)
    return inverse * (scaled - first - xhat * second)


def cost(flops):
    return pl.CostEstimate(flops=COST and flops, bytes_accessed=2**10, transcendentals=0)


def key_start(first):
    return max(0, (first - (LONGEST - 1)) // 256 * 256)


def segment_column(seg_row):
    length = seg_row.shape[1]
    return jnp.broadcast_to(seg_row[...], (128, length)).T[:, :1]


def probabilities(seg_row, seg_col, query, keys, first, last):
    low, high = key_start(first), last
    scores = times_trans(keys[low:high, :], query)
    shape = (high - low, last - first)
    key_place = lax.broadcasted_iota(jnp.int32, shape, 0) + low
    query_place = lax.broadcasted_iota(jnp.int32, shape, 1) + first
    same = seg_col[low:high, :] == seg_row[:, first:last]
    scores = jnp.where(same & (key_place <= query_place), scores, MASKED_SCORE)
    weights = jnp.exp(scores - jnp.max(scores, axis=0, keepdims=True))
    return weights * (1.0 / jnp.sum(weights, axis=0, keepdims=True))


def forward_kernel(c, seg_row, query, key, value, out):
    groups, part = out.shape[:2]
    seg_col = segment_column(seg_row)
    for t in range(groups):
        first = (t * PARTS + c) * part
        last = first + part
        low = key_start(first)
        probs = probabilities(seg_row, seg_col, query[first:last, :], key, first, last)
        out[t] = trans_times(probs.astype(BF16), value[low:last, :]).astype(BF16)


def backward_kernel(size, seg_row, query, key, value, *refs):
    got = refs[:PARTS]
    d_query, d_key, d_value, d_attended, key_sum, value_sum = refs[PARTS:]
    groups, part = got[0].shape[:2]
    for t in range(groups):
        for c in range(PARTS):
            start = (t * PARTS + c) * part
            d_attended[start : start + part, :] = got[c][t]
    seg_col = segment_column(seg_row)
    key_sum[...] = jnp.zeros_like(key_sum)
    value_sum[...] = jnp.zeros_like(value_sum)
    for block in range(query.shape[0] // size):
        low, high = key_start(block * size), (block + 1) * size
        rows = slice(block * size, high)
        probs = probabilities(seg_row, seg_col, query[rows, :], key, block * size, high)
        value_sum[low:high, :] += mm(probs.astype(BF16), d_attended[rows, :])
        d_probs = times_trans(value[low:high, :], d_attended[rows, :])
        inner = jnp.sum(probs * d_probs, axis=0, keepdims=True)
        d_scores = (probs * (d_probs - inner)).astype(BF16)
        d_query[rows, :] = (trans_times(d_scores, key[low:high, :]) * SCALING).astype(BF16)
        key_sum[low:high, :] += mm(d_scores, query[rows, :])
    d_key[...] = key_sum[...].astype(BF16)
    d_value[...] = value_sum[...].astype(BF16)


def attend(c, segments, query, key, value, groups):
    length, local = query.shape
    part = length // groups // PARTS
    tall = pl.BlockSpec((length, HEAD_DIM), lambda h: (0, h))
    return pl.pallas_call(
        functools.partial(forward_kernel, c),
        grid=(local // HEAD_DIM,),
        in_specs=[pl.BlockSpec((1, length), lambda h: (0, 0))] + [tall] * 3,
        out_specs=pl.BlockSpec((groups, part, HEAD_DIM), lambda h: (0, 0, h)),
        out_shape=jax.ShapeDtypeStruct((groups, part, local), BF16),
        compiler_params=pltpu.CompilerParams(vmem_limit_bytes=VMEM),
        cost_estimate=cost(2**20),
    )(segments, query, key, value)


def attend_back(segments, query, key, value, got):
    length = query.shape[0]
    tall = pl.BlockSpec((length, HEAD_DIM), lambda h: (0, h))
    return pl.pallas_call(
        functools.partial(backward_kernel, min(256, length)),
        grid=(query.shape[1] // HEAD_DIM,),
        in_specs=[pl.BlockSpec((1, length), lambda h: (0, 0))]
        + [tall] * 3
        + [pl.BlockSpec(g.shape[:2] + (HEAD_DIM,), lambda h: (0, 0, h)) for g in got],
        out_specs=[tall] * 3,
        scratch_shapes=[
            pltpu.VMEM((length, HEAD_DIM), BF16),
            pltpu.VMEM((length, HEAD_DIM), F32),
            pltpu.VMEM((length, HEAD_DIM), F32),
        ],
        out_shape=[jax.ShapeDtypeStruct(query.shape, BF16)] * 3,
        compiler_params=pltpu.CompilerParams(vmem_limit_bytes=VMEM),
        cost_estimate=cost(10 * query.shape[0] * length * query.shape[1]),
    )(segments, query, key, value, *got)


def place_bits(blocks):
    return blocks.bit_length() - 1


def xor_source(place, me, bits):
    distance = 0
    for bit in range(bits):
        distance = distance + (((place >> (bits - 1 - bit)) & 1) << bit)
    return distance ^ me


def norm_rows(values, gain, bias):
    average = jnp.mean(values, axis=-1, keepdims=True)
    centred = values - average
    inverse = lax.rsqrt(jnp.mean(centred * centred, axis=-1, keepdims=True) + EPSILON)
    return centred * inverse * gain + bias


def project_kernel(x, gain, bias, wq, bq, wk, wv, bv, normed, query, key, value):
    low = norm_rows(x[...].astype(F32), gain[...], bias[...]).astype(BF16)
    normed[...] = low
    query[...] = ((mm(low, wq[...]) + bq[...]) * SCALING).astype(BF16)
    key[...] = mm(low, wk[...]).astype(BF16)
    value[...] = (mm(low, wv[...]) + bv[...]).astype(BF16)


def whole_spec(array):
    return pl.BlockSpec(array.shape, lambda *_: (0,) * array.ndim)


def project(x, gain, bias, wq, bq, wk, wv, bv):
    rows, width = x.shape
    local = wq.shape[1]
    size = min(512, rows)
    args = [x] + [v.reshape(1, -1) if v.ndim == 1 else v for v in (gain, bias, wq, bq, wk, wv, bv)]
    tall = pl.BlockSpec((size, width), lambda i: (i, 0))
    thin = pl.BlockSpec((size, local), lambda i: (i, 0))
    shape = jax.ShapeDtypeStruct((rows, local), BF16)
    return pl.pallas_call(
        project_kernel,
        grid=(rows // size,),
        in_specs=[tall] + [whole_spec(a) for a in args[1:]],
        out_specs=[tall] + [thin] * 3,
        out_shape=[jax.ShapeDtypeStruct(x.shape, BF16)] + [shape] * 3,
        compiler_params=pltpu.CompilerParams(vmem_limit_bytes=VMEM),
        cost_estimate=cost(6 * rows * width * local),
    )(*args)


def middle_kernel(
    steps, here_ref, heads, wo, x, bo, gain, bias, wup, bup, d_hid, wup_rows,
    own_mid, low_out, hidden, d_up, *rest,
):
    first, second = steps
    *terms, mid, low, d_low = rest
    step = pl.program_id(0)
    block = wo.shape[1]
    here = here_ref[1]
    local = heads.shape[2]

    @pl.when(step == 0)
    def _():
        for t in range(heads.shape[0]):
            low[:, t * local : (t + 1) * local] = heads[t]

    @pl.when(step < first)
    def _():
        branch = mm(low[...], wo[...])
        values = x[...].reshape(branch.shape).astype(F32)
        columns = pl.ds(pl.multiple_of(step * block, block), block)
        mid[:, columns] = values + (branch + bo[...])

    @pl.when(step == first)
    def _():
        low[...] = norm_rows(mid[...], gain[...], bias[...]).astype(BF16)
        part = own_mid.shape[0]
        own_mid[...] = mid[pl.ds(pl.multiple_of(here * part, part), part), :]

    @pl.when((step >= first) & (step < first + second))
    def _():
        piece = 256
        for start in range(0, wup.shape[1], piece):
            columns = slice(start, start + piece)
            up_value = mm(low[...], wup[:, columns]) + bup[:, columns]
            below = 0.5 + 0.5 * lax.erf(up_value * (0.5**0.5))
            density = jnp.exp(-0.5 * up_value * up_value) * 0.3989422804014327
            hidden[:, columns] = (up_value * below).astype(BF16)
            slope = ((below + up_value * density) * d_hid[:, columns].astype(F32)).astype(BF16)
            d_up[:, columns] = slope
            place = pl.multiple_of((step - first) * wup.shape[1] + start, piece)
            d_low[:, pl.ds(place, piece)] = slope

    @pl.when(step >= first + second)
    def _():
        value = times_trans(d_low[...], wup_rows[...]).astype(BF16)

        for k, term in enumerate(terms):
            start = first + second + k * first // len(terms)

            @pl.when((step >= start) & (step < start + first // len(terms)))
            def _():
                term[...] = value

        columns = pl.ds(pl.multiple_of((step - first - second) * block, block), block)
        low_out[...] = low[:, columns]


def middle_call(split, c, here, heads, wo, x, bo, gain, bias, wup, bup, d_hid):
    groups, _, part, width = x.shape
    rows = groups * part
    hidden = wup.shape[1]
    block = 512
    first, second = width // block, hidden // block
    bo, gain, bias, bup = (v.reshape(1, -1) for v in (bo, gain, bias, bup))

    def at(index, low, count):
        return jnp.clip(index - low, 0, count - 1)

    def columns(tall, low, count):
        return pl.BlockSpec((tall, block), lambda i, h: (0, at(i, low, count)))

    third = first + second
    return pl.pallas_call(
        functools.partial(middle_kernel, (first, second)),
        grid_spec=pltpu.PrefetchScalarGridSpec(
            num_scalar_prefetch=1,
            grid=(first + second + first,),
            in_specs=[
                whole_spec(heads),
                columns(width, 0, first),
                pl.BlockSpec(
                    (groups, None, part, block), lambda i, h: (0, c, 0, at(i, 0, first))
                ),
                columns(1, 0, first),
                whole_spec(gain),
                whole_spec(bias),
                columns(width, first, second),
                columns(1, first, second),
                pl.BlockSpec((None, rows, block), lambda i, h: (c, 0, at(i, first, second))),
                pl.BlockSpec((block, hidden), lambda i, h: (at(i, third, first), 0)),
            ],
            out_specs=[
                pl.BlockSpec((part, width), lambda i, h: (0, 0)),
                columns(rows, third, first),
                columns(rows, first, second),
                columns(rows, first, second),
            ]
            + [columns(rows, third + k * first // split, first // split) for k in range(split)],
            scratch_shapes=[
                pltpu.VMEM((rows, width), F32),
                pltpu.VMEM((rows, width), BF16),
                pltpu.VMEM((rows, hidden), BF16),
            ],
        ),
        out_shape=[
            jax.ShapeDtypeStruct((part, width), F32),
            jax.ShapeDtypeStruct((rows, width), BF16),
            jax.ShapeDtypeStruct((rows, hidden), BF16),
            jax.ShapeDtypeStruct((rows, hidden), BF16),
        ]
        + [jax.ShapeDtypeStruct((rows, width // split), BF16)] * split,
        compiler_params=pltpu.CompilerParams(vmem_limit_bytes=VMEM),
        cost_estimate=cost(2 * rows * width * (width + 2 * hidden)),
    )(here, heads, wo, x, bo, gain, bias, wup, bup, d_hid, wup)


def middle_back_kernel(terms, mid, cot, gain, wo, d_mid, d_branch, sums, d_att):

    @pl.when(pl.program_id(0) == 0)
    def _():
        d_normed = terms[...].astype(F32)
        values = mid[...]
        centred = values - jnp.mean(values, axis=-1, keepdims=True)
        inverse = lax.rsqrt(jnp.mean(centred * centred, axis=-1, keepdims=True) + EPSILON)
        xhat = centred * inverse
        total = cot[...].astype(F32) + norm_back(d_normed, gain[...], xhat, inverse)
        low = total.astype(BF16)
        d_mid[...] = total
        d_branch[...] = low
        sums[0:1, :] = jnp.sum(d_normed * xhat, axis=0, keepdims=True)
        sums[1:2, :] = jnp.sum(d_normed, axis=0, keepdims=True)
        sums[2:3, :] = jnp.sum(low.astype(F32), axis=0, keepdims=True)

    d_att[...] = times_trans(d_branch[...], wo[...]).astype(BF16)


def middle_back(terms, mid, cot, gain, wo):
    part, width = mid.shape
    groups = lax.axis_size("tensor")
    block = width // groups
    rows = pl.BlockSpec((part, width), lambda j: (0, 0))
    return pl.pallas_call(
        middle_back_kernel,
        grid=(groups,),
        in_specs=[
            rows,
            rows,
            rows,
            pl.BlockSpec((1, width), lambda j: (0, 0)),
            pl.BlockSpec((block, width), lambda j: (j, 0)),
        ],
        out_specs=[
            rows,
            rows,
            pl.BlockSpec((8, width), lambda j: (0, 0)),
            pl.BlockSpec((None, part, block), lambda j: (j, 0, 0)),
        ],
        out_shape=[
            jax.ShapeDtypeStruct((part, width), F32),
            jax.ShapeDtypeStruct((part, width), BF16),
            jax.ShapeDtypeStruct((8, width), F32),
            jax.ShapeDtypeStruct((groups, part, block), BF16),
        ],
        compiler_params=pltpu.CompilerParams(vmem_limit_bytes=VMEM),
        cost_estimate=cost(2 * part * width * width),
    )(terms, mid, cot, gain.reshape(1, -1), wo)


def gradient_terms(lefts, groups, me, blocks):
    half = blocks // 2
    bits = place_bits(blocks)
    part_of = [left[1] if isinstance(left, tuple) else None for left in lefts]
    lefts = [left[0] if isinstance(left, tuple) else left for left in lefts]
    count = len(lefts)
    rights = [right for group in groups for right in group]
    entry_of = [right[1] if isinstance(right, tuple) else None for right in rights]
    rights = [right[0] if isinstance(right, tuple) else right for right in rights]
    width = lefts[0].shape[-1] // blocks
    total = sum(right.shape[-1] for right in rights[::count])

    def source(j, m):
        return xor_source(jnp.where(j < half, j + half, j - half), m[0], bits)

    def right_spec(right, t):
        if t is None:
            return whole_spec(right)
        return pl.BlockSpec((None, None) + right.shape[2:], lambda j, m: (t, m[1], 0, 0))

    def left_spec(left, c):
        if c is None:
            return pl.BlockSpec((left.shape[0], width), lambda j, m: (0, source(j, m)))
        shape = (left.shape[0], None, left.shape[2], width)
        return pl.BlockSpec(shape, lambda j, m: (0, c, 0, source(j, m)))

    def kernel(me_ref, *refs):
        left_refs, right_refs = refs[:count], refs[count:]
        send, keep = refs[-2:]
        step = pl.program_id(0)

        def fill(target):
            place = 0
            turned = [ref[...].reshape(-1, width).T for ref in left_refs]
            for g in range(len(groups)):
                value = None
                for i in range(count):
                    more = mm(turned[i], right_refs[g * count + i][...])
                    value = more if value is None else value + more
                columns = value.shape[1]
                target[:, place : place + columns] = value.astype(BF16)
                place += columns

        @pl.when(step < half)
        def _():
            fill(send)

        @pl.when(step >= half)
        def _():
            fill(keep)

    shape = jax.ShapeDtypeStruct((half, width, total), BF16)
    return pl.pallas_call(
        kernel,
        grid_spec=pltpu.PrefetchScalarGridSpec(
            num_scalar_prefetch=1,
            grid=(blocks,),
            in_specs=[left_spec(left, c) for left, c in zip(lefts, part_of)]
            + [right_spec(right, t) for right, t in zip(rights, entry_of)],
            out_specs=[
                pl.BlockSpec((None, width, total), lambda j, m: (jnp.minimum(j, half - 1), 0, 0)),
                pl.BlockSpec((None, width, total), lambda j, m: (jnp.maximum(j - half, 0), 0, 0)),
            ],
        ),
        out_shape=[shape, shape],
        compiler_params=pltpu.CompilerParams(vmem_limit_bytes=VMEM),
        cost_estimate=cost(2**20),
    )(me, *lefts, *rights)


def normed_back_kernel(dq, dk, dv, wq, wk, wv, x, terms, gain_sum, bias_sum):
    total = times_trans(dq[...], wq[...]) + times_trans(dk[...], wk[...])
    total = total + times_trans(dv[...], wv[...])
    terms[...] = total.astype(BF16)
    values = x[...].astype(F32)
    centred = values - jnp.mean(values, axis=-1, keepdims=True)
    inverse = lax.rsqrt(jnp.mean(centred * centred, axis=-1, keepdims=True) + EPSILON)

    @pl.when(pl.program_id(0) == 0)
    def _():
        gain_sum[...] = jnp.zeros_like(gain_sum)
        bias_sum[...] = jnp.zeros_like(bias_sum)

    gain_sum[...] += jnp.sum(total * (centred * inverse), axis=0, keepdims=True)
    bias_sum[...] += jnp.sum(total, axis=0, keepdims=True)


def normed_back(dq, dk, dv, wq, wk, wv, x):
    rows, width = x.shape
    size = min(512, rows)
    thin = pl.BlockSpec((size, dq.shape[1]), lambda i: (i, 0))
    tall = pl.BlockSpec((size, width), lambda i: (i, 0))
    line = pl.BlockSpec((1, width), lambda i: (0, 0))
    return pl.pallas_call(
        normed_back_kernel,
        grid=(rows // size,),
        in_specs=[thin] * 3 + [whole_spec(w) for w in (wq, wk, wv)] + [tall],
        out_specs=[tall, line, line],
        out_shape=[
            jax.ShapeDtypeStruct((rows, width), BF16),
            jax.ShapeDtypeStruct((1, width), F32),
            jax.ShapeDtypeStruct((1, width), F32),
        ],
        compiler_params=pltpu.CompilerParams(vmem_limit_bytes=VMEM),
        cost_estimate=cost(6 * rows * width * dq.shape[1]),
    )(dq, dk, dv, wq, wk, wv, x)


def input_back(d_normed, x, d_mid, gain):
    rows, width = x.shape
    size = min(128, rows)

    def kernel(terms, x_ref, mid, gain_ref, out):
        values = x_ref[...].astype(F32)
        centred = values - jnp.mean(values, axis=-1, keepdims=True)
        inverse = lax.rsqrt(jnp.mean(centred * centred, axis=-1, keepdims=True) + EPSILON)
        back = norm_back(terms[...].astype(F32), gain_ref[...], centred * inverse, inverse)
        out[...] = mid[...] + back

    tall = pl.BlockSpec((size, width), lambda i: (i, 0))
    return pl.pallas_call(
        kernel,
        grid=(rows // size,),
        in_specs=[tall, tall, tall, pl.BlockSpec((1, width), lambda i: (0, 0))],
        out_specs=tall,
        out_shape=jax.ShapeDtypeStruct((rows, width), F32),
        compiler_params=pltpu.CompilerParams(vmem_limit_bytes=VMEM),
        cost_estimate=cost(2**20),
    )(d_normed, x, d_mid, gain.reshape(1, -1))


def both_parts(lefts, weight, transposed, columns, groups=None):
    block = min(512, columns)
    part_of = [left[1] if isinstance(left, tuple) else None for left in lefts]
    lefts = [left[0] if isinstance(left, tuple) else left for left in lefts]
    depth = lefts[0].shape[-1]
    rows = lefts[0].shape[0] * (1 if part_of[0] is None else lefts[0].shape[2])

    def kernel(*refs):
        weight_ref, out = refs[-2:]
        for c in range(len(lefts)):
            left = refs[c][...].reshape(-1, depth)
            product = times_trans if transposed else mm
            value = product(left, weight_ref[...]).astype(BF16)
            if groups is None:
                out[c] = value
            else:
                out[:, c] = value.reshape(groups, rows // groups, block)

    def left_spec(left, c):
        if c is None:
            return whole_spec(left)
        return pl.BlockSpec((left.shape[0], None) + left.shape[2:], lambda j: (0, c, 0, 0))

    shape = (len(lefts), rows)
    if groups is not None:
        shape = (groups, len(lefts), rows // groups)
    if transposed:
        weight_spec = pl.BlockSpec((block, depth), lambda j: (j, 0))
    else:
        weight_spec = pl.BlockSpec((depth, block), lambda j: (0, j))
    return pl.pallas_call(
        kernel,
        grid=(columns // block,),
        in_specs=[left_spec(left, c) for left, c in zip(lefts, part_of)] + [weight_spec],
        out_specs=pl.BlockSpec(shape + (block,), lambda j: (0,) * len(shape) + (j,)),
        out_shape=jax.ShapeDtypeStruct(shape + (columns,), BF16),
        compiler_params=pltpu.CompilerParams(vmem_limit_bytes=VMEM),
        cost_estimate=cost(2 * len(lefts) * rows * depth * columns),
    )(*lefts, weight)


def swap_bit(values, axis, bit):
    size = lax.axis_size(axis)
    return lax.ppermute(values, axis, [(i, i ^ (1 << bit)) for i in range(size)])


def third(k, steps):
    return range((k - 1) * steps // 3 + 1, k * steps // 3 + 1)


def fence(things, arrays=()):
    lists = [thing.live for thing in things]
    flat = lax.optimization_barrier(tuple(v for values in lists for v in values) + tuple(arrays))
    place = 0
    for thing, values in zip(things, lists):
        thing.live = list(flat[place : place + len(values)])
        place += len(values)
    return flat[place:]


def exchange(values):
    return lax.all_to_all(values, "tensor", 0, 0)


def add_and_split(sources, outs, dims):
    places = 2**dims
    rows = sources[0][0].shape[1]
    size = min(128, rows)
    widths = [sum(stop - start for _, start, stop in picks) for picks, _ in outs]

    def kernel(*refs):
        target = 2 * len(sources)
        for picks, dim in outs:
            shift = dims - 1 - dim
            for half in range(2):
                chosen = [p for p in range(places) if (p >> shift) & 1 == half]
                at = 0
                for source, start, stop in picks:
                    keep, got = refs[2 * source : 2 * source + 2]
                    for q, p in enumerate(chosen):
                        value = keep[p, :, start:stop].astype(F32) + got[p, :, start:stop].astype(F32)
                        refs[target][q, :, at : at + stop - start] = value.astype(BF16)
                    at += stop - start
                target += 1

    def block(count, columns):
        return pl.BlockSpec((count, size, columns), lambda i: (0, i, 0))

    flat = [v for pair in sources for v in pair]
    return pl.pallas_call(
        kernel,
        grid=(rows // size,),
        in_specs=[block(places, v.shape[2]) for v in flat],
        out_specs=[block(places // 2, w) for w in widths for _ in range(2)],
        out_shape=[
            jax.ShapeDtypeStruct((places // 2, rows, w), BF16) for w in widths for _ in range(2)
        ],
        compiler_params=pltpu.CompilerParams(vmem_limit_bytes=VMEM),
        cost_estimate=cost(2**20),
    )(*flat)


def finish_sum(live, width, cuts, turned, kind):
    rows, columns = live[0].shape[1:]
    count = columns // width
    total = 2 * columns

    def kernel(*refs):
        sums = []
        for c in range(2 * count):
            keep, got = refs[2 * (c % 2) : 2 * (c % 2) + 2]
            place = slice(c // 2 * width, (c // 2 + 1) * width)
            sums.append(keep[0, :, place].astype(F32) + got[0, :, place].astype(F32))
        value = jnp.concatenate(sums, axis=1)
        if turned:
            refs[4][...] = value.T.astype(kind)
            return
        for k in range(cuts):
            refs[4 + k][...] = value[:, k * total // cuts : (k + 1) * total // cuts].astype(kind)

    size = rows if turned else min(64, rows)
    shape = (total, rows) if turned else (rows, total // cuts)
    block = (total, rows) if turned else (size, total // cuts)
    return pl.pallas_call(
        kernel,
        grid=(rows // size,),
        in_specs=[pl.BlockSpec((1, size, columns), lambda i: (0, i, 0))] * 4,
        out_specs=[pl.BlockSpec(block, lambda i: (i, 0) if not turned else (0, 0))] * cuts,
        out_shape=[jax.ShapeDtypeStruct(shape, kind)] * cuts,
        compiler_params=pltpu.CompilerParams(vmem_limit_bytes=VMEM),
        cost_estimate=cost(2**20),
    )(*live)


class DpSum:
    def __init__(self, send, keep, cuts):
        self.live = [send, keep]
        self.cuts = cuts
        self.rest = place_bits(lax.axis_size("dp")) - 1
        self.width = keep.shape[-1] // cuts
        self.left = [list(range(1, self.rest + 1)) for _ in range(2)]

    def core(self):
        self.live = [self.live[1], swap_bit(self.live[0], "dp", 0)]

    def dim(self, odd):
        return len(self.left[odd]) - 1 if odd else 0

    def split(self):
        outs = [
            ([(0, c * self.width, (c + 1) * self.width)], self.dim(c % 2)) for c in range(self.cuts)
        ]
        self.live = list(add_and_split([tuple(self.live)], outs, self.rest))

    def first(self, *cuts):
        for c in cuts:
            values = self.live[2 * c + 1]
            self.live[2 * c + 1] = swap_bit(values, "dp", self.left[c % 2][self.dim(c % 2)])

    def add(self):
        bits = [left[self.dim(odd)] for odd, left in enumerate(self.left)]
        for odd in range(2):
            self.left[odd].remove(bits[odd])
        count = len(self.live) // 2
        sources = [(self.live[2 * k], self.live[2 * k + 1]) for k in range(count)]
        outs = [
            ([(k, 0, sources[k][0].shape[2]) for k in range(odd, count, 2)], self.dim(odd))
            for odd in range(2)
        ]
        self.live = list(add_and_split(sources, outs, len(self.left[0])))

    def send(self):
        for odd in range(2):
            bit = self.left[odd][self.dim(odd)]
            self.live[2 * odd + 1] = swap_bit(self.live[2 * odd + 1], "dp", bit)
        while len(self.left[0]) > 1:
            self.add()
            self.send()

    def total(self, cuts=1, turned=False, kind=F32):
        return finish_sum(self.live, self.width, cuts, turned, kind)


class WeightGather:
    def __init__(self, own, me):
        self.blocks = lax.axis_size("dp")
        self.size = lax.axis_size("tensor")
        self.usual = (self.size, self.blocks) == (4, 8)
        self.me = me
        share = own.shape[1 if self.usual else 0] // self.blocks
        axis = 1 if self.usual else 0
        self.live = [lax.dynamic_slice_in_dim(own, me[0] * share, share, axis)]

    def advance(self, k):
        if not self.usual:
            if k == 0:
                self.live = [lax.all_gather(self.live[0], ("tensor", "dp"), axis=0, tiled=True)]
            return
        if k == 0:
            own = self.live[0]
            self.live += [
                lax.ppermute(own, "tensor", [(i, (i + m) % self.size) for i in range(self.size)])
                for m in range(1, self.size)
            ]
        elif k == 1:
            own, one, two, three = self.live
            even = lax.axis_index("tensor") % 2 == 0
            near = jnp.concatenate([jnp.where(even, own, one), jnp.where(even, three, own)])
            far = jnp.concatenate([jnp.where(even, two, three), jnp.where(even, one, two)])
            self.live = [near, swap_bit(near, "dp", 1), far, swap_bit(far, "dp", 2)]
            self.live += [swap_bit(near, "dp", 0), swap_bit(far, "dp", 0)]
        elif k == 2:
            near, near_one, far, far_one, near_core, far_core = self.live
            near, far = jnp.stack([near, near_one]), jnp.stack([far, far_one])
            self.live = [near, far, near_core[None], far_core[None]]
            self.live += [swap_bit(near, "dp", 2), swap_bit(far, "dp", 1)]
            self.live += [swap_bit(near_one, "dp", 0)[None], swap_bit(far_one, "dp", 0)[None]]
        elif k == 3:
            near, far, near_core, far_core, near_two, far_two, near_one_core, far_one_core = self.live
            own = [(near, 0), (near, 1), (far, 0), (far, 1)]
            other = [(v, 0) for v in (near_core, near_one_core, far_core, far_one_core)]
            self.live = [near_two, far_two, self.place(own, other, 0, None)]
        else:
            near_two, far_two, half = self.live
            self.live = [near_two, swap_bit(near_two, "dp", 0)]
            self.live += [far_two, swap_bit(far_two, "dp", 0), half]

    def place(self, own, other, late, half):
        rows, width = own[0][0].shape[1:]
        blocks = own + other

        def kernel(me_ref, *refs):
            out = refs[-1]
            step, odd = pl.program_id(0), me_ref[0] & 1
            for k in range(4):
                for flip in range(2):

                    @pl.when((step == k) & (odd == flip))
                    def _():
                        out[:, flip * width : (flip + 1) * width] = refs[k][...]
                        out[:, (1 - flip) * width : (2 - flip) * width] = refs[k + 4][...]

        def source(entry):
            return pl.BlockSpec((None, rows, width), lambda s, m: (entry, 0, 0))

        def target(s, m):
            top, one = s < 2, s & 1
            low = jnp.where(top, 2 * one + 4 * late, 4 * one + 2 * late)
            return (jnp.where(top, m[2], 1 - m[2]), (low ^ m[0]) >> 1)

        more = [] if half is None else [half]
        return pl.pallas_call(
            kernel,
            grid_spec=pltpu.PrefetchScalarGridSpec(
                num_scalar_prefetch=1,
                grid=(4,),
                in_specs=[source(entry) for _, entry in blocks]
                + [pl.BlockSpec(memory_space=pl.ANY)] * len(more),
                out_specs=pl.BlockSpec((rows, 2 * width), target),
            ),
            out_shape=jax.ShapeDtypeStruct((2 * rows, 8 * width), BF16),
            input_output_aliases={9: 0} if more else {},
            compiler_params=pltpu.CompilerParams(vmem_limit_bytes=VMEM),
            cost_estimate=cost(2**20),
        )(self.me, *[array for array, _ in blocks], *more)

    def whole(self):
        if not self.usual:
            return self.live[0]
        near, near_core, far, far_core, half = self.live
        own = [(near, 0), (near, 1), (far, 0), (far, 1)]
        other = [(near_core, 0), (near_core, 1), (far_core, 0), (far_core, 1)]
        return self.place(own, other, 1, half)


class SmallSum:
    def __init__(self, vectors, me):
        self.vectors = vectors
        self.blocks = blocks = lax.axis_size("dp")
        self.bits = place_bits(blocks)
        places = jnp.stack([xor_source(p, me, self.bits) for p in range(blocks)]).reshape(-1)
        self.ordered = sorted(range(len(vectors)), key=lambda i: not vectors[i][1])
        wide = [vectors[i][0].reshape(blocks, -1) for i in self.ordered]
        wide = jnp.take(jnp.concatenate(wide, axis=1), places, axis=0)
        self.live = [wide.reshape((2,) * self.bits + wide.shape[1:])]

    def move(self):
        self.steps = getattr(self, "steps", 0) + 1
        while self.live[0].ndim > 1:
            values = self.live[0]
            self.live = [values[0] + swap_bit(values[1], "dp", self.bits - values.ndim + 1)]
            if self.steps < 3:
                return

    def tensor(self):
        values = self.live[0]
        both = sum(v[0].shape[0] // self.blocks for v in self.vectors if v[1])
        summed, alone = values[..., :both], values[..., both:]
        for bit in range(place_bits(lax.axis_size("tensor"))):
            summed = summed + swap_bit(summed, "tensor", bit)
        self.live = [jnp.concatenate([summed, alone], axis=-1)]

    def total(self):
        out, start = [None] * len(self.vectors), 0
        for i in self.ordered:
            size = self.vectors[i][0].shape[0] // self.blocks
            out[i] = self.live[0][start : start + size]
            start += size
        return out


def on_device(
    inputs,
    segments,
    cotangent,
    norm1_gain,
    norm1_bias,
    query_weight,
    query_bias,
    key_weight,
    value_weight,
    value_bias,
    output_weight,
    output_bias,
    norm2_gain,
    norm2_bias,
    up_weight,
    up_bias,
    down_weight,
    down_bias,
):
    groups = lax.axis_size("tensor")
    blocks = lax.axis_size("dp")
    here = lax.axis_index("tensor").astype(jnp.int32)
    side = here // (groups // 2)
    me = lax.axis_index("dp").astype(jnp.int32)
    me = jnp.stack([me, here, side])
    rows, width = inputs.shape
    share = rows // groups
    part = share // PARTS
    local = query_weight.shape[1]
    size = width // blocks

    def by_part(values):
        return values.reshape(groups, PARTS, part, values.shape[1])

    def own(values):
        return lax.dynamic_slice_in_dim(values, here * share, share, 0)

    weight = WeightGather(output_weight, me)
    weight.advance(0)
    normed, query, key, value = project(
        inputs,
        norm1_gain,
        norm1_bias,
        query_weight,
        query_bias,
        key_weight,
        value_weight,
        value_bias,
    )
    heads = [None] * PARTS
    heads[0] = attend(0, segments, query, key, value, groups)
    cot, heads[0], query, key, value = fence([weight], (cotangent, heads[0], query, key, value))

    heads[0] = lax.all_gather(heads[0].reshape(groups * part, local), "tensor", axis=0)
    weight.advance(1)
    heads[1] = attend(1, segments, query, key, value, groups)
    cot, heads[1] = fence([weight], (cot, heads[1]))
    heads[1] = lax.all_gather(heads[1].reshape(groups * part, local), "tensor", axis=0)
    weight.advance(2)
    cot_parts = by_part(cot)
    cots = [(cot_parts, c) for c in range(PARTS)]
    d_hidden = both_parts(cots, down_weight, True, down_weight.shape[0])
    d_hidden, cot = fence([], (d_hidden, cot))
    weight.advance(3)
    d_hidden, cot = fence([weight], (d_hidden, cot))
    weight.advance(4)
    fence([weight])
    whole = weight.whole()
    whole, heads[0] = fence([], (whole, heads[0]))

    own_mid, low, hidden, d_up, terms = ([None] * PARTS for _ in range(5))

    def middle(c):
        own_mid[c], low[c], hidden[c], d_up[c], *term = middle_call(
            1,
            c,
            me,
            heads[c],
            whole,
            by_part(inputs),
            output_bias,
            norm2_gain,
            norm2_bias,
            up_weight,
            up_bias,
            d_hidden,
        )
        terms[c] = term[0].reshape(groups, part, width)

    middle(0)
    terms[0], heads[1] = fence([], (terms[0], heads[1]))

    terms[0] = lax.psum_scatter(terms[0], "tensor", scatter_dimension=0)
    middle(1)
    cot_own = own(cot)
    terms[1], cot_own, low[0], low[1], d_up[0], d_up[1] = fence(
        [], (terms[1], cot_own, *low, *d_up)
    )

    terms[1] = lax.psum_scatter(terms[1], "tensor", scatter_dimension=0)
    up_terms = gradient_terms(low, [d_up], me, blocks)
    d_mids, d_branches, sums = ([None] * PARTS for _ in range(3))

    def back(c):
        d_mids[c], d_branches[c], sums[c], d_att = middle_back(
            terms[c], own_mid[c], cot_own[c * part : (c + 1) * part], norm2_gain, whole
        )
        return d_att

    terms[0], hidden[0], hidden[1], *up_terms = fence([], (terms[0], *hidden, *up_terms))
    d_att = back(0)
    d_att, hidden[0], hidden[1] = fence([], (d_att, *hidden))
    out_terms = both_parts(hidden, down_weight, False, width, groups)
    out_terms, hidden[0], hidden[1] = fence([], (out_terms, *hidden))
    down_terms = gradient_terms(cots, [hidden], me, blocks)
    d_att, *down_terms = fence([], (d_att, *down_terms))
    got = [exchange(d_att), None]
    cot_sum = column_sums(cot)
    up_bias_sum = column_sums(d_up[0]) + column_sums(d_up[1])
    up_sum = DpSum(*up_terms, 2)
    down_sum = DpSum(*down_terms, 4)
    terms[1], out_terms, d_branches[0], cot_sum, up_bias_sum = fence(
        [up_sum, down_sum], (terms[1], out_terms, d_branches[0], cot_sum, up_bias_sum)
    )

    d_att = back(1)
    d_att, got[0], *d_branches = fence([up_sum, down_sum], (d_att, got[0], *d_branches))
    got[1] = exchange(d_att)
    up_sum.core()
    down_sum.core()
    views = [h.reshape(groups, groups, part, local) for h in heads]
    wo_terms = gradient_terms(d_branches, [[(v, t) for v in views] for t in range(groups)], me, blocks)
    wo_sum = DpSum(*wo_terms, 2)
    got[1], out_terms = fence([wo_sum, up_sum, down_sum], (got[1], out_terms))

    out_sum = lax.psum_scatter(out_terms, "tensor", scatter_dimension=0)
    up_sum.split()
    up_sum.first(0, 1)
    wo_sum.core()
    d_query, d_key, d_value = attend_back(segments, query, key, value, got)
    wo_sum.split()
    d_query, d_key, d_value = fence([up_sum, wo_sum, down_sum], (d_query, d_key, d_value))
    wo_sum.first(0, 1)
    qkv_sum = DpSum(
        *gradient_terms([normed], [[d] for d in (d_query, d_key, d_value)], me, blocks), 2
    )
    down_sum.split()
    d_query, d_key, d_value = fence([wo_sum, qkv_sum, down_sum], (d_query, d_key, d_value))
    qkv_sum.core()
    down_sum.first(0, 3)
    terms_in, gain1, bias1 = normed_back(
        d_query, d_key, d_value, query_weight, key_weight, value_weight, inputs
    )
    gain1, bias1, terms_in, d_query, d_value = fence(
        [qkv_sum, wo_sum, down_sum], (gain1, bias1, terms_in, d_query, d_value)
    )

    d_normed = lax.psum_scatter(
        terms_in.reshape(groups, share, width), "tensor", scatter_dimension=0
    )
    down_sum.first(1, 2)
    qkv_sum.split()
    wo_sum.add()
    gain1, bias1, d_query, d_value = fence(
        [qkv_sum, wo_sum, down_sum], (gain1, bias1, d_query, d_value)
    )
    qkv_sum.first(0, 1)
    wo_sum.send()
    two = sums[0] + sums[1]
    small = SmallSum(
        [
            (gain1[0], True),
            (bias1[0], True),
            (two[0], True),
            (two[1], True),
            (two[2], True),
            (cot_sum, False),
            (column_sums(d_query), False),
            (column_sums(d_value), False),
            (up_bias_sum, False),
        ],
        me[:1],
    )
    small.tensor()
    down_sum.add()
    out_sum, *_ = fence([qkv_sum, wo_sum, down_sum, small, up_sum], (out_sum,))
    down_sum.send()
    qkv_sum.add()
    qkv_sum.send()
    small.move()
    small.move()
    small.move()
    wo_terms = wo_sum.total(turned=True, kind=BF16)[0].reshape(groups, local, size)
    to_all = [
        lax.dynamic_index_in_dim(wo_terms, (here - m) % groups, 0, keepdims=False)
        for m in range(groups)
    ]
    up_sum.add()
    out_sum, *to_all = fence([qkv_sum, small, down_sum, up_sum], (out_sum, *to_all))
    wo_got = [to_all[0]]
    for m in range(1, groups):
        ring = [(i, (i - m) % groups) for i in range(groups)]
        wo_got.append(lax.ppermute(to_all[m], "tensor", ring))
    up_sum.send()
    total = [own_mid[c] + (out_sum[c].astype(F32) + down_bias) for c in range(PARTS)]
    output = jnp.concatenate([t.astype(BF16) for t in total], axis=0)
    qkv_grads = qkv_sum.total(3)
    (up_weight_grad,) = up_sum.total()
    (down_weight_grad,) = down_sum.total(turned=True)
    d_mid = jnp.concatenate(d_mids, axis=0)
    rows_own = own(inputs)
    small_sums = small.total()
    up_weight_grad, down_weight_grad, output, d_mid, rows_own, *others = fence(
        [],
        (up_weight_grad, down_weight_grad, output, d_mid, rows_own, *qkv_grads, *small_sums),
    )
    qkv_grads, small_sums = others[:3], others[3:]
    input_grad = input_back(d_normed, rows_own, d_mid, norm1_gain)
    input_grad, *wo_got = fence([], (input_grad, *wo_got))
    output_weight_grad = sum(g.astype(F32) for g in wo_got)
    (
        norm1_gain_grad,
        norm1_bias_grad,
        norm2_gain_grad,
        norm2_bias_grad,
        output_bias_grad,
        down_bias_grad,
        query_bias_grad,
        value_bias_grad,
        up_bias_grad,
    ) = small_sums
    return (
        output,
        input_grad,
        norm1_gain_grad,
        norm1_bias_grad,
        qkv_grads[0],
        query_bias_grad,
        qkv_grads[1],
        qkv_grads[2],
        value_bias_grad,
        output_weight_grad,
        output_bias_grad,
        norm2_gain_grad,
        norm2_bias_grad,
        up_weight_grad,
        up_bias_grad,
        down_weight_grad,
        down_bias_grad,
    )


def solution(mesh):
    return jax.shard_map(
        on_device,
        mesh=mesh,
        in_specs=(
            P("dp", None),
            P("dp", None),
            P("dp", None),
            P(),
            P(),
            P(None, "tensor"),
            P("tensor"),
            P(None, "tensor"),
            P(None, "tensor"),
            P("tensor"),
            P("tensor", None),
            P(),
            P(),
            P(),
            P(None, "tensor"),
            P("tensor"),
            P("tensor", None),
            P(),
        ),
        out_specs=(
            P(("dp", "tensor"), None),
            P(("dp", "tensor"), None),
            P("dp"),
            P("dp"),
            P("dp", "tensor"),
            P(("tensor", "dp")),
            P("dp", "tensor"),
            P("dp", "tensor"),
            P(("tensor", "dp")),
            P("tensor", "dp"),
            P("dp"),
            P("dp"),
            P("dp"),
            P("dp", "tensor"),
            P(("tensor", "dp")),
            P("tensor", "dp"),
            P("dp"),
        ),
        check_vma=False,
    )
```

```python
import functools

import jax
import jax.numpy as jnp
from jax import lax
from jax.experimental import pallas as pl
from jax.experimental.pallas import tpu as pltpu
from jax.sharding import PartitionSpec as P

HEAD_DIM = 128
LONGEST = 512
EPSILON = 1e-05
MASKED_SCORE = -1e30
SCALING = HEAD_DIM ** (-0.5)
F32 = jnp.float32
BF16 = jnp.bfloat16
PARTS = 2
COST = 0
VMEM = 60 * 2**20


def mm(left_side, right_side):
    return lax.dot_general(
        left_side, right_side, (((1,), (0,)), ((), ())), preferred_element_type=F32
    )


def times_trans(left_side, right_side):
    return lax.dot_general(
        left_side, right_side, (((1,), (1,)), ((), ())), preferred_element_type=F32
    )


def trans_times(left_side, right_side):
    return lax.dot_general(
        left_side, right_side, (((0,), (0,)), ((), ())), preferred_element_type=F32
    )


def column_sums(values):
    return jnp.sum(values.astype(F32), axis=0)


def row_stats(rows):
    average = jnp.mean(rows, axis=-1, keepdims=True)
    centred = rows - average
    spread = jnp.mean(centred * centred, axis=-1, keepdims=True)
    return average, lax.rsqrt(spread + EPSILON)


def norm_back(d_normed, gain, xhat, inverse):
    scaled = d_normed * gain
    first = jnp.mean(scaled, axis=-1, keepdims=True)
    second = jnp.mean(scaled * xhat, axis=-1, keepdims=True)
    return inverse * (scaled - first - xhat * second)


def cost(flops):
    return pl.CostEstimate(flops=COST and flops, bytes_accessed=2**10, transcendentals=0)


def key_start(first):
    return max(0, (first - (LONGEST - 1)) // 256 * 256)


def segment_column(seg_row):
    length = seg_row.shape[1]
    return jnp.broadcast_to(seg_row[...], (128, length)).T[:, :1]


def probabilities(seg_row, seg_col, query, keys, first, last):
    low, high = key_start(first), last
    scores = times_trans(keys[low:high, :], query)
    shape = (high - low, last - first)
    key_place = lax.broadcasted_iota(jnp.int32, shape, 0) + low
    query_place = lax.broadcasted_iota(jnp.int32, shape, 1) + first
    same = seg_col[low:high, :] == seg_row[:, first:last]
    scores = jnp.where(same & (key_place <= query_place), scores, MASKED_SCORE)
    weights = jnp.exp(scores - jnp.max(scores, axis=0, keepdims=True))
    return weights * (1.0 / jnp.sum(weights, axis=0, keepdims=True))


def forward_kernel(c, seg_row, query, key, value, out):
    groups, part = out.shape[:2]
    seg_col = segment_column(seg_row)
    for t in range(groups):
        first = (t * PARTS + c) * part
        last = first + part
        low = key_start(first)
        probs = probabilities(seg_row, seg_col, query[first:last, :], key, first, last)
        out[t] = trans_times(probs.astype(BF16), value[low:last, :]).astype(BF16)


def backward_kernel(size, seg_row, query, key, value, *refs):
    got = refs[:PARTS]
    d_query, d_key, d_value, d_attended, key_sum, value_sum = refs[PARTS:]
    groups, part = got[0].shape[:2]
    for t in range(groups):
        for c in range(PARTS):
            start = (t * PARTS + c) * part
            d_attended[start : start + part, :] = got[c][t]
    seg_col = segment_column(seg_row)
    key_sum[...] = jnp.zeros_like(key_sum)
    value_sum[...] = jnp.zeros_like(value_sum)
    for block in range(query.shape[0] // size):
        low, high = key_start(block * size), (block + 1) * size
        rows = slice(block * size, high)
        probs = probabilities(seg_row, seg_col, query[rows, :], key, block * size, high)
        value_sum[low:high, :] += mm(probs.astype(BF16), d_attended[rows, :])
        d_probs = times_trans(value[low:high, :], d_attended[rows, :])
        inner = jnp.sum(probs * d_probs, axis=0, keepdims=True)
        d_scores = (probs * (d_probs - inner)).astype(BF16)
        d_query[rows, :] = (trans_times(d_scores, key[low:high, :]) * SCALING).astype(BF16)
        key_sum[low:high, :] += mm(d_scores, query[rows, :])
    d_key[...] = key_sum[...].astype(BF16)
    d_value[...] = value_sum[...].astype(BF16)


def attend(c, segments, query, key, value, groups):
    length, local = query.shape
    part = length // groups // PARTS
    tall = pl.BlockSpec((length, HEAD_DIM), lambda h: (0, h))
    return pl.pallas_call(
        functools.partial(forward_kernel, c),
        grid=(local // HEAD_DIM,),
        in_specs=[pl.BlockSpec((1, length), lambda h: (0, 0))] + [tall] * 3,
        out_specs=pl.BlockSpec((groups, part, HEAD_DIM), lambda h: (0, 0, h)),
        out_shape=jax.ShapeDtypeStruct((groups, part, local), BF16),
        compiler_params=pltpu.CompilerParams(vmem_limit_bytes=VMEM),
        cost_estimate=cost(2**20),
    )(segments, query, key, value)


def attend_back(segments, query, key, value, got):
    length = query.shape[0]
    tall = pl.BlockSpec((length, HEAD_DIM), lambda h: (0, h))
    return pl.pallas_call(
        functools.partial(backward_kernel, min(256, length)),
        grid=(query.shape[1] // HEAD_DIM,),
        in_specs=[pl.BlockSpec((1, length), lambda h: (0, 0))]
        + [tall] * 3
        + [pl.BlockSpec(g.shape[:2] + (HEAD_DIM,), lambda h: (0, 0, h)) for g in got],
        out_specs=[tall] * 3,
        scratch_shapes=[
            pltpu.VMEM((length, HEAD_DIM), BF16),
            pltpu.VMEM((length, HEAD_DIM), F32),
            pltpu.VMEM((length, HEAD_DIM), F32),
        ],
        out_shape=[jax.ShapeDtypeStruct(query.shape, BF16)] * 3,
        compiler_params=pltpu.CompilerParams(vmem_limit_bytes=VMEM),
        cost_estimate=cost(10 * query.shape[0] * length * query.shape[1]),
    )(segments, query, key, value, *got)


def place_bits(blocks):
    return blocks.bit_length() - 1


def xor_source(place, me, bits):
    distance = 0
    for bit in range(bits):
        distance = distance + (((place >> (bits - 1 - bit)) & 1) << bit)
    return distance ^ me


def norm_rows(values, gain, bias):
    average = jnp.mean(values, axis=-1, keepdims=True)
    centred = values - average
    inverse = lax.rsqrt(jnp.mean(centred * centred, axis=-1, keepdims=True) + EPSILON)
    return centred * inverse * gain + bias


def project_kernel(x, gain, bias, wq, bq, wk, wv, bv, normed, query, key, value):
    low = norm_rows(x[...].astype(F32), gain[...], bias[...]).astype(BF16)
    normed[...] = low
    query[...] = ((mm(low, wq[...]) + bq[...]) * SCALING).astype(BF16)
    key[...] = mm(low, wk[...]).astype(BF16)
    value[...] = (mm(low, wv[...]) + bv[...]).astype(BF16)


def whole_spec(array):
    return pl.BlockSpec(array.shape, lambda *_: (0,) * array.ndim)


def project(x, gain, bias, wq, bq, wk, wv, bv):
    rows, width = x.shape
    local = wq.shape[1]
    size = min(512, rows)
    args = [x] + [v.reshape(1, -1) if v.ndim == 1 else v for v in (gain, bias, wq, bq, wk, wv, bv)]
    tall = pl.BlockSpec((size, width), lambda i: (i, 0))
    thin = pl.BlockSpec((size, local), lambda i: (i, 0))
    shape = jax.ShapeDtypeStruct((rows, local), BF16)
    return pl.pallas_call(
        project_kernel,
        grid=(rows // size,),
        in_specs=[tall] + [whole_spec(a) for a in args[1:]],
        out_specs=[tall] + [thin] * 3,
        out_shape=[jax.ShapeDtypeStruct(x.shape, BF16)] + [shape] * 3,
        compiler_params=pltpu.CompilerParams(vmem_limit_bytes=VMEM),
        cost_estimate=cost(6 * rows * width * local),
    )(*args)


def middle_kernel(
    steps, here_ref, heads, wo, x, bo, gain, bias, wup, bup, d_hid, wup_rows,
    own_mid, low_out, hidden, d_up, *rest,
):
    first, second = steps
    *terms, mid, low, d_low = rest
    step = pl.program_id(0)
    block = wo.shape[1]
    here = here_ref[1]
    local = heads.shape[2]

    @pl.when(step == 0)
    def _():
        for t in range(heads.shape[0]):
            low[:, t * local : (t + 1) * local] = heads[t]

    @pl.when(step < first)
    def _():
        branch = mm(low[...], wo[...])
        values = x[...].reshape(branch.shape).astype(F32)
        columns = pl.ds(pl.multiple_of(step * block, block), block)
        mid[:, columns] = values + (branch + bo[...])

    @pl.when(step == first)
    def _():
        low[...] = norm_rows(mid[...], gain[...], bias[...]).astype(BF16)
        part = own_mid.shape[0]
        own_mid[...] = mid[pl.ds(pl.multiple_of(here * part, part), part), :]

    @pl.when((step >= first) & (step < first + second))
    def _():
        piece = 256
        for start in range(0, wup.shape[1], piece):
            columns = slice(start, start + piece)
            up_value = mm(low[...], wup[:, columns]) + bup[:, columns]
            below = 0.5 + 0.5 * lax.erf(up_value * (0.5**0.5))
            density = jnp.exp(-0.5 * up_value * up_value) * 0.3989422804014327
            hidden[:, columns] = (up_value * below).astype(BF16)
            slope = ((below + up_value * density) * d_hid[:, columns].astype(F32)).astype(BF16)
            d_up[:, columns] = slope
            place = pl.multiple_of((step - first) * wup.shape[1] + start, piece)
            d_low[:, pl.ds(place, piece)] = slope

    @pl.when(step >= first + second)
    def _():
        value = times_trans(d_low[...], wup_rows[...]).astype(BF16)

        for k, term in enumerate(terms):
            start = first + second + k * first // len(terms)

            @pl.when((step >= start) & (step < start + first // len(terms)))
            def _():
                term[...] = value

        columns = pl.ds(pl.multiple_of((step - first - second) * block, block), block)
        low_out[...] = low[:, columns]


def middle_call(split, c, here, heads, wo, x, bo, gain, bias, wup, bup, d_hid):
    groups, _, part, width = x.shape
    rows = groups * part
    hidden = wup.shape[1]
    block = 512
    first, second = width // block, hidden // block
    bo, gain, bias, bup = (v.reshape(1, -1) for v in (bo, gain, bias, bup))

    def at(index, low, count):
        return jnp.clip(index - low, 0, count - 1)

    def columns(tall, low, count):
        return pl.BlockSpec((tall, block), lambda i, h: (0, at(i, low, count)))

    third = first + second
    return pl.pallas_call(
        functools.partial(middle_kernel, (first, second)),
        grid_spec=pltpu.PrefetchScalarGridSpec(
            num_scalar_prefetch=1,
            grid=(first + second + first,),
            in_specs=[
                whole_spec(heads),
                columns(width, 0, first),
                pl.BlockSpec(
                    (groups, None, part, block), lambda i, h: (0, c, 0, at(i, 0, first))
                ),
                columns(1, 0, first),
                whole_spec(gain),
                whole_spec(bias),
                columns(width, first, second),
                columns(1, first, second),
                pl.BlockSpec((None, rows, block), lambda i, h: (c, 0, at(i, first, second))),
                pl.BlockSpec((block, hidden), lambda i, h: (at(i, third, first), 0)),
            ],
            out_specs=[
                pl.BlockSpec((part, width), lambda i, h: (0, 0)),
                columns(rows, third, first),
                columns(rows, first, second),
                columns(rows, first, second),
            ]
            + [columns(rows, third + k * first // split, first // split) for k in range(split)],
            scratch_shapes=[
                pltpu.VMEM((rows, width), F32),
                pltpu.VMEM((rows, width), BF16),
                pltpu.VMEM((rows, hidden), BF16),
            ],
        ),
        out_shape=[
            jax.ShapeDtypeStruct((part, width), F32),
            jax.ShapeDtypeStruct((rows, width), BF16),
            jax.ShapeDtypeStruct((rows, hidden), BF16),
            jax.ShapeDtypeStruct((rows, hidden), BF16),
        ]
        + [jax.ShapeDtypeStruct((rows, width // split), BF16)] * split,
        compiler_params=pltpu.CompilerParams(vmem_limit_bytes=VMEM),
        cost_estimate=cost(2 * rows * width * (width + 2 * hidden)),
    )(here, heads, wo, x, bo, gain, bias, wup, bup, d_hid, wup)


def middle_back_kernel(terms, mid, cot, gain, wo, d_mid, d_branch, sums, d_att):

    @pl.when(pl.program_id(0) == 0)
    def _():
        d_normed = terms[...].astype(F32)
        values = mid[...]
        centred = values - jnp.mean(values, axis=-1, keepdims=True)
        inverse = lax.rsqrt(jnp.mean(centred * centred, axis=-1, keepdims=True) + EPSILON)
        xhat = centred * inverse
        total = cot[...].astype(F32) + norm_back(d_normed, gain[...], xhat, inverse)
        low = total.astype(BF16)
        d_mid[...] = total
        d_branch[...] = low
        sums[0:1, :] = jnp.sum(d_normed * xhat, axis=0, keepdims=True)
        sums[1:2, :] = jnp.sum(d_normed, axis=0, keepdims=True)
        sums[2:3, :] = jnp.sum(low.astype(F32), axis=0, keepdims=True)

    d_att[...] = times_trans(d_branch[...], wo[...]).astype(BF16)


def middle_back(terms, mid, cot, gain, wo):
    part, width = mid.shape
    groups = lax.axis_size("tensor")
    block = width // groups
    rows = pl.BlockSpec((part, width), lambda j: (0, 0))
    return pl.pallas_call(
        middle_back_kernel,
        grid=(groups,),
        in_specs=[
            rows,
            rows,
            rows,
            pl.BlockSpec((1, width), lambda j: (0, 0)),
            pl.BlockSpec((block, width), lambda j: (j, 0)),
        ],
        out_specs=[
            rows,
            rows,
            pl.BlockSpec((8, width), lambda j: (0, 0)),
            pl.BlockSpec((None, part, block), lambda j: (j, 0, 0)),
        ],
        out_shape=[
            jax.ShapeDtypeStruct((part, width), F32),
            jax.ShapeDtypeStruct((part, width), BF16),
            jax.ShapeDtypeStruct((8, width), F32),
            jax.ShapeDtypeStruct((groups, part, block), BF16),
        ],
        compiler_params=pltpu.CompilerParams(vmem_limit_bytes=VMEM),
        cost_estimate=cost(2 * part * width * width),
    )(terms, mid, cot, gain.reshape(1, -1), wo)


def gradient_terms(lefts, groups, me, blocks):
    half = blocks // 2
    bits = place_bits(blocks)
    part_of = [left[1] if isinstance(left, tuple) else None for left in lefts]
    lefts = [left[0] if isinstance(left, tuple) else left for left in lefts]
    count = len(lefts)
    rights = [right for group in groups for right in group]
    entry_of = [right[1] if isinstance(right, tuple) else None for right in rights]
    rights = [right[0] if isinstance(right, tuple) else right for right in rights]
    width = lefts[0].shape[-1] // blocks
    total = sum(right.shape[-1] for right in rights[::count])

    def source(j, m):
        return xor_source(jnp.where(j < half, j + half, j - half), m[0], bits)

    def right_spec(right, t):
        if t is None:
            return whole_spec(right)
        return pl.BlockSpec((None, None) + right.shape[2:], lambda j, m: (t, m[1], 0, 0))

    def left_spec(left, c):
        if c is None:
            return pl.BlockSpec((left.shape[0], width), lambda j, m: (0, source(j, m)))
        shape = (left.shape[0], None, left.shape[2], width)
        return pl.BlockSpec(shape, lambda j, m: (0, c, 0, source(j, m)))

    def kernel(me_ref, *refs):
        left_refs, right_refs = refs[:count], refs[count:]
        send, keep = refs[-2:]
        step = pl.program_id(0)

        def fill(target):
            place = 0
            turned = [ref[...].reshape(-1, width).T for ref in left_refs]
            for g in range(len(groups)):
                value = None
                for i in range(count):
                    more = mm(turned[i], right_refs[g * count + i][...])
                    value = more if value is None else value + more
                columns = value.shape[1]
                target[:, place : place + columns] = value.astype(BF16)
                place += columns

        @pl.when(step < half)
        def _():
            fill(send)

        @pl.when(step >= half)
        def _():
            fill(keep)

    shape = jax.ShapeDtypeStruct((half, width, total), BF16)
    return pl.pallas_call(
        kernel,
        grid_spec=pltpu.PrefetchScalarGridSpec(
            num_scalar_prefetch=1,
            grid=(blocks,),
            in_specs=[left_spec(left, c) for left, c in zip(lefts, part_of)]
            + [right_spec(right, t) for right, t in zip(rights, entry_of)],
            out_specs=[
                pl.BlockSpec((None, width, total), lambda j, m: (jnp.minimum(j, half - 1), 0, 0)),
                pl.BlockSpec((None, width, total), lambda j, m: (jnp.maximum(j - half, 0), 0, 0)),
            ],
        ),
        out_shape=[shape, shape],
        compiler_params=pltpu.CompilerParams(vmem_limit_bytes=VMEM),
        cost_estimate=cost(2**20),
    )(me, *lefts, *rights)


def normed_back_kernel(dq, dk, dv, wq, wk, wv, x, terms, gain_sum, bias_sum):
    total = times_trans(dq[...], wq[...]) + times_trans(dk[...], wk[...])
    total = total + times_trans(dv[...], wv[...])
    terms[...] = total.astype(BF16)
    values = x[...].astype(F32)
    centred = values - jnp.mean(values, axis=-1, keepdims=True)
    inverse = lax.rsqrt(jnp.mean(centred * centred, axis=-1, keepdims=True) + EPSILON)

    @pl.when(pl.program_id(0) == 0)
    def _():
        gain_sum[...] = jnp.zeros_like(gain_sum)
        bias_sum[...] = jnp.zeros_like(bias_sum)

    gain_sum[...] += jnp.sum(total * (centred * inverse), axis=0, keepdims=True)
    bias_sum[...] += jnp.sum(total, axis=0, keepdims=True)


def normed_back(dq, dk, dv, wq, wk, wv, x):
    rows, width = x.shape
    size = min(512, rows)
    thin = pl.BlockSpec((size, dq.shape[1]), lambda i: (i, 0))
    tall = pl.BlockSpec((size, width), lambda i: (i, 0))
    line = pl.BlockSpec((1, width), lambda i: (0, 0))
    return pl.pallas_call(
        normed_back_kernel,
        grid=(rows // size,),
        in_specs=[thin] * 3 + [whole_spec(w) for w in (wq, wk, wv)] + [tall],
        out_specs=[tall, line, line],
        out_shape=[
            jax.ShapeDtypeStruct((rows, width), BF16),
            jax.ShapeDtypeStruct((1, width), F32),
            jax.ShapeDtypeStruct((1, width), F32),
        ],
        compiler_params=pltpu.CompilerParams(vmem_limit_bytes=VMEM),
        cost_estimate=cost(6 * rows * width * dq.shape[1]),
    )(dq, dk, dv, wq, wk, wv, x)


def input_back(d_normed, x, d_mid, gain):
    rows, width = x.shape
    size = min(128, rows)

    def kernel(terms, x_ref, mid, gain_ref, out):
        values = x_ref[...].astype(F32)
        centred = values - jnp.mean(values, axis=-1, keepdims=True)
        inverse = lax.rsqrt(jnp.mean(centred * centred, axis=-1, keepdims=True) + EPSILON)
        back = norm_back(terms[...].astype(F32), gain_ref[...], centred * inverse, inverse)
        out[...] = mid[...] + back

    tall = pl.BlockSpec((size, width), lambda i: (i, 0))
    return pl.pallas_call(
        kernel,
        grid=(rows // size,),
        in_specs=[tall, tall, tall, pl.BlockSpec((1, width), lambda i: (0, 0))],
        out_specs=tall,
        out_shape=jax.ShapeDtypeStruct((rows, width), F32),
        compiler_params=pltpu.CompilerParams(vmem_limit_bytes=VMEM),
        cost_estimate=cost(2**20),
    )(d_normed, x, d_mid, gain.reshape(1, -1))


def both_parts(lefts, weight, transposed, columns, groups=None):
    block = min(512, columns)
    part_of = [left[1] if isinstance(left, tuple) else None for left in lefts]
    lefts = [left[0] if isinstance(left, tuple) else left for left in lefts]
    depth = lefts[0].shape[-1]
    rows = lefts[0].shape[0] * (1 if part_of[0] is None else lefts[0].shape[2])

    def kernel(*refs):
        weight_ref, out = refs[-2:]
        for c in range(len(lefts)):
            left = refs[c][...].reshape(-1, depth)
            product = times_trans if transposed else mm
            value = product(left, weight_ref[...]).astype(BF16)
            if groups is None:
                out[c] = value
            else:
                out[:, c] = value.reshape(groups, rows // groups, block)

    def left_spec(left, c):
        if c is None:
            return whole_spec(left)
        return pl.BlockSpec((left.shape[0], None) + left.shape[2:], lambda j: (0, c, 0, 0))

    shape = (len(lefts), rows)
    if groups is not None:
        shape = (groups, len(lefts), rows // groups)
    if transposed:
        weight_spec = pl.BlockSpec((block, depth), lambda j: (j, 0))
    else:
        weight_spec = pl.BlockSpec((depth, block), lambda j: (0, j))
    return pl.pallas_call(
        kernel,
        grid=(columns // block,),
        in_specs=[left_spec(left, c) for left, c in zip(lefts, part_of)] + [weight_spec],
        out_specs=pl.BlockSpec(shape + (block,), lambda j: (0,) * len(shape) + (j,)),
        out_shape=jax.ShapeDtypeStruct(shape + (columns,), BF16),
        compiler_params=pltpu.CompilerParams(vmem_limit_bytes=VMEM),
        cost_estimate=cost(2 * len(lefts) * rows * depth * columns),
    )(*lefts, weight)


def swap_bit(values, axis, bit):
    size = lax.axis_size(axis)
    return lax.ppermute(values, axis, [(i, i ^ (1 << bit)) for i in range(size)])


def third(k, steps):
    return range((k - 1) * steps // 3 + 1, k * steps // 3 + 1)


def fence(things, arrays=()):
    lists = [thing.live for thing in things]
    flat = lax.optimization_barrier(tuple(v for values in lists for v in values) + tuple(arrays))
    place = 0
    for thing, values in zip(things, lists):
        thing.live = list(flat[place : place + len(values)])
        place += len(values)
    return flat[place:]


def exchange(values):
    return lax.all_to_all(values, "tensor", 0, 0)


def add_and_split(sources, outs, dims):
    places = 2**dims
    rows = sources[0][0].shape[1]
    size = min(128, rows)
    widths = [sum(stop - start for _, start, stop in picks) for picks, _ in outs]

    def kernel(*refs):
        target = 2 * len(sources)
        for picks, dim in outs:
            shift = dims - 1 - dim
            for half in range(2):
                chosen = [p for p in range(places) if (p >> shift) & 1 == half]
                at = 0
                for source, start, stop in picks:
                    keep, got = refs[2 * source : 2 * source + 2]
                    for q, p in enumerate(chosen):
                        value = keep[p, :, start:stop].astype(F32) + got[p, :, start:stop].astype(F32)
                        refs[target][q, :, at : at + stop - start] = value.astype(BF16)
                    at += stop - start
                target += 1

    def block(count, columns):
        return pl.BlockSpec((count, size, columns), lambda i: (0, i, 0))

    flat = [v for pair in sources for v in pair]
    return pl.pallas_call(
        kernel,
        grid=(rows // size,),
        in_specs=[block(places, v.shape[2]) for v in flat],
        out_specs=[block(places // 2, w) for w in widths for _ in range(2)],
        out_shape=[
            jax.ShapeDtypeStruct((places // 2, rows, w), BF16) for w in widths for _ in range(2)
        ],
        compiler_params=pltpu.CompilerParams(vmem_limit_bytes=VMEM),
        cost_estimate=cost(2**20),
    )(*flat)


def finish_sum(live, width, cuts, turned, kind):
    rows, columns = live[0].shape[1:]
    count = columns // width
    total = 2 * columns

    def kernel(*refs):
        sums = []
        for c in range(2 * count):
            keep, got = refs[2 * (c % 2) : 2 * (c % 2) + 2]
            place = slice(c // 2 * width, (c // 2 + 1) * width)
            sums.append(keep[0, :, place].astype(F32) + got[0, :, place].astype(F32))
        value = jnp.concatenate(sums, axis=1)
        if turned:
            refs[4][...] = value.T.astype(kind)
            return
        for k in range(cuts):
            refs[4 + k][...] = value[:, k * total // cuts : (k + 1) * total // cuts].astype(kind)

    size = rows if turned else min(64, rows)
    shape = (total, rows) if turned else (rows, total // cuts)
    block = (total, rows) if turned else (size, total // cuts)
    return pl.pallas_call(
        kernel,
        grid=(rows // size,),
        in_specs=[pl.BlockSpec((1, size, columns), lambda i: (0, i, 0))] * 4,
        out_specs=[pl.BlockSpec(block, lambda i: (i, 0) if not turned else (0, 0))] * cuts,
        out_shape=[jax.ShapeDtypeStruct(shape, kind)] * cuts,
        compiler_params=pltpu.CompilerParams(vmem_limit_bytes=VMEM),
        cost_estimate=cost(2**20),
    )(*live)


class DpSum:
    def __init__(self, send, keep, cuts):
        self.live = [send, keep]
        self.cuts = cuts
        self.rest = place_bits(lax.axis_size("dp")) - 1
        self.width = keep.shape[-1] // cuts
        self.left = [list(range(1, self.rest + 1)) for _ in range(2)]

    def core(self):
        self.live = [self.live[1], swap_bit(self.live[0], "dp", 0)]

    def dim(self, odd):
        return len(self.left[odd]) - 1 if odd else 0

    def split(self):
        outs = [
            ([(0, c * self.width, (c + 1) * self.width)], self.dim(c % 2)) for c in range(self.cuts)
        ]
        self.live = list(add_and_split([tuple(self.live)], outs, self.rest))

    def first(self, *cuts):
        for c in cuts:
            values = self.live[2 * c + 1]
            self.live[2 * c + 1] = swap_bit(values, "dp", self.left[c % 2][self.dim(c % 2)])

    def add(self):
        bits = [left[self.dim(odd)] for odd, left in enumerate(self.left)]
        for odd in range(2):
            self.left[odd].remove(bits[odd])
        count = len(self.live) // 2
        sources = [(self.live[2 * k], self.live[2 * k + 1]) for k in range(count)]
        outs = [
            ([(k, 0, sources[k][0].shape[2]) for k in range(odd, count, 2)], self.dim(odd))
            for odd in range(2)
        ]
        self.live = list(add_and_split(sources, outs, len(self.left[0])))

    def send(self):
        for odd in range(2):
            bit = self.left[odd][self.dim(odd)]
            self.live[2 * odd + 1] = swap_bit(self.live[2 * odd + 1], "dp", bit)
        while len(self.left[0]) > 1:
            self.add()
            self.send()

    def total(self, cuts=1, turned=False, kind=F32):
        return finish_sum(self.live, self.width, cuts, turned, kind)


class WeightGather:
    def __init__(self, own, me):
        self.blocks = lax.axis_size("dp")
        self.size = lax.axis_size("tensor")
        self.usual = (self.size, self.blocks) == (4, 8)
        self.me = me
        share = own.shape[1 if self.usual else 0] // self.blocks
        axis = 1 if self.usual else 0
        self.live = [lax.dynamic_slice_in_dim(own, me[0] * share, share, axis)]

    def advance(self, k):
        if not self.usual:
            if k == 0:
                self.live = [lax.all_gather(self.live[0], ("tensor", "dp"), axis=0, tiled=True)]
            return
        if k == 0:
            own = self.live[0]
            self.live += [
                lax.ppermute(own, "tensor", [(i, (i + m) % self.size) for i in range(self.size)])
                for m in range(1, self.size)
            ]
        elif k == 1:
            own, one, two, three = self.live
            even = lax.axis_index("tensor") % 2 == 0
            near = jnp.concatenate([jnp.where(even, own, one), jnp.where(even, three, own)])
            far = jnp.concatenate([jnp.where(even, two, three), jnp.where(even, one, two)])
            self.live = [near, swap_bit(near, "dp", 1), far, swap_bit(far, "dp", 2)]
            self.live += [swap_bit(near, "dp", 0), swap_bit(far, "dp", 0)]
        elif k == 2:
            near, near_one, far, far_one, near_core, far_core = self.live
            near, far = jnp.stack([near, near_one]), jnp.stack([far, far_one])
            self.live = [near, far, near_core[None], far_core[None]]
            self.live += [swap_bit(near, "dp", 2), swap_bit(far, "dp", 1)]
            self.live += [swap_bit(near_one, "dp", 0)[None], swap_bit(far_one, "dp", 0)[None]]
        elif k == 3:
            near, far, near_core, far_core, near_two, far_two, near_one_core, far_one_core = self.live
            own = [(near, 0), (near, 1), (far, 0), (far, 1)]
            other = [(v, 0) for v in (near_core, near_one_core, far_core, far_one_core)]
            self.live = [near_two, far_two, self.place(own, other, 0, None)]
        else:
            near_two, far_two, half = self.live
            self.live = [near_two, swap_bit(near_two, "dp", 0)]
            self.live += [far_two, swap_bit(far_two, "dp", 0), half]

    def place(self, own, other, late, half):
        rows, width = own[0][0].shape[1:]
        blocks = own + other

        def kernel(me_ref, *refs):
            out = refs[-1]
            step, odd = pl.program_id(0), me_ref[0] & 1
            for k in range(4):
                for flip in range(2):

                    @pl.when((step == k) & (odd == flip))
                    def _():
                        out[:, flip * width : (flip + 1) * width] = refs[k][...]
                        out[:, (1 - flip) * width : (2 - flip) * width] = refs[k + 4][...]

        def source(entry):
            return pl.BlockSpec((None, rows, width), lambda s, m: (entry, 0, 0))

        def target(s, m):
            top, one = s < 2, s & 1
            low = jnp.where(top, 2 * one + 4 * late, 4 * one + 2 * late)
            return (jnp.where(top, m[2], 1 - m[2]), (low ^ m[0]) >> 1)

        more = [] if half is None else [half]
        return pl.pallas_call(
            kernel,
            grid_spec=pltpu.PrefetchScalarGridSpec(
                num_scalar_prefetch=1,
                grid=(4,),
                in_specs=[source(entry) for _, entry in blocks]
                + [pl.BlockSpec(memory_space=pl.ANY)] * len(more),
                out_specs=pl.BlockSpec((rows, 2 * width), target),
            ),
            out_shape=jax.ShapeDtypeStruct((2 * rows, 8 * width), BF16),
            input_output_aliases={9: 0} if more else {},
            compiler_params=pltpu.CompilerParams(vmem_limit_bytes=VMEM),
            cost_estimate=cost(2**20),
        )(self.me, *[array for array, _ in blocks], *more)

    def whole(self):
        if not self.usual:
            return self.live[0]
        near, near_core, far, far_core, half = self.live
        own = [(near, 0), (near, 1), (far, 0), (far, 1)]
        other = [(near_core, 0), (near_core, 1), (far_core, 0), (far_core, 1)]
        return self.place(own, other, 1, half)


class SmallSum:
    def __init__(self, vectors, me):
        self.vectors = vectors
        self.blocks = blocks = lax.axis_size("dp")
        self.bits = place_bits(blocks)
        places = jnp.stack([xor_source(p, me, self.bits) for p in range(blocks)]).reshape(-1)
        self.ordered = sorted(range(len(vectors)), key=lambda i: not vectors[i][1])
        wide = [vectors[i][0].reshape(blocks, -1) for i in self.ordered]
        wide = jnp.take(jnp.concatenate(wide, axis=1), places, axis=0)
        self.live = [wide.reshape((2,) * self.bits + wide.shape[1:])]

    def move(self):
        self.steps = getattr(self, "steps", 0) + 1
        while self.live[0].ndim > 1:
            values = self.live[0]
            self.live = [values[0] + swap_bit(values[1], "dp", self.bits - values.ndim + 1)]
            if self.steps < 3:
                return

    def tensor(self):
        values = self.live[0]
        both = sum(v[0].shape[0] // self.blocks for v in self.vectors if v[1])
        summed, alone = values[..., :both], values[..., both:]
        for bit in range(place_bits(lax.axis_size("tensor"))):
            summed = summed + swap_bit(summed, "tensor", bit)
        self.live = [jnp.concatenate([summed, alone], axis=-1)]

    def total(self):
        out, start = [None] * len(self.vectors), 0
        for i in self.ordered:
            size = self.vectors[i][0].shape[0] // self.blocks
            out[i] = self.live[0][start : start + size]
            start += size
        return out


def on_device(
    inputs,
    segments,
    cotangent,
    norm1_gain,
    norm1_bias,
    query_weight,
    query_bias,
    key_weight,
    value_weight,
    value_bias,
    output_weight,
    output_bias,
    norm2_gain,
    norm2_bias,
    up_weight,
    up_bias,
    down_weight,
    down_bias,
):
    groups = lax.axis_size("tensor")
    blocks = lax.axis_size("dp")
    here = lax.axis_index("tensor").astype(jnp.int32)
    side = here // (groups // 2)
    me = lax.axis_index("dp").astype(jnp.int32)
    me = jnp.stack([me, here, side])
    rows, width = inputs.shape
    share = rows // groups
    part = share // PARTS
    local = query_weight.shape[1]
    size = width // blocks

    def by_part(values):
        return values.reshape(groups, PARTS, part, values.shape[1])

    def own(values):
        return lax.dynamic_slice_in_dim(values, here * share, share, 0)

    weight = WeightGather(output_weight, me)
    weight.advance(0)
    normed, query, key, value = project(
        inputs,
        norm1_gain,
        norm1_bias,
        query_weight,
        query_bias,
        key_weight,
        value_weight,
        value_bias,
    )
    heads = [None] * PARTS
    heads[0] = attend(0, segments, query, key, value, groups)
    cot, heads[0], query, key, value = fence([weight], (cotangent, heads[0], query, key, value))

    heads[0] = lax.all_gather(heads[0].reshape(groups * part, local), "tensor", axis=0)
    weight.advance(1)
    heads[1] = attend(1, segments, query, key, value, groups)
    cot_sum = column_sums(cot)
    cot, heads[1], cot_sum = fence([weight], (cot, heads[1], cot_sum))
    heads[1] = lax.all_gather(heads[1].reshape(groups * part, local), "tensor", axis=0)
    weight.advance(2)
    cot_parts = by_part(cot)
    cots = [(cot_parts, c) for c in range(PARTS)]
    d_hidden = both_parts(cots, down_weight, True, down_weight.shape[0])
    d_hidden, cot = fence([], (d_hidden, cot))
    weight.advance(3)
    d_hidden, cot = fence([weight], (d_hidden, cot))
    weight.advance(4)
    fence([weight])
    whole = weight.whole()
    whole, heads[0] = fence([], (whole, heads[0]))

    own_mid, low, hidden, d_up, terms = ([None] * PARTS for _ in range(5))

    def middle(c):
        own_mid[c], low[c], hidden[c], d_up[c], *term = middle_call(
            1,
            c,
            me,
            heads[c],
            whole,
            by_part(inputs),
            output_bias,
            norm2_gain,
            norm2_bias,
            up_weight,
            up_bias,
            d_hidden,
        )
        terms[c] = term[0].reshape(groups, part, width)

    middle(0)
    terms[0], heads[1] = fence([], (terms[0], heads[1]))

    terms[0] = lax.psum_scatter(terms[0], "tensor", scatter_dimension=0)
    middle(1)
    cot_own = own(cot)
    terms[1], cot_own, low[0], low[1], d_up[0], d_up[1] = fence(
        [], (terms[1], cot_own, *low, *d_up)
    )

    terms[1] = lax.psum_scatter(terms[1], "tensor", scatter_dimension=0)
    up_terms = gradient_terms(low, [d_up], me, blocks)
    d_mids, d_branches, sums = ([None] * PARTS for _ in range(3))

    def back(c):
        d_mids[c], d_branches[c], sums[c], d_att = middle_back(
            terms[c], own_mid[c], cot_own[c * part : (c + 1) * part], norm2_gain, whole
        )
        return d_att

    terms[0], hidden[0], hidden[1], *up_terms = fence([], (terms[0], *hidden, *up_terms))
    d_att = back(0)
    d_att, hidden[0], hidden[1] = fence([], (d_att, *hidden))
    out_terms = both_parts(hidden, down_weight, False, width, groups)
    out_terms, hidden[0], hidden[1] = fence([], (out_terms, *hidden))
    down_terms = gradient_terms(cots, [hidden], me, blocks)
    d_att, *down_terms = fence([], (d_att, *down_terms))
    got = [exchange(d_att), None]
    up_sum = DpSum(*up_terms, 2)
    down_sum = DpSum(*down_terms, 4)
    terms[1], out_terms, d_branches[0] = fence(
        [up_sum, down_sum], (terms[1], out_terms, d_branches[0])
    )

    d_att = back(1)
    d_att, got[0], *d_branches = fence([up_sum, down_sum], (d_att, got[0], *d_branches))
    got[1] = exchange(d_att)
    up_sum.core()
    down_sum.core()
    views = [h.reshape(groups, groups, part, local) for h in heads]
    wo_terms = gradient_terms(d_branches, [[(v, t) for v in views] for t in range(groups)], me, blocks)
    wo_sum = DpSum(*wo_terms, 2)
    got[1], out_terms = fence([wo_sum, up_sum, down_sum], (got[1], out_terms))

    out_sum = lax.psum_scatter(out_terms, "tensor", scatter_dimension=0)
    up_sum.split()
    up_sum.first(0, 1)
    wo_sum.core()
    d_query, d_key, d_value = attend_back(segments, query, key, value, got)
    wo_sum.split()
    d_query, d_key, d_value = fence([up_sum, wo_sum, down_sum], (d_query, d_key, d_value))
    wo_sum.first(0, 1)
    qkv_sum = DpSum(
        *gradient_terms([normed], [[d] for d in (d_query, d_key, d_value)], me, blocks), 2
    )
    down_sum.split()
    d_query, d_key, d_value = fence([wo_sum, qkv_sum, down_sum], (d_query, d_key, d_value))
    qkv_sum.core()
    down_sum.first(0, 3)
    terms_in, gain1, bias1 = normed_back(
        d_query, d_key, d_value, query_weight, key_weight, value_weight, inputs
    )
    gain1, bias1, terms_in, d_query, d_value, d_up[0], d_up[1] = fence(
        [qkv_sum, wo_sum, down_sum], (gain1, bias1, terms_in, d_query, d_value, *d_up)
    )

    d_normed = lax.psum_scatter(
        terms_in.reshape(groups, share, width), "tensor", scatter_dimension=0
    )
    down_sum.first(1, 2)
    qkv_sum.split()
    wo_sum.add()
    up_bias_sum = column_sums(d_up[0]) + column_sums(d_up[1])
    gain1, bias1, d_query, d_value, up_bias_sum = fence(
        [qkv_sum, wo_sum, down_sum], (gain1, bias1, d_query, d_value, up_bias_sum)
    )
    qkv_sum.first(0, 1)
    wo_sum.send()
    two = sums[0] + sums[1]
    small = SmallSum(
        [
            (gain1[0], True),
            (bias1[0], True),
            (two[0], True),
            (two[1], True),
            (two[2], True),
            (cot_sum, False),
            (column_sums(d_query), False),
            (column_sums(d_value), False),
            (up_bias_sum, False),
        ],
        me[:1],
    )
    small.tensor()
    down_sum.add()
    out_sum, *_ = fence([qkv_sum, wo_sum, down_sum, small, up_sum], (out_sum,))
    down_sum.send()
    qkv_sum.add()
    qkv_sum.send()
    small.move()
    small.move()
    small.move()
    wo_terms = wo_sum.total(turned=True, kind=BF16)[0].reshape(groups, local, size)
    to_all = [
        lax.dynamic_index_in_dim(wo_terms, (here - m) % groups, 0, keepdims=False)
        for m in range(groups)
    ]
    up_sum.add()
    out_sum, *to_all = fence([qkv_sum, small, down_sum, up_sum], (out_sum, *to_all))
    wo_got = [to_all[0]]
    for m in range(1, groups):
        ring = [(i, (i - m) % groups) for i in range(groups)]
        wo_got.append(lax.ppermute(to_all[m], "tensor", ring))
    up_sum.send()
    total = [own_mid[c] + (out_sum[c].astype(F32) + down_bias) for c in range(PARTS)]
    output = jnp.concatenate([t.astype(BF16) for t in total], axis=0)
    qkv_grads = qkv_sum.total(3)
    (up_weight_grad,) = up_sum.total()
    (down_weight_grad,) = down_sum.total(turned=True)
    d_mid = jnp.concatenate(d_mids, axis=0)
    rows_own = own(inputs)
    small_sums = small.total()
    up_weight_grad, down_weight_grad, output, d_mid, rows_own, *others = fence(
        [],
        (up_weight_grad, down_weight_grad, output, d_mid, rows_own, *qkv_grads, *small_sums),
    )
    qkv_grads, small_sums = others[:3], others[3:]
    input_grad = input_back(d_normed, rows_own, d_mid, norm1_gain)
    input_grad, *wo_got = fence([], (input_grad, *wo_got))
    output_weight_grad = sum(g.astype(F32) for g in wo_got)
    (
        norm1_gain_grad,
        norm1_bias_grad,
        norm2_gain_grad,
        norm2_bias_grad,
        output_bias_grad,
        down_bias_grad,
        query_bias_grad,
        value_bias_grad,
        up_bias_grad,
    ) = small_sums
    return (
        output,
        input_grad,
        norm1_gain_grad,
        norm1_bias_grad,
        qkv_grads[0],
        query_bias_grad,
        qkv_grads[1],
        qkv_grads[2],
        value_bias_grad,
        output_weight_grad,
        output_bias_grad,
        norm2_gain_grad,
        norm2_bias_grad,
        up_weight_grad,
        up_bias_grad,
        down_weight_grad,
        down_bias_grad,
    )


def solution(mesh):
    return jax.shard_map(
        on_device,
        mesh=mesh,
        in_specs=(
            P("dp", None),
            P("dp", None),
            P("dp", None),
            P(),
            P(),
            P(None, "tensor"),
            P("tensor"),
            P(None, "tensor"),
            P(None, "tensor"),
            P("tensor"),
            P("tensor", None),
            P(),
            P(),
            P(),
            P(None, "tensor"),
            P("tensor"),
            P("tensor", None),
            P(),
        ),
        out_specs=(
            P(("dp", "tensor"), None),
            P(("dp", "tensor"), None),
            P("dp"),
            P("dp"),
            P("dp", "tensor"),
            P(("tensor", "dp")),
            P("dp", "tensor"),
            P("dp", "tensor"),
            P(("tensor", "dp")),
            P("tensor", "dp"),
            P("dp"),
            P("dp"),
            P("dp"),
            P("dp", "tensor"),
            P(("tensor", "dp")),
            P("tensor", "dp"),
            P("dp"),
        ),
        check_vma=False,
    )
```
